32 devices in a mesh: group: 16 (over z, x, core), dp: 2 (over y).
Axes of the slice: x: 2, y: 2, z: 4, core: 2. Of those that a mesh axis runs over, the one named last changes fastest.
Arguments:
- frames: bfloat16 [32768, 768], P(('group', 'dp')), may hold values from -6 to 6
- lengths: int32 [32, 2], P(('group', 'dp')), may hold values from 0 to 1024, as said below
- mask_starts: int32 [32768], P(('group', 'dp')), may hold values 0 or 1
- width_code: int32 [16], P('group'), may hold values from 0 to 2
- head_code: int32 [16], P('group'), may hold values from 0 to 4
- ffn_code: int32 [16], P('group'), may hold values from 0 to 2
- qkv_weight: float32 [768, 2304], P('group'), may hold values from -0.3125 to 0.3125
- out_weight: float32 [768, 768], P('group'), may hold values from -0.625 to 0.625
- ffn_in_weight: float32 [768, 3072], P('group'), may hold values from -0.21875 to 0.21875
- ffn_out_weight: float32 [3072, 768], P('group'), may hold values from -0.109375 to 0.109375
- ffn_bias: float32 [3072, 1], P('group'), may hold values from -3 to 3
- norm_gains: float32 [768, 2], P('group'), may hold values from 0.1 to 1.9
- shifts: float32 [768, 7], P('group'), may hold values from -3 to 3
- cotangent: bfloat16 [32768, 768], P(('group', 'dp')), may hold values from -6 to 6
Outputs:
- layer_out: bfloat16 [32768, 768], P(('group', 'dp'))
- frames_grad: float32 [32768, 768], P(('group', 'dp'))
- qkv_grad: float32 [768, 2304], P('group')
- out_grad: float32 [768, 768], P('group')
- ffn_in_grad: float32 [768, 3072], P('group')
- ffn_out_grad: float32 [3072, 768], P('group')
- ffn_bias_grad: float32 [3072, 1], P('group')
- gains_grad: float32 [768, 2], P('group')
- shifts_grad: float32 [768, 7], P('group')
The draws below stay inside these ranges and needn't reach their ends.
Inputs may be any that keep to these rules, and one draw needn't show every extreme that they name: `lengths`: per device: the first utterance has 300 to 1024 frames, the second is 0 (absent) or 300 or more, together at most 1024; some device holds one utterance of exactly 1024 frames.
All inputs are finite; a program needn't handle non-finite values. No bound on the sum of `mask_starts` on one device may be relied on, other than what follows from the above.
Results may differ from the reference program's by a relative error of at most 0.015.
The reference program's roundings to bfloat16 on the way count: a program that leaves them out, or rounds other values in their place, can miss the bound.
Values may be sent and summed in bfloat16 or wider, within the bound.
A program may use at most 192 MiB of HBM per device.

```python
import jax
import jax.numpy as jnp
from jax import lax

D = 768
HEADS = 12
FF = 3072
FRAMES = 1024
MIN_LEN = 300
SPAN = 10
UTT_DEV = 2
TOKENS = 32768
N_GROUP = 16
N_DP = 2
DEVICES = 32


def draw_lengths(key, part):
    key = jax.random.fold_in(key, 11)
    first_key, second_key, pick_key = jax.random.split(key, 3)
    firsts = jax.random.randint(first_key, (DEVICES,), MIN_LEN, FRAMES + 1)
    room = FRAMES - firsts
    seconds = jax.random.randint(second_key, (DEVICES,), 0, room + 1)
    seconds = jnp.where(seconds >= MIN_LEN, seconds, 0)
    chosen = jax.random.randint(pick_key, (), 0, DEVICES)
    places = jnp.arange(DEVICES)
    firsts = jnp.where(places == chosen, FRAMES, firsts)
    seconds = jnp.where(places == chosen, 0, seconds)
    return jnp.stack([firsts, seconds], axis=1).astype(jnp.int32)


def touch_ends(entries, own_key, least, high):
    longest = entries.shape.index(max(entries.shape))
    spots = []
    for shift in (0, 1):
        where = [jax.random.randint(jax.random.fold_in(own_key, axis), (), 0, length) for axis, length in enumerate(entries.shape)]
        where[longest] = (where[longest] + shift) % entries.shape[longest]
        spots.append(tuple(where))
    return entries.at[spots[0]].set(least).at[spots[1]].set(high)


def block_levels(key, dims, cuts, least, largest):
    level, own = 1.0, jax.random.fold_in(key, 6)
    for axis_at, blocks in cuts:
        steps = jnp.exp(jax.random.uniform(jax.random.fold_in(own, axis_at), (blocks,), jnp.float32, least / len(cuts), largest / len(cuts)))
        level = level * jnp.repeat(steps, dims[axis_at] // blocks).reshape([-1 if axis == axis_at else 1 for axis in range(len(dims))])
    return level


def gaussian(own_key, extent, width, bound, cuts=(), kind=jnp.bfloat16):
    values = width * jax.random.normal(own_key, extent, jnp.float32)
    if cuts:
        values = values * block_levels(own_key, extent, cuts, -0.22, 0.18)
    return jnp.clip(values, -bound, bound).astype(kind)


def setup_inputs(seed: int = 0) -> dict:
    streams_of = jax.random.split(jax.random.key(seed), 15)
    frames = gaussian(streams_of[0], (TOKENS, D), 1.0, 6.0, ((0, 32),))
    lengths = draw_lengths(jax.random.fold_in(streams_of[14], 71), 0)
    mask_starts = touch_ends((jax.random.randint(streams_of[2], (TOKENS,), 0, 125) < 1).astype(jnp.int32), jax.random.fold_in(streams_of[2], 1), 0, 1)
    width_code = touch_ends(jax.random.randint(streams_of[3], (N_GROUP,), 0, 3), jax.random.fold_in(streams_of[3], 1), 0, 2).astype(jnp.int32)
    head_code = touch_ends(jax.random.randint(streams_of[4], (N_GROUP,), 0, HEADS // 3 + 1), jax.random.fold_in(streams_of[4], 1), 0, (HEADS // 3 + 1) - 1).astype(jnp.int32)
    ffn_code = touch_ends(jax.random.randint(streams_of[5], (N_GROUP,), 0, 3), jax.random.fold_in(streams_of[5], 1), 0, 2).astype(jnp.int32)
    qkv_weight = gaussian(streams_of[6], (D, 3 * D), (D // 2) ** -0.5, 0.3125, ((0, 16),), jnp.float32)
    out_weight = gaussian(streams_of[7], (D, D), (D // 8) ** -0.5, 0.625, ((0, 16),), jnp.float32)
    ffn_in_weight = gaussian(streams_of[8], (D, FF), D ** -0.5, 0.21875, ((0, 16),), jnp.float32)
    ffn_out_weight = gaussian(streams_of[9], (FF, D), FF ** -0.5, 0.109375, ((0, 16),), jnp.float32)
    ffn_bias = gaussian(streams_of[10], (FF, 1), 0.5, 3.0, ((0, 16),), jnp.float32)
    norm_gains = jnp.clip(1.0 + 0.18 * jax.random.normal(streams_of[11], (D, 2), jnp.float32), 0.1, 1.9)
    shifts = gaussian(streams_of[12], (D, 7), 0.5, 3.0, ((0, 16),), jnp.float32)
    cotangent = gaussian(streams_of[13], (TOKENS, D), 1.0, 6.0, ((0, 32),))
    return dict(frames=frames, lengths=lengths, mask_starts=mask_starts, width_code=width_code, head_code=head_code, ffn_code=ffn_code, qkv_weight=qkv_weight, out_weight=out_weight, ffn_in_weight=ffn_in_weight, ffn_out_weight=ffn_out_weight, ffn_bias=ffn_bias, norm_gains=norm_gains, shifts=shifts, cotangent=cotangent)


@jax.custom_vjp
def low(v):
    return lax.optimization_barrier(v.astype(jnp.bfloat16)).astype(jnp.float32)

@jax.custom_vjp
def low_back(v):
    return v

def low_keep(v):
    return (low(v), None)

def low_pass(kept, grad):
    return (grad,)

def back_keep(v):
    return (v, None)

def back_low(kept, grad):
    return (low(grad),)
low.defvjp(low_keep, low_pass)
low_back.defvjp(back_keep, back_low)
highest = lax.Precision.HIGHEST
norm_eps = 1e-05
far_score = -1000000000.0

def subnet_masks(width_pick, head_pick, ffn_pick):
    sub_width = D * (4 + width_pick) // 6
    head_count = HEADS - HEADS // 3 + head_pick
    ffn_width = sub_width * (6 + ffn_pick) // 2
    feature_mask = (jnp.arange(D, dtype=jnp.int32) < sub_width).astype(jnp.float32)
    head_mask = (jnp.arange(D, dtype=jnp.int32) < head_count * (D // HEADS)).astype(jnp.float32)
    ffn_mask = (jnp.arange(FF, dtype=jnp.int32) < ffn_width).astype(jnp.float32)
    return (feature_mask, head_mask, ffn_mask, sub_width.astype(jnp.float32))

def frame_layout(block_lengths, starts):
    places = jnp.arange(FRAMES, dtype=jnp.int32)
    bounds = jnp.cumsum(block_lengths).astype(jnp.int32)
    segment = lax.optimization_barrier(jnp.sum((places[:, None] >= bounds[None, :]).astype(jnp.int32), axis=1))
    live_rows = (segment < UTT_DEV).astype(jnp.int32)
    hit_count = jnp.zeros((FRAMES,), jnp.int32)
    for offset in range(SPAN):
        earlier = jnp.concatenate([jnp.zeros((offset,), jnp.int32), starts[:FRAMES - offset]])
        earlier_seg = jnp.concatenate([jnp.full((offset,), -1, jnp.int32), segment[:FRAMES - offset]])
        hit_count = jnp.maximum(hit_count, ((earlier == 1) & (earlier_seg == segment)).astype(jnp.int32))
    masked = hit_count * live_rows
    return (segment, live_rows.astype(jnp.float32), masked.astype(jnp.float32))

def layer_norm(residual, gain_vec, shift_vec, feature_mask, sub_width):
    center = lax.optimization_barrier(jnp.sum(residual, axis=1, keepdims=True)) / sub_width
    centered = (residual - center) * feature_mask
    variance = lax.optimization_barrier(jnp.sum(centered * centered, axis=1, keepdims=True)) / sub_width
    return centered * lax.rsqrt(variance + norm_eps) * gain_vec * feature_mask + shift_vec * feature_mask

def head_pair(query_pair, key_pair, value_pair, same_seg):
    head_dim = D // HEADS
    query_heads = query_pair.reshape(FRAMES, 2, head_dim)
    key_heads = key_pair.reshape(FRAMES, 2, head_dim)
    value_heads = value_pair.reshape(FRAMES, 2, head_dim)
    scores = jnp.einsum('qhd,khd->hqk', query_heads, key_heads, precision=highest) * head_dim ** (-0.5)
    scores = low_back(scores)
    scores = jnp.where(same_seg[None], scores, far_score)
    row_peak = lax.optimization_barrier(jnp.max(scores, axis=2, keepdims=True))
    weights = jnp.exp(scores - row_peak)
    probs = weights / lax.optimization_barrier(jnp.sum(weights, axis=2, keepdims=True))
    pair_mixed = jnp.einsum('hqk,khd->qhd', low(probs), value_heads, precision=highest)
    return pair_mixed.reshape(FRAMES, 2 * head_dim)

def attention(queries, keys, values, same_seg):
    pair_width = 2 * (D // HEADS)

    def split_pairs(matrix):
        return matrix.reshape(FRAMES, HEADS // 2, pair_width).transpose(1, 0, 2)

    def one_pair(trio):
        return head_pair(trio[0], trio[1], trio[2], same_seg)
    mixed = lax.map(jax.checkpoint(one_pair), (split_pairs(queries), split_pairs(keys), split_pairs(values)))
    return mixed.transpose(1, 0, 2).reshape(FRAMES, D)

def layer_forward(block_in, weights, masks, same_seg, live_rows, masked):
    qkv_mat, out_mat, in_mat, down_mat, bias_col, gains_pair, shift_table = weights
    feature_mask, head_mask, ffn_mask, sub_width = masks
    three_mask = jnp.concatenate([head_mask, head_mask, head_mask])
    start_vec = jnp.where(masked[:, None] > 0, shift_table[:, 6][None, :], block_in) * feature_mask
    projected = jnp.dot(low(start_vec), qkv_mat * feature_mask[:, None] * three_mask[None, :], precision=highest)
    proj_bias = jnp.concatenate([shift_table[:, 0] * head_mask, jnp.zeros((D,), jnp.float32), shift_table[:, 1] * head_mask])
    projected = low(low_back(projected + proj_bias))
    mixed = attention(projected[:, :D], projected[:, D:2 * D], projected[:, 2 * D:], same_seg)
    mixed = low(low_back(mixed))
    branch = low_back(jnp.dot(mixed, out_mat * head_mask[:, None] * feature_mask[None, :], precision=highest) + shift_table[:, 2] * feature_mask)
    hidden_one = layer_norm(start_vec + branch, gains_pair[:, 0], shift_table[:, 4], feature_mask, sub_width)
    pre_act = low_back(jnp.dot(low(hidden_one), in_mat * feature_mask[:, None] * ffn_mask[None, :], precision=highest) + bias_col[:, 0] * ffn_mask)
    act_low = low(jax.nn.gelu(pre_act, approximate=False))
    ffn_branch = low_back(jnp.dot(act_low, down_mat * ffn_mask[:, None] * feature_mask[None, :], precision=highest) + shift_table[:, 3] * feature_mask)
    result = layer_norm(hidden_one + ffn_branch, gains_pair[:, 1], shift_table[:, 5], feature_mask, sub_width)
    return result * live_rows[:, None]

def reference(frames, lengths, mask_starts, width_code, head_code, ffn_code, qkv_weight, out_weight, ffn_in_weight, ffn_out_weight, ffn_bias, norm_gains, shifts, cotangent):
    qkv_full = qkv_weight.astype(jnp.bfloat16)
    out_full = out_weight.astype(jnp.bfloat16)
    ffn_in_full = ffn_in_weight.astype(jnp.bfloat16)
    ffn_out_full = ffn_out_weight.astype(jnp.bfloat16)
    ffn_bias_full = ffn_bias.astype(jnp.bfloat16)
    gains_full = norm_gains.astype(jnp.bfloat16)
    shifts_full = shifts.astype(jnp.bfloat16)
    params = (qkv_full.astype(jnp.float32), out_full.astype(jnp.float32), ffn_in_full.astype(jnp.float32), ffn_out_full.astype(jnp.float32), ffn_bias_full.astype(jnp.float32), gains_full.astype(jnp.float32), shifts_full.astype(jnp.float32))
    frame_blocks = frames.reshape(DEVICES, FRAMES, D)
    cot_blocks = cotangent.reshape(DEVICES, FRAMES, D)
    start_blocks = mask_starts.reshape(DEVICES, FRAMES)

    def one_block(totals, block):
        block_frames, block_cot, block_lengths, block_starts, device = block
        owner = device // N_DP
        masks = subnet_masks(width_code[owner], head_code[owner], ffn_code[owner])
        segment, live_rows, masked = frame_layout(block_lengths, block_starts)
        same_seg = segment[:, None] == segment[None, :]

        def forward(block_in, *weights):
            return layer_forward(block_in, weights, masks, same_seg, live_rows, masked)
        result, pull = jax.vjp(forward, block_frames.astype(jnp.float32), *params)
        grads = pull(block_cot.astype(jnp.float32))
        totals = tuple((total + grad for total, grad in zip(totals, grads[1:])))
        return (totals, (result.astype(jnp.bfloat16), grads[0]))
    start_totals = tuple((jnp.zeros(param.shape, jnp.float32) for param in params))
    totals, (out_blocks, grad_blocks) = lax.scan(one_block, start_totals, (frame_blocks, cot_blocks, lengths, start_blocks, jnp.arange(DEVICES, dtype=jnp.int32)))
    layer_out = out_blocks.reshape(TOKENS, D)
    frames_grad = grad_blocks.reshape(TOKENS, D)
    return (layer_out, frames_grad, totals[0], totals[1], totals[2], totals[3], totals[4], totals[5], totals[6])
```

```python
import functools

import jax
import jax.numpy as jnp
from jax import lax
from jax.experimental import pallas as pl
from jax.experimental.pallas import tpu as pltpu
from jax.sharding import PartitionSpec as P

D = 768
HEADS = 12
FF = 3072
FRAMES = 1024
SPAN = 10
UTT_DEV = 2


norm_eps = 1e-05
far_score = -1000000000.0
root_half = 0.7071067811865476
inv_root_tau = 0.3989422804014327


MESH = pl.DeviceIdType.MESH


class Place:
    def __init__(self, depth):
        group, dp = lax.axis_index("group"), lax.axis_index("dp")
        self.depth = depth
        self.group, self.dp = group, dp
        self.z, self.x, self.c, self.y = group // 4, (group // 2) % 2, group % 2, dp % 2
        self.core_dev = (group + 1 - 2 * self.c, dp)
        self.x_dev = (group + 2 - 4 * self.x, dp)
        self.y_dev = (group, dp + 1 - 2 * self.y)

    def z_at(self, step):
        return lax.rem(self.z + step, self.depth)

    def z_from(self, step):
        return lax.rem(self.z - step + self.depth, self.depth)

    def z_dev(self, step):
        return ((self.z_at(step) * 2 + self.x) * 2 + self.c, self.dp)

    def greet(self):
        barrier = pltpu.get_barrier_semaphore()
        devs = [self.core_dev, self.x_dev, self.y_dev] + [self.z_dev(s) for s in range(1, self.depth)]
        for dev in devs:
            pl.semaphore_signal(barrier, inc=1, device_id=dev, device_id_type=MESH)
        pl.semaphore_wait(barrier, len(devs))


class Copies:
    def __init__(self, send_sems, recv_sems):
        self.send_sems, self.recv_sems, self.count, self.made = send_sems, recv_sems, 0, []

    def to(self, src, dst, dev):
        spot = self.count
        self.count += 1
        copy = pltpu.make_async_remote_copy(
            src_ref=src, dst_ref=dst, send_sem=self.send_sems.at[spot], recv_sem=self.recv_sems.at[spot],
            device_id=dev, device_id_type=MESH)
        self.made.append(copy)
        return copy

    def finish(self):
        for copy in self.made:
            copy.wait_send()


def halves(width, y):
    half = width // 2
    mine = pl.ds(pl.multiple_of(y * half, 128), half)
    other = pl.ds(pl.multiple_of((1 - y) * half, 128), half)
    return mine, other


def gather_cross(here, copies, own, at, width):
    z, x, c = here.z, here.x, here.c
    mine, other = halves(width, here.y)
    full = slice(None)
    steps = range(1, here.depth)
    first = copies.to(own(mine), at(z, x, c, mine), here.x_dev)
    own_core = copies.to(own(full), at(z, x, c, full), here.core_dev)
    own_z = [copies.to(own(mine), at(z, x, c, mine), here.z_dev(s)) for s in steps]

    def same(zz, xx, cols, dev):
        return copies.to(at(zz, xx, c, cols), at(zz, xx, c, cols), dev)

    side_z = [same(z, 1 - x, mine, here.z_dev(s)) for s in steps]
    spots = [(z, 1 - x)] + [(here.z_from(s), x) for s in steps] + [(here.z_from(s), 1 - x) for s in steps]
    y_hops = [same(zz, xx, mine, here.y_dev) for zz, xx in spots]
    core_mine = [same(zz, xx, mine, here.core_dev) for zz, xx in spots]
    core_other = [same(zz, xx, other, here.core_dev) for zz, xx in spots]
    n = len(own_z)

    def stage0():
        first.start()
        for copy in own_z:
            copy.start()
        own_core.start()

    def stage1():
        first.wait_recv()
        for copy in side_z:
            copy.start()
        y_hops[0].start()
        core_mine[0].start()

    def stage2():
        for k in range(n):
            own_z[k].wait_recv()
            y_hops[1 + k].start()
            core_mine[1 + k].start()

    def stage3():
        for k in range(n):
            side_z[k].wait_recv()
            y_hops[1 + n + k].start()
            core_mine[1 + n + k].start()

    def stage4():
        for k in range(1 + 2 * n):
            y_hops[k].wait_recv()
            core_other[k].start()

    def stage5():
        own_core.wait_recv()
        for copy in core_mine + core_other:
            copy.wait_recv()

    return [stage0, stage1, stage2, stage3, stage4, stage5]


def gather_line(here, copies, own, at, width):
    z, x, c = here.z, here.x, here.c
    mine, other = halves(width, here.y)
    full = slice(None)
    steps = range(1, here.depth)
    own_z = [copies.to(own(mine), at(z, x, c, mine), here.z_dev(s)) for s in steps]
    own_x = copies.to(own(full), at(z, x, c, full), here.x_dev)
    own_core = copies.to(own(full), at(z, x, c, full), here.core_dev)

    def same(zz, xx, cols, dev):
        return copies.to(at(zz, xx, c, cols), at(zz, xx, c, cols), dev)

    froms = [here.z_from(s) for s in steps]
    y_hops = [same(zz, x, mine, here.y_dev) for zz in froms]
    x_mine = [same(zz, x, mine, here.x_dev) for zz in froms]
    x_other = [same(zz, x, other, here.x_dev) for zz in froms]
    core_side = same(z, 1 - x, full, here.core_dev)
    core_mine = [same(zz, x, mine, here.core_dev) for zz in froms]
    core_other = [same(zz, x, other, here.core_dev) for zz in froms]
    core_x_mine = [same(zz, 1 - x, mine, here.core_dev) for zz in froms]
    core_x_other = [same(zz, 1 - x, other, here.core_dev) for zz in froms]
    n = len(own_z)

    def stage0():
        for copy in own_z:
            copy.start()
        own_x.start()
        own_core.start()

    def stage1():
        for k in range(n):
            own_z[k].wait_recv()
            y_hops[k].start()
            x_mine[k].start()
            core_mine[k].start()

    def stage2():
        own_x.wait_recv()
        core_side.start()

    def stage3():
        for k in range(n):
            y_hops[k].wait_recv()
            x_other[k].start()
            core_other[k].start()

    def stage4():
        for k in range(n):
            x_mine[k].wait_recv()
            core_x_mine[k].start()
        for k in range(n):
            x_other[k].wait_recv()
            core_x_other[k].start()

    def stage5():
        own_core.wait_recv()
        core_side.wait_recv()
        for copy in core_mine + core_other + core_x_mine + core_x_other:
            copy.wait_recv()

    return [stage0, stage1, stage2, stage3, stage4, stage5]


def gather_copies(depth):
    return 2 + (depth - 1) * 2 + 3 * (2 * depth - 1) + (depth - 1) * 8 + 3


def plus(a, b):
    return (a.astype(jnp.float32) + b.astype(jnp.float32)).astype(jnp.bfloat16)


def reduce_part(here, copies, parts, room, final, width, cross):
    z, x, c, depth = here.z, here.x, here.c, here.depth
    mine, other = halves(width, here.y)
    steps = range(1, depth)
    if cross:
        first, second, third, fourth, fifth = room
        core = copies.to(parts.at[:, :, 1 - c], first, here.core_dev)
        to_y = copies.to(first.at[:, :, :, other], second, here.y_dev)
        to_z = [copies.to(second.at[here.z_at(s)], third.at[s - 1], here.z_dev(s)) for s in steps]
        to_x = copies.to(fourth.at[1 - x], fifth, here.x_dev)
        back = copies.to(final.at[:, mine], final.at[:, mine], here.y_dev)

        def stage0():
            core.start()

        def stage1():
            core.wait_recv()

            @pl.loop(0, depth)
            def _(zz):
                for xx in range(2):
                    first[zz, xx] = plus(parts[zz, xx, c], first[zz, xx])
            to_y.start()

        def stage2():
            to_y.wait_recv()

            @pl.loop(0, depth)
            def _(zz):
                for xx in range(2):
                    second[zz, xx] = plus(first[zz, xx, :, mine], second[zz, xx])
            for copy in to_z:
                copy.start()

        def stage3():
            for copy in to_z:
                copy.wait_recv()

            @pl.loop(0, 2)
            def _(xx):
                total = second[z, xx].astype(jnp.float32)
                for s in steps:
                    total += third[s - 1, xx].astype(jnp.float32)
                fourth[xx] = total.astype(jnp.bfloat16)
            to_x.start()

        def stage4():
            to_x.wait_recv()
            final[:, mine] = plus(fourth[x], fifth[...])
            back.start()

        def stage5():
            back.wait_recv()
    else:
        first, second, third, fourth = room
        core = copies.to(parts.at[:, :, 1 - c], first, here.core_dev)
        to_x = copies.to(first.at[:, 1 - x], second, here.x_dev)
        to_y = copies.to(second.at[:, :, other], third, here.y_dev)
        to_z = [copies.to(third.at[here.z_at(s)], fourth.at[s - 1], here.z_dev(s)) for s in steps]
        back = copies.to(final.at[:, mine], final.at[:, mine], here.y_dev)

        def stage0():
            core.start()

        def stage1():
            core.wait_recv()

            @pl.loop(0, depth)
            def _(zz):
                for xx in range(2):
                    first[zz, xx] = plus(parts[zz, xx, c], first[zz, xx])
            to_x.start()

        def stage2():
            to_x.wait_recv()

            @pl.loop(0, depth)
            def _(zz):
                second[zz] = plus(first[zz, x], second[zz])
            to_y.start()

        def stage3():
            to_y.wait_recv()

            @pl.loop(0, depth)
            def _(zz):
                third[zz] = plus(second[zz, :, mine], third[zz])
            for copy in to_z:
                copy.start()

        def stage4():
            for copy in to_z:
                copy.wait_recv()
            total = third[z].astype(jnp.float32)
            for s in steps:
                total += fourth[s - 1].astype(jnp.float32)
            final[:, mine] = total.astype(jnp.bfloat16)
            back.start()

        def stage5():
            back.wait_recv()

    return [stage0, stage1, stage2, stage3, stage4, stage5]


def reduce_room(depth, rows, width, cross):
    half = width // 2
    if cross:
        shapes = [(depth, 2, rows, width), (depth, 2, rows, half), (depth - 1, 2, rows, half), (2, rows, half), (rows, half)]
    else:
        shapes = [(depth, 2, rows, width), (depth, rows, width), (depth, rows, half), (depth - 1, rows, half)]
    return [pltpu.VMEM(shape, jnp.bfloat16) for shape in shapes]


def reduce_copies(depth):
    return 4 + depth - 1


def run_stages(plans, skew=0):
    order = []
    for at, plan in enumerate(plans):
        for s, stage in enumerate(plan):
            order.append((s, at, stage))
    for _, _, stage in sorted(order, key=lambda t: (t[0], t[1])):
        stage()


def gather_all(depth, head, kv, wide, down):
    rows, drows = head.shape[0], down.shape[0]

    def kernel(head_ref, kv_ref, wide_ref, down_ref, head_full, kv_full, wide_full, down_full, send, recv, local):
        here = Place(depth)
        z, x, c = here.z, here.x, here.c
        copies = Copies(send, recv)
        plans = [
            gather_cross(here, copies, lambda cols: head_ref.at[:, cols], lambda zz, xx, cc, cols: head_full.at[zz, xx, cc, :, cols], head.shape[1]),
            gather_line(here, copies, lambda cols: kv_ref.at[:, :, cols], lambda zz, xx, cc, cols: kv_full.at[:, zz, xx, cc, :, cols], 768),
            gather_cross(here, copies, lambda cols: down_ref.at[:, cols], lambda zz, xx, cc, cols: down_full.at[zz, xx, cc, :, cols], 768),
            gather_line(here, copies, lambda cols: wide_ref.at[:, :, cols], lambda zz, xx, cc, cols: wide_full.at[:, zz, xx, cc, :, cols], 768),
        ]
        here.greet()
        keep = [
            pltpu.make_async_copy(head_ref, head_full.at[z, x, c], local.at[0]),
            pltpu.make_async_copy(kv_ref, kv_full.at[:, z, x, c], local.at[1]),
            pltpu.make_async_copy(wide_ref, wide_full.at[:, z, x, c], local.at[2]),
            pltpu.make_async_copy(down_ref, down_full.at[z, x, c], local.at[3]),
        ]
        for copy in keep:
            copy.start()
        run_stages(plans)
        for copy in keep:
            copy.wait()
        copies.finish()

    count = 2 * gather_copies(depth)
    any_spec = pl.BlockSpec(memory_space=pl.ANY)
    return pl.pallas_call(
        kernel,
        out_shape=(
            jax.ShapeDtypeStruct((depth, 2, 2, rows, head.shape[1]), jnp.bfloat16),
            jax.ShapeDtypeStruct((2, depth, 2, 2, rows, 768), jnp.bfloat16),
            jax.ShapeDtypeStruct((5, depth, 2, 2, rows, 768), jnp.bfloat16),
            jax.ShapeDtypeStruct((depth, 2, 2, drows, 768), jnp.bfloat16),
        ),
        in_specs=[any_spec] * 4,
        out_specs=(any_spec,) * 4,
        scratch_shapes=[pltpu.SemaphoreType.DMA((count,)), pltpu.SemaphoreType.DMA((count,)), pltpu.SemaphoreType.DMA((4,))],
        compiler_params=pltpu.CompilerParams(collective_id=0, has_side_effects=True),
        name="gather_all",
    )(head, kv, wide, down)


def reduce_all(depth, parts, crosses, vmem=60):
    n = len(parts)
    sizes = [(p.shape[3], p.shape[4]) for p in parts]

    def kernel(*refs):
        ins, outs, rest = refs[:n], refs[n:2 * n], refs[2 * n:]
        here = Place(depth)
        copies = Copies(rest[0], rest[1])
        at, plans = 2, []
        for k in range(n):
            room = rest[at:at + (5 if crosses[k] else 4)]
            at += len(room)
            plans.append(reduce_part(here, copies, ins[k], room, outs[k], sizes[k][1], crosses[k]))
        here.greet()
        run_stages(plans)
        copies.finish()

    rooms = []
    for (rows, width), cross in zip(sizes, crosses):
        rooms += reduce_room(depth, rows, width, cross)
    count = reduce_copies(depth) * n
    return pl.pallas_call(
        kernel,
        out_shape=tuple(jax.ShapeDtypeStruct(s, jnp.bfloat16) for s in sizes),
        in_specs=[pl.BlockSpec(memory_space=pltpu.VMEM)] * n,
        out_specs=(pl.BlockSpec(memory_space=pltpu.VMEM),) * n,
        scratch_shapes=[pltpu.SemaphoreType.DMA((count,)), pltpu.SemaphoreType.DMA((count,))] + rooms,
        compiler_params=pltpu.CompilerParams(collective_id=1, has_side_effects=True, vmem_limit_bytes=vmem * 2**20),
        name="reduce_all",
    )(*parts)


def subnet_masks(width_pick, head_pick, ffn_pick):
    sub_width = D * (4 + width_pick) // 6
    head_count = HEADS - HEADS // 3 + head_pick
    ffn_width = sub_width * (6 + ffn_pick) // 2
    feature_mask = (jnp.arange(D, dtype=jnp.int32) < sub_width).astype(jnp.float32)
    head_mask = (jnp.arange(D, dtype=jnp.int32) < head_count * (D // HEADS)).astype(jnp.float32)
    ffn_mask = (jnp.arange(FF, dtype=jnp.int32) < ffn_width).astype(jnp.float32)
    return (feature_mask, head_mask, ffn_mask, sub_width.astype(jnp.float32))


def frame_layout(block_lengths, starts):
    places = jnp.arange(FRAMES, dtype=jnp.int32)
    bounds = jnp.cumsum(block_lengths)
    segment = jnp.sum((places[:, None] >= bounds[None, :]).astype(jnp.int32), axis=1)
    live_rows = (segment < UTT_DEV).astype(jnp.int32)
    hit_count = jnp.zeros((FRAMES,), jnp.int32)
    for offset in range(SPAN):
        earlier = jnp.concatenate([jnp.zeros((offset,), jnp.int32), starts[: FRAMES - offset]])
        earlier_seg = jnp.concatenate(
            [jnp.full((offset,), -1, jnp.int32), segment[: FRAMES - offset]]
        )
        hit_count = jnp.maximum(
            hit_count, ((earlier == 1) & (earlier_seg == segment)).astype(jnp.int32)
        )
    masked = hit_count * live_rows
    return (segment, live_rows.astype(jnp.float32), masked.astype(jnp.float32))


def norm_forward(residual, gain_vec, shift_vec, feature_mask, sub_width):
    center = jnp.sum(residual, axis=1, keepdims=True) / sub_width
    centered = (residual - center) * feature_mask
    variance = jnp.sum(centered * centered, axis=1, keepdims=True) / sub_width
    inv_std = lax.rsqrt(variance + norm_eps)
    normed = centered * inv_std
    return (normed * gain_vec * feature_mask + shift_vec * feature_mask, normed, inv_std)


def norm_backward(grad_out, gain_vec, normed, inv_std, feature_mask, sub_width):
    grad_normed = grad_out * gain_vec * feature_mask
    mean_grad = jnp.sum(grad_normed, axis=1, keepdims=True) / sub_width
    mean_cross = jnp.sum(grad_normed * normed, axis=1, keepdims=True) / sub_width
    grad_in = inv_std * (grad_normed - mean_grad - normed * mean_cross) * feature_mask
    return (grad_in, jnp.sum(grad_out * normed, axis=0), jnp.sum(grad_out, axis=0) * feature_mask)


def gelu_slope(pre_act):
    return (
        0.5 * (1.0 + lax.erf(pre_act * root_half))
        + pre_act * jnp.exp(-0.5 * pre_act * pre_act) * inv_root_tau
    )


def column_block(matrix, col_start, col_count):
    return lax.dynamic_slice_in_dim(matrix, col_start, col_count, 1)


def on_device(
    dp_size,
    frames,
    lengths,
    mask_starts,
    width_code,
    head_code,
    ffn_code,
    qkv_weight,
    out_weight,
    ffn_in_weight,
    ffn_out_weight,
    ffn_bias,
    norm_gains,
    shifts,
    cotangent,
):
    feature_mask, head_mask, ffn_mask, sub_width = subnet_masks(
        width_code[0], head_code[0], ffn_code[0]
    )
    segment, live_rows, masked = frame_layout(lengths[0], mask_starts)
    same_seg = segment[:, None] == segment[None, :]
    frame_rows = frames.shape[0]
    head_dim = D // HEADS
    pair_width = 2 * head_dim
    score_scale = head_dim ** (-0.5)
    three_mask = jnp.concatenate([head_mask, head_mask, head_mask])

    def pair_scores(projected, col_start):
        query_heads = column_block(projected, col_start, pair_width).reshape(
            frame_rows, 2, head_dim
        )
        key_heads = column_block(projected, D + col_start, pair_width).reshape(
            frame_rows, 2, head_dim
        )
        value_heads = column_block(projected, 2 * D + col_start, pair_width).reshape(
            frame_rows, 2, head_dim
        )
        scores = (
            jnp.einsum("qhd,khd->hqk", query_heads, key_heads, preferred_element_type=jnp.float32)
            * score_scale
        )
        return (query_heads, key_heads, value_heads, jnp.where(same_seg[None], scores, far_score))

    def attention_part(qkv_full, out_full, gains_full, shifts_full):
        shift_table = shifts_full.astype(jnp.float32)
        start_vec = (
            jnp.where(masked[:, None] > 0, shift_table[:, 6][None, :], frames.astype(jnp.float32))
            * feature_mask
        )
        start_low = start_vec.astype(jnp.bfloat16)
        qkv_masked = qkv_full * (feature_mask[:, None] * three_mask[None, :]).astype(jnp.bfloat16)
        proj_bias = jnp.concatenate(
            [
                shift_table[:, 0] * head_mask,
                jnp.zeros((D,), jnp.float32),
                shift_table[:, 1] * head_mask,
            ]
        )
        projected = (
            jnp.dot(start_low, qkv_masked, preferred_element_type=jnp.float32) + proj_bias
        ).astype(jnp.bfloat16)

        def pair_forward(pair_index, loop_state):
            mixed_buf, lse_buf = loop_state
            col_start = pair_index * pair_width
            query_heads, key_heads, value_heads, scores = pair_scores(projected, col_start)
            row_peak = jnp.max(scores, axis=2, keepdims=True)
            weights = jnp.exp(scores - row_peak)
            denominator = jnp.sum(weights, axis=2, keepdims=True)
            weights_low = (weights / denominator).astype(jnp.bfloat16)
            pair_mixed = jnp.einsum(
                "hqk,khd->qhd", weights_low, value_heads, preferred_element_type=jnp.float32
            )
            mixed_buf = lax.dynamic_update_slice(
                mixed_buf,
                pair_mixed.reshape(frame_rows, pair_width).astype(jnp.bfloat16),
                (0, col_start),
            )
            lse_buf = lax.dynamic_update_slice(
                lse_buf, (row_peak + jnp.log(denominator))[:, :, 0], (2 * pair_index, 0)
            )
            return (mixed_buf, lse_buf)

        mixed_low, lse_buf = lax.fori_loop(
            0,
            HEADS // 2,
            pair_forward,
            (jnp.zeros((frame_rows, D), jnp.bfloat16), jnp.zeros((HEADS, frame_rows), jnp.float32)),
        )
        out_masked = out_full * (head_mask[:, None] * feature_mask[None, :]).astype(jnp.bfloat16)
        branch = (
            jnp.dot(mixed_low, out_masked, preferred_element_type=jnp.float32)
            + shift_table[:, 2] * feature_mask
        )
        gains_table = gains_full.astype(jnp.float32)
        hidden_one, normed_one, inv_one = norm_forward(
            start_vec + branch, gains_table[:, 0], shift_table[:, 4], feature_mask, sub_width
        )
        return (
            start_low,
            qkv_masked,
            projected,
            mixed_low,
            lse_buf,
            out_masked,
            hidden_one,
            normed_one,
            inv_one,
        )

    rows = qkv_weight.shape[0]
    groups = D // rows
    low = jnp.bfloat16
    small = jnp.concatenate([shifts, norm_gains, ffn_bias.reshape(4, rows).T, jnp.zeros((rows, 243), jnp.float32)], axis=1)
    head_own = jnp.concatenate([qkv_weight[:, :D], small], axis=1).astype(low)
    kv_own = jnp.stack([qkv_weight[:, D : 2 * D], qkv_weight[:, 2 * D :]]).astype(low)
    wide_own = jnp.stack([out_weight] + [ffn_in_weight[:, k * D : (k + 1) * D] for k in range(4)]).astype(low)
    down_own = ffn_out_weight.astype(low)
    fused = rows % 16 == 0 and groups % 4 == 0 and dp_size % 2 == 0
    if fused:
        head_full, kv_full, wide_full, down_full = gather_all(groups // 4, head_own, kv_own, wide_own, down_own)
    else:
        head_full = lax.all_gather(head_own, "group", axis=0, tiled=True)
        kv_full = lax.all_gather(kv_own, "group", axis=1, tiled=True)
        wide_full = lax.all_gather(wide_own, "group", axis=1, tiled=True)
        down_full = lax.all_gather(down_own, "group", axis=0, tiled=True)
    head_full = head_full.reshape(D, D + 256)
    kv_full, wide_full = kv_full.reshape(2, D, D), wide_full.reshape(5, D, D)
    ffn_out_full = down_full.reshape(FF, D)
    qkv_full = jnp.concatenate([head_full[:, :D], kv_full[0], kv_full[1]], axis=1)
    out_full = wide_full[0]
    ffn_in_full = jnp.concatenate([wide_full[1], wide_full[2], wide_full[3], wide_full[4]], axis=1)
    shifts_full, gains_full = head_full[:, D : D + 7], head_full[:, D + 7 : D + 9]
    ffn_bias_full = head_full[:, D + 9 : D + 13].reshape(groups, rows, 4).transpose(0, 2, 1).reshape(FF, 1)
    front_state = attention_part(qkv_full, out_full, gains_full, shifts_full)
    (
        start_low,
        qkv_masked,
        projected,
        mixed_low,
        lse_buf,
        out_masked,
        hidden_one,
        normed_one,
        inv_one,
    ) = front_state
    shift_table = shifts_full.astype(jnp.float32)
    gains_table = gains_full.astype(jnp.float32)
    hidden_low = hidden_one.astype(jnp.bfloat16)
    in_masked = ffn_in_full * (feature_mask[:, None] * ffn_mask[None, :]).astype(jnp.bfloat16)
    pre_act = (
        jnp.dot(hidden_low, in_masked, preferred_element_type=jnp.float32)
        + ffn_bias_full[:, 0].astype(jnp.float32) * ffn_mask
    )
    act_low = jax.nn.gelu(pre_act, approximate=False).astype(jnp.bfloat16)
    down_masked = ffn_out_full * (ffn_mask[:, None] * feature_mask[None, :]).astype(jnp.bfloat16)
    ffn_branch = (
        jnp.dot(act_low, down_masked, preferred_element_type=jnp.float32)
        + shift_table[:, 3] * feature_mask
    )
    result, normed_two, inv_two = norm_forward(
        hidden_one + ffn_branch, gains_table[:, 1], shift_table[:, 5], feature_mask, sub_width
    )
    layer_out = (result * live_rows[:, None]).astype(jnp.bfloat16)
    grad_result = cotangent.astype(jnp.float32) * live_rows[:, None]
    grad_two, gain_two, shift_two = norm_backward(
        grad_result, gains_table[:, 1], normed_two, inv_two, feature_mask, sub_width
    )
    grad_ffn = grad_two.astype(jnp.bfloat16)
    ffn_out_part = jnp.einsum("tf,td->fd", act_low, grad_ffn, preferred_element_type=jnp.float32)
    grad_act = jnp.einsum("td,fd->tf", grad_ffn, down_masked, preferred_element_type=jnp.float32)
    grad_pre = (grad_act * gelu_slope(pre_act)).astype(jnp.bfloat16)
    ffn_in_part = jnp.einsum("td,tf->df", hidden_low, grad_pre, preferred_element_type=jnp.float32)
    grad_hidden = (
        jnp.einsum("tf,df->td", grad_pre, in_masked, preferred_element_type=jnp.float32) + grad_two
    )
    grad_one, gain_one, shift_one = norm_backward(
        grad_hidden, gains_table[:, 0], normed_one, inv_one, feature_mask, sub_width
    )
    grad_branch = grad_one.astype(jnp.bfloat16)
    out_part = jnp.einsum("ta,td->ad", mixed_low, grad_branch, preferred_element_type=jnp.float32)
    grad_mixed = jnp.einsum(
        "td,ad->ta", grad_branch, out_masked, preferred_element_type=jnp.float32
    ).astype(jnp.bfloat16)

    def pair_backward(pair_index, grad_proj):
        col_start = pair_index * pair_width
        query_heads, key_heads, value_heads, scores = pair_scores(projected, col_start)
        grad_heads = column_block(grad_mixed, col_start, pair_width).reshape(
            frame_rows, 2, head_dim
        )
        pair_lse = lax.dynamic_slice_in_dim(lse_buf, 2 * pair_index, 2, 0)
        probs = jnp.exp(scores - pair_lse[:, :, None])
        grad_values = jnp.einsum(
            "hqk,qhd->khd",
            probs.astype(jnp.bfloat16),
            grad_heads,
            preferred_element_type=jnp.float32,
        )
        grad_probs = jnp.einsum(
            "qhd,khd->hqk", grad_heads, value_heads, preferred_element_type=jnp.float32
        )
        row_inner = jnp.sum(probs * grad_probs, axis=2, keepdims=True)
        grad_scores = (probs * (grad_probs - row_inner)).astype(jnp.bfloat16)
        grad_queries = (
            jnp.einsum("hqk,khd->qhd", grad_scores, key_heads, preferred_element_type=jnp.float32)
            * score_scale
        )
        grad_keys = (
            jnp.einsum("hqk,qhd->khd", grad_scores, query_heads, preferred_element_type=jnp.float32)
            * score_scale
        )
        grad_proj = lax.dynamic_update_slice(
            grad_proj,
            grad_queries.reshape(frame_rows, pair_width).astype(jnp.bfloat16),
            (0, col_start),
        )
        grad_proj = lax.dynamic_update_slice(
            grad_proj,
            grad_keys.reshape(frame_rows, pair_width).astype(jnp.bfloat16),
            (0, D + col_start),
        )
        grad_proj = lax.dynamic_update_slice(
            grad_proj,
            grad_values.reshape(frame_rows, pair_width).astype(jnp.bfloat16),
            (0, 2 * D + col_start),
        )
        return grad_proj

    grad_proj = lax.fori_loop(
        0, HEADS // 2, pair_backward, jnp.zeros((frame_rows, 3 * D), jnp.bfloat16)
    )
    qkv_part = jnp.einsum("td,tc->dc", start_low, grad_proj, preferred_element_type=jnp.float32)
    grad_start = (
        jnp.einsum("tc,dc->td", grad_proj, qkv_masked, preferred_element_type=jnp.float32)
        + grad_one
    )
    frames_grad = grad_start * (1.0 - masked[:, None])
    proj_sums = jnp.sum(grad_proj, axis=0, dtype=jnp.float32)
    shifts_part = jnp.stack(
        [
            proj_sums[:D],
            proj_sums[2 * D :],
            jnp.sum(grad_branch, axis=0, dtype=jnp.float32),
            jnp.sum(grad_ffn, axis=0, dtype=jnp.float32),
            shift_one,
            shift_two,
            jnp.sum(grad_start * masked[:, None], axis=0),
        ],
        axis=1,
    )
    gains_part = jnp.stack([gain_one, gain_two], axis=1)
    ffn_bias_part = jnp.sum(grad_pre, axis=0, dtype=jnp.float32)[:, None]
    bias_cols = ffn_bias_part.reshape(groups, 4, rows).transpose(0, 2, 1).reshape(D, 4)
    small_part = jnp.concatenate([shifts_part, gains_part, bias_cols, jnp.zeros((D, 243), jnp.float32)], axis=1)
    head_part = jnp.concatenate([qkv_part[:, :D], small_part], axis=1)
    parts = [head_part, qkv_part[:, D : 2 * D], qkv_part[:, 2 * D :], out_part]
    parts += [ffn_in_part[:, k * D : (k + 1) * D] for k in range(4)] + [ffn_out_part]
    if fused:
        shaped = [p.astype(low).reshape(groups // 4, 2, 2, p.shape[0] // groups, p.shape[1]) for p in parts]
        crosses = [True, False, False, False, True, True, False, False, False]
        owned = reduce_all(groups // 4, shaped, crosses)
        if dp_size > 2:
            owned = [0.5 * lax.psum(p, "dp").astype(jnp.float32) for p in owned]
    else:
        owned = [lax.psum_scatter(p, "group", scatter_dimension=0, tiled=True) for p in parts]
        owned = [lax.psum(p.astype(low), "dp") for p in owned]
    owned = [p.astype(jnp.float32) for p in owned]
    qkv_grad = jnp.concatenate([owned[0][:, :D], owned[1], owned[2]], axis=1)
    out_grad, ffn_in_grad, ffn_out_grad = owned[3], jnp.concatenate(owned[4:8], axis=1), owned[8]
    shifts_grad, gains_grad = owned[0][:, D : D + 7], owned[0][:, D + 7 : D + 9]
    ffn_bias_grad = owned[0][:, D + 9 : D + 13].T.reshape(4 * rows, 1)
    return (
        layer_out,
        frames_grad,
        qkv_grad,
        out_grad,
        ffn_in_grad,
        ffn_out_grad,
        ffn_bias_grad,
        gains_grad,
        shifts_grad,
    )


def solution(mesh):
    placed = (
        P(("group", "dp"), None),
        P(("group", "dp"), None),
        P(("group", "dp")),
        P("group"),
        P("group"),
        P("group"),
        P("group", None),
        P("group", None),
        P("group", None),
        P("group", None),
        P("group", None),
        P("group", None),
        P("group", None),
        P(("group", "dp"), None),
    )
    return jax.shard_map(
        functools.partial(on_device, mesh.shape["dp"]),
        mesh=mesh,
        in_specs=placed,
        out_specs=(
            P(("group", "dp"), None),
            P(("group", "dp"), None),
            P("group", None),
            P("group", None),
            P("group", None),
            P("group", None),
            P("group", None),
            P("group", None),
            P("group", None),
        ),
        check_vma=False,
    )
```

```python
import functools

import jax
import jax.numpy as jnp
from jax import lax
from jax.experimental import pallas as pl
from jax.experimental.pallas import tpu as pltpu
from jax.sharding import PartitionSpec as P

D = 768
HEADS = 12
FF = 3072
SPAN = 10
CHUNKS = 3
CHUNK = D // CHUNKS
CHUNK_PAIRS = HEADS // (2 * CHUNKS)
SMALL = 256
BLOCK = 512

norm_eps = 1e-05
far_score = -float(2**30)
root_half = 0.7071067811865476
inv_root_tau = 0.3989422804014327

F32, LOW = jnp.float32, jnp.bfloat16
NN = (((1,), (0,)), ((), ()))
NT = (((1,), (1,)), ((), ()))
TN = (((0,), (0,)), ((), ()))
MESH = pl.DeviceIdType.MESH
MIB = 2**20


def dot(a, b, dims=NN):
    return lax.dot_general(a, b, dims, preferred_element_type=F32)


def lane_row(n):
    return lax.broadcasted_iota(jnp.int32, (1, n), 1)


def row_sum(v):
    return jnp.sum(v, axis=1, keepdims=True)


def col_sum(v):
    return jnp.sum(v, axis=0, keepdims=True)


def subnet(codes):
    width = (D // 6) * (4 + codes[0])
    return width, (HEADS - HEADS // 3 + codes[1]) * (D // HEADS), (width * (6 + codes[2])) // 2


class Place:
    def __init__(self, depth):
        group, dp = lax.axis_index("group"), lax.axis_index("dp")
        self.depth = depth
        self.z, self.x, self.c, self.y = group // 4, (group // 2) % 2, group % 2, dp % 2
        self.dp = dp
        self.core_dev = (group + 1 - 2 * self.c, dp)
        self.x_dev = (group + 2 - 4 * self.x, dp)
        self.y_dev = (group, dp + 1 - 2 * self.y)

    def z_at(self, step):
        return lax.rem(self.z + step, self.depth)

    def z_from(self, step):
        return lax.rem(self.z - step + self.depth, self.depth)

    def z_dev(self, step):
        return ((self.z_at(step) * 2 + self.x) * 2 + self.c, self.dp)

    def greet(self):
        barrier = pltpu.get_barrier_semaphore()
        devs = [self.core_dev, self.x_dev, self.y_dev] + [self.z_dev(s) for s in range(1, self.depth)]
        for dev in devs:
            pl.semaphore_signal(barrier, inc=1, device_id=dev, device_id_type=MESH)
        pl.semaphore_wait(barrier, len(devs))


class Copies:
    def __init__(self, send_sems, recv_sems):
        self.send_sems, self.recv_sems, self.made = send_sems, recv_sems, []

    def to(self, src, dst, dev):
        spot = len(self.made)
        copy = pltpu.make_async_remote_copy(
            src_ref=src,
            dst_ref=dst,
            send_sem=self.send_sems.at[spot],
            recv_sem=self.recv_sems.at[spot],
            device_id=dev,
            device_id_type=MESH,
        )
        self.made.append(copy)
        return copy

    def finish(self):
        for copy in self.made:
            copy.wait_send()


def halves(width, y):
    half = width // 2
    mine = pl.ds(pl.multiple_of(y * half, 128), half)
    other = pl.ds(pl.multiple_of((1 - y) * half, 128), half)
    return mine, other


def gather_cross(here, copies, own, at, width):
    z, x, c = here.z, here.x, here.c
    mine, other = halves(width, here.y)
    full = slice(None)
    steps = range(1, here.depth)

    def same(zz, xx, cols, dev):
        return copies.to(at(zz, xx, c, cols), at(zz, xx, c, cols), dev)

    first = copies.to(own(mine), at(z, x, c, mine), here.x_dev)
    own_core = copies.to(own(full), at(z, x, c, full), here.core_dev)
    own_z = [copies.to(own(mine), at(z, x, c, mine), here.z_dev(s)) for s in steps]
    side_z = [same(z, 1 - x, mine, here.z_dev(s)) for s in steps]
    spots = [(z, 1 - x)] + [(here.z_from(s), x) for s in steps] + [(here.z_from(s), 1 - x) for s in steps]
    y_hops = [same(zz, xx, mine, here.y_dev) for zz, xx in spots]
    core_mine = [same(zz, xx, mine, here.core_dev) for zz, xx in spots]
    core_other = [same(zz, xx, other, here.core_dev) for zz, xx in spots]
    n = len(own_z)

    def stage0():
        first.start()
        for copy in own_z:
            copy.start()
        own_core.start()

    def stage1():
        first.wait_recv()
        for copy in side_z:
            copy.start()
        y_hops[0].start()
        core_mine[0].start()

    def stage2():
        for k in range(n):
            own_z[k].wait_recv()
            y_hops[1 + k].start()
            core_mine[1 + k].start()

    def stage3():
        for k in range(n):
            side_z[k].wait_recv()
            y_hops[1 + n + k].start()
            core_mine[1 + n + k].start()

    def stage4():
        for k in range(1 + 2 * n):
            y_hops[k].wait_recv()
            core_other[k].start()

    def stage5():
        own_core.wait_recv()
        for copy in core_mine + core_other:
            copy.wait_recv()

    return [stage0, stage1, stage2, stage3, stage4, stage5]


def gather_line(here, copies, own, at, width):
    z, x, c = here.z, here.x, here.c
    mine, other = halves(width, here.y)
    full = slice(None)
    steps = range(1, here.depth)

    def same(zz, xx, cols, dev):
        return copies.to(at(zz, xx, c, cols), at(zz, xx, c, cols), dev)

    own_z = [copies.to(own(mine), at(z, x, c, mine), here.z_dev(s)) for s in steps]
    own_x = copies.to(own(full), at(z, x, c, full), here.x_dev)
    own_core = copies.to(own(full), at(z, x, c, full), here.core_dev)
    froms = [here.z_from(s) for s in steps]
    y_hops = [same(zz, x, mine, here.y_dev) for zz in froms]
    x_mine = [same(zz, x, mine, here.x_dev) for zz in froms]
    x_other = [same(zz, x, other, here.x_dev) for zz in froms]
    core_side = same(z, 1 - x, full, here.core_dev)
    core_mine = [same(zz, x, mine, here.core_dev) for zz in froms]
    core_other = [same(zz, x, other, here.core_dev) for zz in froms]
    core_x_mine = [same(zz, 1 - x, mine, here.core_dev) for zz in froms]
    core_x_other = [same(zz, 1 - x, other, here.core_dev) for zz in froms]
    n = len(own_z)

    def stage0():
        for copy in own_z:
            copy.start()
        own_x.start()
        own_core.start()

    def stage1():
        for k in range(n):
            own_z[k].wait_recv()
            y_hops[k].start()
            x_mine[k].start()
            core_mine[k].start()

    def stage2():
        own_x.wait_recv()
        core_side.start()

    def stage3():
        for k in range(n):
            y_hops[k].wait_recv()
            x_other[k].start()
            core_other[k].start()

    def stage4():
        for k in range(n):
            x_mine[k].wait_recv()
            core_x_mine[k].start()
        for k in range(n):
            x_other[k].wait_recv()
            core_x_other[k].start()

    def stage5():
        own_core.wait_recv()
        core_side.wait_recv()
        for copy in core_mine + core_other + core_x_mine + core_x_other:
            copy.wait_recv()

    return [stage0, stage1, stage2, stage3, stage4, stage5]


def gather_cross_copies(depth):
    return 2 + (depth - 1) * 2 + 3 * (2 * depth - 1)


def gather_line_copies(depth):
    return (depth - 1) * 8 + 3


def plus(a, b):
    return (a.astype(F32) + b.astype(F32)).astype(LOW)


def reduce_part(here, copies, sibling, kept, room, final, width, cross):
    z, x, depth = here.z, here.x, here.depth
    mine, other = halves(width, here.y)
    steps = range(1, depth)
    if cross:
        first, second, third, fourth, fifth = room
        core = copies.to(sibling, first, here.core_dev)
        to_y = copies.to(first.at[:, :, :, other], second, here.y_dev)
        to_z = [copies.to(second.at[here.z_at(s)], third.at[s - 1], here.z_dev(s)) for s in steps]
        to_x = copies.to(fourth.at[1 - x], fifth, here.x_dev)
    else:
        first, second, third, fourth = room
        core = copies.to(sibling, first, here.core_dev)
        to_x = copies.to(first.at[:, 1 - x], second, here.x_dev)
        to_y = copies.to(second.at[:, :, other], third, here.y_dev)
        to_z = [copies.to(third.at[here.z_at(s)], fourth.at[s - 1], here.z_dev(s)) for s in steps]
    back = copies.to(final.at[:, mine], final.at[:, mine], here.y_dev)

    def stage0():
        core.start()

    def stage1():
        core.wait_recv()

        @pl.loop(0, depth)
        def _(zz):
            for xx in range(2):
                first[zz, xx] = plus(kept(zz, xx), first[zz, xx])

        if cross:
            to_y.start()
        else:
            to_x.start()

    def stage2():
        if cross:
            to_y.wait_recv()

            @pl.loop(0, depth)
            def _(zz):
                for xx in range(2):
                    second[zz, xx] = plus(first[zz, xx, :, mine], second[zz, xx])

            for copy in to_z:
                copy.start()
        else:
            to_x.wait_recv()

            @pl.loop(0, depth)
            def _(zz):
                second[zz] = plus(first[zz, x], second[zz])

            to_y.start()

    def stage3():
        if cross:
            for copy in to_z:
                copy.wait_recv()

            @pl.loop(0, 2)
            def _(xx):
                total = second[z, xx].astype(F32)
                for s in steps:
                    total += third[s - 1, xx].astype(F32)
                fourth[xx] = total.astype(LOW)

            to_x.start()
        else:
            to_y.wait_recv()

            @pl.loop(0, depth)
            def _(zz):
                third[zz] = plus(second[zz, :, mine], third[zz])

            for copy in to_z:
                copy.start()

    def stage4():
        if cross:
            to_x.wait_recv()
            final[:, mine] = plus(fourth[x], fifth[...])
        else:
            for copy in to_z:
                copy.wait_recv()
            total = third[z].astype(F32)
            for s in steps:
                total += fourth[s - 1].astype(F32)
            final[:, mine] = total.astype(LOW)
        back.start()

    def stage5():
        back.wait_recv()

    return [stage0, stage1, stage2, stage3, stage4, stage5]


def reduce_room(depth, rows, width, cross):
    half = width // 2
    if cross:
        shapes = [(depth, 2, rows, width), (depth, 2, rows, half), (depth - 1, 2, rows, half), (2, rows, half), (rows, half)]
    else:
        shapes = [(depth, 2, rows, width), (depth, rows, width), (depth, rows, half), (depth - 1, rows, half)]
    return [pltpu.VMEM(shape, LOW) for shape in shapes]


def reduce_copies(depth):
    return 4 + depth - 1


def run(plans, todo):
    for plan, stage in todo:
        plans[plan][stage]()


def hook(at, actions):
    for k, action in actions.items():
        pl.when(at == k)(action)


def split3(v):
    high = v.astype(LOW).astype(F32)
    rest = v - high
    middle = rest.astype(LOW).astype(F32)
    return high, middle, rest - middle


def frame_tables(lengths, starts, frames, edge, query_side, key_side):
    lane = lane_row(128)
    place = lax.broadcasted_iota(jnp.int32, (frames, 1), 0)
    first, second = lengths[0, 0], lengths[0, 0] + lengths[0, 1]
    segment = (place >= first).astype(jnp.int32) + (place >= second).astype(jnp.int32)
    spread = jnp.broadcast_to(starts[...][:, None, :], (frames // 128, 128, 128)).reshape(frames, 128)
    start = jnp.max(jnp.where(lane == lax.rem(place, 128), spread, 0), axis=1, keepdims=True)
    edge[0:16, :] = jnp.full((16, 1), -1, jnp.int32)
    edge[pl.ds(16, frames), :] = jnp.where(start == 1, segment, -1)
    masked = segment < 0
    for offset in range(SPAN):
        masked = masked | (edge[pl.ds(16 - offset, frames), :] == segment)
    live = segment < 2
    masked = masked & live
    query_side[...] = jnp.where((lane < 3) & (lane != segment), far_score, 0.0).astype(LOW)
    ones = (lane == segment) | ((lane >= 3) & (lane < 6)) | ((lane == 6) & live) | ((lane == 7) & masked)
    key_side[...] = jnp.where(ones, 1.0, 0.0).astype(LOW)


def attend(proj, chunk, query_side, key_side, mixed, peaks, actions):
    frames = mixed.shape[0]
    blocks = frames // BLOCK
    lane = lane_row(128)

    @pl.loop(0, CHUNK_PAIRS)
    def _(part):
        pair = chunk * CHUNK_PAIRS + part
        col = pl.multiple_of(part * 128, 128)

        @pl.loop(0, blocks)
        def _(block):
            hook(pair * blocks + block, actions)
            rows = pl.ds(pl.multiple_of(block * BLOCK, BLOCK), BLOCK)
            query = proj[rows, pl.ds(col, 128)]
            keys = jnp.concatenate([proj[:, pl.ds(pl.multiple_of(CHUNK + col, 128), 128)], key_side[...]], axis=1)
            values = proj[:, pl.ds(pl.multiple_of(2 * CHUNK + col, 128), 128)]
            values = jnp.concatenate([values, jnp.ones((frames, 128), LOW)], axis=1)
            side = query_side[rows, :]
            found = []
            for h in range(2):
                own = jnp.where((lane < 64) == (h == 0), query, jnp.zeros_like(query))
                scores = dot(jnp.concatenate([own, side], axis=1), keys, NT)
                peak = jnp.max(scores, axis=1, keepdims=True)
                weights = jnp.exp(scores - peak).astype(LOW)
                sums = dot(weights, values)
                total = sums[:, 128:]
                high, middle, low = split3(-(peak + jnp.log(total)))
                table = jnp.where(lane == 3, high, jnp.where(lane == 4, middle, jnp.where(lane == 5, low, side.astype(F32))))
                peaks[2 * pair + h, rows, :] = table.astype(LOW)
                found.append(sums[:, :128] / total)
            mixed[rows, pl.ds(pl.multiple_of(pair * 128, 128), 128)] = jnp.where(lane < 64, found[0], found[1]).astype(LOW)


def attend_back(proj, chunk, peaks, key_side, grad_mixed, mixed, grad_proj, inner, grad_query, actions):
    frames = mixed.shape[0]
    blocks = frames // BLOCK
    lane = lane_row(128)

    @pl.loop(0, CHUNK_PAIRS)
    def _(part):
        pair = chunk * CHUNK_PAIRS + part
        all_col = pl.ds(pl.multiple_of(pair * 128, 128), 128)
        query_cols = pl.ds(pl.multiple_of(part * 128, 128), 128)
        key_cols = pl.ds(pl.multiple_of(CHUNK + part * 128, 128), 128)
        value_cols = pl.ds(pl.multiple_of(2 * CHUNK + part * 128, 128), 128)
        prod = grad_mixed[:, all_col].astype(F32) * mixed[:, all_col].astype(F32)
        for h in range(2):
            high, middle, low = split3(-row_sum(jnp.where((lane < 64) == (h == 0), prod, 0.0)))
            table = jnp.where(lane == 3, high, jnp.where(lane == 4, middle, jnp.where(lane == 5, low, 0.0)))
            inner[h] = table.astype(LOW)

        @pl.loop(0, blocks)
        def _(block):
            hook(pair * blocks + block, actions)
            rows = pl.ds(pl.multiple_of(block * BLOCK, BLOCK), BLOCK)
            key, value, side = proj[rows, key_cols], proj[rows, value_cols], key_side[rows, :]
            keys = jnp.concatenate([key, side], axis=1)
            values = jnp.concatenate([value, side], axis=1)
            query, grad = proj[:, query_cols], grad_mixed[:, all_col]
            grad_v = grad_k = grad_q = 0.0
            for h in range(2):
                own = (lane < 64) == (h == 0)
                query_h = jnp.where(own, query, jnp.zeros_like(query))
                grad_h = jnp.where(own, grad, jnp.zeros_like(grad))
                key_h = jnp.where(own, key, jnp.zeros_like(key))
                probs = jnp.exp(dot(keys, jnp.concatenate([query_h, peaks[2 * part + h]], axis=1), NT))
                shifted = dot(values, jnp.concatenate([grad_h, inner[h]], axis=1), NT)
                grad_s = (probs * shifted).astype(LOW)
                grad_v += dot(probs.astype(LOW), grad_h)
                grad_k += dot(grad_s, query_h)
                grad_q += dot(grad_s, key_h, TN)
            grad_proj[rows, key_cols] = grad_k.astype(LOW)
            grad_proj[rows, value_cols] = grad_v.astype(LOW)

            @pl.when(block == 0)
            def _():
                grad_query[...] = grad_q

            @pl.when(block > 0)
            def _():
                grad_query[...] += grad_q

        grad_proj[:, query_cols] = (grad_query[...] * 0.125).astype(LOW)


VM = pl.BlockSpec(memory_space=pltpu.VMEM)
SM = pl.BlockSpec(memory_space=pltpu.SMEM)
HBM = pl.BlockSpec(memory_space=pl.ANY)


def flat(value):
    return value.reshape(D, value.shape[-1])


def chunk_cols(matrix, j):
    return [matrix[:, k * D + j * CHUNK : k * D + (j + 1) * CHUNK] for k in range(3)]


GATHER_FIRST = [(0, 0), (1, 0), (0, 1), (0, 2), (0, 3), (1, 1), (2, 0), (0, 4), (1, 2), (3, 0), (4, 0), (0, 5)]
GATHER_THEN = {
    0: [(1, 3), (2, 1), (2, 2), (3, 1)],
    1: [(1, 4)],
    2: [(2, 3), (3, 2)],
    3: [(4, 1), (4, 2), (2, 4)],
    6: [(3, 3)],
    7: [(4, 3)],
    11: [(3, 4), (4, 4)],
}
GATHER_CHUNK = {1: [(1, 5)], 2: [(2, 5)]}
GATHER_LAST = [(3, 5), (4, 5)]


def front(depth, codes, lengths, starts, frames, weights):
    count = frames.shape[0]

    def body(codes, lengths, starts, frames, small_full, chunk_weight, proj, x0, mixed, peaks, key_side, small, query_side, edge, early, enter, actions):
        width, heads, _ = subnet(codes)
        features = (lane_row(D) < width).astype(F32)
        frame_tables(lengths, starts, count, edge, query_side, key_side)
        early()
        small[...] = flat(small_full()).astype(F32).T[0:16, :]
        masked = key_side[:, 7:8].astype(F32)
        start = jnp.where(masked > 0, small[6:7, :], frames[...].astype(F32)) * features
        x0[...] = start.astype(LOW)
        for j in range(CHUNKS):
            enter(j)
            cols = slice(j * CHUNK, (j + 1) * CHUNK)
            active = (lane_row(CHUNK) + j * CHUNK < heads).astype(F32)
            value = dot(x0[...], flat(chunk_weight(j)))
            for k in range(3):
                piece = value[:, k * CHUNK : (k + 1) * CHUNK]
                if k != 1:
                    piece = piece + small[k // 2 : k // 2 + 1, cols]
                piece = (piece * active).astype(LOW)
                proj[j, :, k * CHUNK : (k + 1) * CHUNK] = piece * jnp.asarray(0.125, LOW) if k == 0 else piece
            attend(proj.at[j], j, query_side, key_side, mixed, peaks, actions)

    shape = jax.ShapeDtypeStruct
    found = (
        shape((CHUNKS, count, D), LOW),
        shape((count, D), LOW),
        shape((count, D), LOW),
        shape((HEADS, count, 128), LOW),
        shape((count, 128), LOW),
        shape((16, D), F32),
    )
    scratch = [pltpu.VMEM((count, 128), LOW), pltpu.VMEM((count + 16, 1), jnp.int32)]
    params = dict(has_side_effects=True, vmem_limit_bytes=62 * MIB)
    if not depth:

        def plain(codes, lengths, starts, frames, head, chunks, *rest):
            def weight(j):
                return chunks[j - 1] if j else head[:, :D]

            body(codes, lengths, starts, frames, lambda: head[:, D : D + 128], weight, *rest, lambda: None, lambda j: None, {})

        return pl.pallas_call(
            plain,
            out_shape=found,
            in_specs=[SM, SM, VM, VM, VM, VM],
            out_specs=(VM,) * 6,
            scratch_shapes=scratch,
            compiler_params=pltpu.CompilerParams(vmem_limit_bytes=62 * MIB),
            name="front_plain",
        )(codes, lengths, starts, frames, *weights)

    rows, tall = weights[0].shape[0], weights[3].shape[0]

    def fused(*refs):
        codes, lengths, starts, frames = refs[:4]
        qkv_own, out_own, in_own, down_own, bias_own, gains_own, shifts_own = refs[4:11]
        proj, x0, mixed, peaks, key_side, small, head, chunks, wide, down = refs[11:21]
        query_side, edge, pad, head_low, chunks_low, wide_low, down_low, send, recv, local = refs[21:]
        here = Place(depth)
        z, x, c = here.z, here.x, here.c
        copies = Copies(send, recv)

        def flat_plan(gather, own, full, width):
            return gather(here, copies, lambda cols: own.at[:, cols], lambda zz, xx, cc, cols: full.at[zz, xx, cc, :, cols], width)

        plans = [
            flat_plan(gather_cross, head_low, head, D + SMALL),
            flat_plan(gather_line, chunks_low.at[0], chunks.at[0], D),
            flat_plan(gather_line, chunks_low.at[1], chunks.at[1], D),
            flat_plan(gather_cross, down_low, down, D),
            gather_line(here, copies, lambda cols: wide_low.at[:, :, cols], lambda zz, xx, cc, cols: wide.at[:, zz, xx, cc, :, cols], D),
        ]
        keep = [
            pltpu.make_async_copy(head_low, head.at[z, x, c], local.at[0]),
            pltpu.make_async_copy(chunks_low, chunks.at[:, z, x, c], local.at[1]),
            pltpu.make_async_copy(wide_low, wide.at[:, z, x, c], local.at[2]),
            pltpu.make_async_copy(down_low, down.at[z, x, c], local.at[3]),
        ]
        pad[...] = jnp.zeros_like(pad)
        pad[:, 0:7] = shifts_own[...]
        pad[:, 7:9] = gains_own[...]
        for j in range(4):
            pad[:, 9 + j : 10 + j] = bias_own[j * rows : (j + 1) * rows, :]
        for j in range(CHUNKS):
            low = jnp.concatenate(chunk_cols(qkv_own, j), axis=1).astype(LOW)
            if j:
                chunks_low[j - 1] = low
            else:
                head_low[:, :D] = low
        head_low[:, D:] = pad[...].astype(LOW)
        wide_low[0] = out_own[...].astype(LOW)
        for k in range(4):
            wide_low[1 + k] = in_own[:, k * D : (k + 1) * D].astype(LOW)
        down_low[...] = down_own[...].astype(LOW)
        here.greet()

        def early():
            for copy in keep:
                copy.start()
            run(plans, GATHER_FIRST)
            keep[0].wait()
            keep[1].wait()

        def enter(j):
            run(plans, GATHER_CHUNK.get(j, []))

        actions = {k: functools.partial(run, plans, todo) for k, todo in GATHER_THEN.items()}
        body(codes, lengths, starts, frames, lambda: head[:, :, :, :, D : D + 128], lambda j: chunks[j - 1] if j else head[:, :, :, :, :D],
             proj, x0, mixed, peaks, key_side, small, query_side, edge, early, enter, actions)
        run(plans, GATHER_LAST)
        keep[2].wait()
        keep[3].wait()
        copies.finish()

    copies = 2 * gather_cross_copies(depth) + 3 * gather_line_copies(depth)
    return pl.pallas_call(
        fused,
        out_shape=found
        + (
            shape((depth, 2, 2, rows, D + SMALL), LOW),
            shape((2, depth, 2, 2, rows, D), LOW),
            shape((5, depth, 2, 2, rows, D), LOW),
            shape((depth, 2, 2, tall, D), LOW),
        ),
        in_specs=[SM, SM] + [VM] * 9,
        out_specs=(VM,) * 8 + (HBM, HBM),
        scratch_shapes=scratch
        + [
            pltpu.VMEM((rows, SMALL), F32),
            pltpu.VMEM((rows, D + SMALL), LOW),
            pltpu.VMEM((2, rows, D), LOW),
            pltpu.VMEM((5, rows, D), LOW),
            pltpu.VMEM((tall, D), LOW),
            pltpu.SemaphoreType.DMA((copies,)),
            pltpu.SemaphoreType.DMA((copies,)),
            pltpu.SemaphoreType.DMA((4,)),
        ],
        compiler_params=pltpu.CompilerParams(collective_id=0, **params),
        name="front",
    )(codes, lengths, starts, frames, *weights)


def normal_parts(v):
    bell = jnp.exp(v * v * -0.5)
    t = 1.0 / (1.0 + (0.3275911 * root_half) * jnp.abs(v))
    tail = t * (0.127414796 + t * (-0.142248368 + t * (0.7107068705 + t * (-0.7265760135 + t * 0.5307027145)))) * bell
    return jnp.where(v < 0, tail, 1.0 - tail), bell


def middle(codes, mixed, x0, cotangent, key_side, wide, down, small, bias):
    count = mixed.shape[0]
    size = BLOCK
    steps = count // size

    def kernel(codes, mixed, x0, cotangent, key_side, wide, down, small, bias, out, grad_mixed, grad_one, wide_part, down_part,
               sums, bias_sums, wide_v, down_v, mixed_all, hidden_all, act_all, pre_all, ffn_all, branch_all, slope, stage, in_sems, out_sems):
        step = pl.program_id(0)
        width, heads, units = subnet(codes)
        features = (lane_row(D) < width).astype(F32)
        active = (lane_row(D) < heads).astype(F32)
        scale = 1.0 / width.astype(F32)
        rows = pl.ds(pl.multiple_of(step * size, size), size)
        loads = [pltpu.make_async_copy(wide.at[k], wide_v.at[k], in_sems.at[k]) for k in range(5)]
        loads += [pltpu.make_async_copy(down.at[k], down_v.at[k], in_sems.at[5 + k]) for k in range(4)]

        def ready(k):
            pl.when(step == 0)(loads[k].wait)

        @pl.when(step == 0)
        def _():
            for load in loads:
                load.start()
            sums[...] = jnp.zeros_like(sums)
            bias_sums[...] = jnp.zeros_like(bias_sums)

        def param(k):
            return small[k : k + 1, :]

        mixed_all[rows, :] = mixed[...]
        ready(0)
        resid = x0[...].astype(F32) + (dot(mixed[...], wide_v[0]) + param(2)) * features
        centered = (resid - row_sum(resid) * scale) * features
        inv_one = lax.rsqrt(row_sum(centered * centered) * scale + norm_eps)
        normed_one = centered * inv_one
        hidden = (normed_one * param(7) + param(4)) * features
        hidden_low = hidden.astype(LOW)
        hidden_all[rows, :] = hidden_low
        branch = 0.0
        for j in range(4):
            ready(1 + j)
            unit_mask = (lane_row(D) + j * D < units).astype(F32)
            pre = (dot(hidden_low, wide_v[1 + j]) + bias[j : j + 1, :]) * unit_mask
            share, bell = normal_parts(pre)
            act = (pre * share).astype(LOW)
            act_all[j, rows, :] = act
            slope[j] = (share + pre * bell * inv_root_tau) * unit_mask
            ready(5 + j)
            branch += dot(act, down_v[j])
        resid = hidden + (branch + param(3)) * features
        centered = (resid - row_sum(resid) * scale) * features
        inv_two = lax.rsqrt(row_sum(centered * centered) * scale + norm_eps)
        normed_two = centered * inv_two
        live = key_side[:, 6:7].astype(F32)
        out[...] = ((normed_two * param(8) + param(5)) * features * live).astype(LOW)
        grad_out = cotangent[...].astype(F32) * live
        grad_n = grad_out * (param(8) * features)
        grad_two = inv_two * features * (grad_n - row_sum(grad_n) * scale - normed_two * (row_sum(grad_n * normed_two) * scale))
        grad_ffn = grad_two.astype(LOW)
        ffn_all[rows, :] = grad_ffn
        back = 0.0
        for j in range(4):
            grad_pre = (dot(grad_ffn, down_v[j], NT) * slope[j]).astype(LOW)
            pre_all[j, rows, :] = grad_pre
            bias_sums[j : j + 1, :] += col_sum(grad_pre.astype(F32))
            back += dot(grad_pre, wide_v[1 + j], NT)
        grad_hidden = grad_two + back * features
        grad_n = grad_hidden * (param(7) * features)
        grad_res = inv_one * features * (grad_n - row_sum(grad_n) * scale - normed_one * (row_sum(grad_n * normed_one) * scale))
        grad_one[...] = grad_res
        grad_branch = grad_res.astype(LOW)
        branch_all[rows, :] = grad_branch
        grad_mixed[...] = (dot(grad_branch, wide_v[0], NT) * active).astype(LOW)
        sums[0:1, :] += col_sum(grad_branch.astype(F32))
        sums[1:2, :] += col_sum(grad_ffn.astype(F32))
        sums[2:3, :] += col_sum(grad_hidden) * features
        sums[3:4, :] += col_sum(grad_out) * features
        sums[4:5, :] += col_sum(grad_hidden * normed_one)
        sums[5:6, :] += col_sum(grad_out * normed_two)

        @pl.when(step == steps - 1)
        def _():
            sent = []
            for k in range(9):
                if k >= 2:
                    sent[k - 2].wait()
                if k < 4:
                    value, place = dot(act_all[k], ffn_all[...], TN), down_part.at[k]
                elif k < 8:
                    value, place = dot(hidden_all[...], pre_all[k - 4], TN), wide_part.at[k - 3]
                else:
                    value, place = dot(mixed_all[...], branch_all[...], TN), wide_part.at[0]
                stage[k % 2] = value.astype(LOW)
                sent.append(pltpu.make_async_copy(stage.at[k % 2], place, out_sems.at[k % 2]))
                sent[k].start()
            sent[7].wait()
            sent[8].wait()

    block = pl.BlockSpec((size, D), lambda i: (i, 0))
    shape = jax.ShapeDtypeStruct
    return pl.pallas_call(
        kernel,
        grid=(steps,),
        in_specs=[SM, block, block, block, pl.BlockSpec((size, 128), lambda i: (i, 0)), HBM, HBM]
        + [pl.BlockSpec((16, D), lambda i: (0, 0)), pl.BlockSpec((4, D), lambda i: (0, 0))],
        out_specs=(block, block, block, HBM, HBM, pl.BlockSpec((8, D), lambda i: (0, 0)), pl.BlockSpec((4, D), lambda i: (0, 0))),
        out_shape=(
            shape((count, D), LOW),
            shape((count, D), LOW),
            shape((count, D), F32),
            shape((5, D, D), LOW),
            shape((4, D, D), LOW),
            shape((8, D), F32),
            shape((4, D), F32),
        ),
        scratch_shapes=[
            pltpu.VMEM((5, D, D), LOW),
            pltpu.VMEM((4, D, D), LOW),
            pltpu.VMEM((count, D), LOW),
            pltpu.VMEM((count, D), LOW),
            pltpu.VMEM((4, count, D), LOW),
            pltpu.VMEM((4, count, D), LOW),
            pltpu.VMEM((count, D), LOW),
            pltpu.VMEM((count, D), LOW),
            pltpu.VMEM((4, size, D), F32),
            pltpu.VMEM((2, D, D), LOW),
            pltpu.SemaphoreType.DMA((9,)),
            pltpu.SemaphoreType.DMA((2,)),
        ],
        compiler_params=pltpu.CompilerParams(vmem_limit_bytes=62 * MIB),
        name="middle",
    )(codes, mixed, x0, cotangent, key_side, wide, down, small, bias)


SUM_CROSS = [False, True, False, False, False, False, False, False, False, False, True, False, True]
SUM_THEN = {
    2: [(0, 1), (1, 1), (2, 1)],
    3: [(3, 1), (4, 1), (5, 1)],
    5: [(2, 2), (9, 1), (0, 3)],
    6: [(3, 2), (1, 3)],
    7: [(2, 3), (0, 4), (4, 2)],
    9: [(10, 1), (6, 2), (3, 4), (5, 3), (2, 5)],
    10: [(4, 4), (7, 2)],
    11: [(5, 4), (10, 2), (8, 2)],
}
SUM_CHUNK = {
    0: [(9, 0), (6, 1), (7, 1), (8, 1), (0, 2), (1, 2)],
    1: [(10, 0), (3, 3), (0, 5), (5, 2), (2, 4), (4, 3)],
    2: [(11, 0), (12, 0)],
}
SUM_LAST = [
    (6, 3), (3, 5), (4, 5), (9, 2), (1, 4), (7, 3), (5, 5), (10, 3), (8, 3), (11, 1),
    (12, 1), (10, 4), (6, 4), (9, 3), (1, 5), (7, 4), (11, 2), (12, 2), (8, 4), (10, 5),
    (6, 5), (7, 5), (9, 4), (11, 3), (8, 5), (9, 5), (12, 3), (11, 4), (12, 4), (11, 5),
    (12, 5),
]


def back(depth, codes, proj, peaks, key_side, grad_mixed, mixed, x0, grad_one, chunk_full, sums, bias_sums, wide_part, down_part):
    count = mixed.shape[0]
    heads = HEADS // CHUNKS

    def body(codes, proj, peaks, key_side, grad_mixed, mixed, x0, grad_one, chunk_full, sums, bias_sums, frames_grad,
             proj_v, peaks_v, weight_v, grad_proj, inner, grad_query, total, rows_v, loads, weight_at, put, actions, chunk_done):
        width, _, _ = subnet(codes)
        features = (lane_row(D) < width).astype(F32)
        one = pltpu.make_async_copy(grad_one, total, loads.at[6])
        out = pltpu.make_async_copy(total, frames_grad, loads.at[7])

        def fetch(j):
            return [
                pltpu.make_async_copy(proj.at[j], proj_v.at[j % 2], loads.at[j % 2]),
                pltpu.make_async_copy(peaks.at[pl.ds(j * heads, heads)], peaks_v.at[j % 2], loads.at[2 + j % 2]),
                pltpu.make_async_copy(weight_at(j), weight_v.at[j % 2], loads.at[4 + j % 2]),
            ]

        for copy in fetch(0):
            copy.start()
        one.start()
        rows_v[...] = jnp.zeros_like(rows_v)
        rows_v[2:6, :] = sums[0:4, :]
        rows_v[7:9, :] = sums[4:6, :]
        rows_v[9:13, :] = bias_sums[...]
        for j in range(CHUNKS):
            for copy in fetch(j):
                copy.wait()
            if j + 1 < CHUNKS:
                for copy in fetch(j + 1):
                    copy.start()
            attend_back(proj_v.at[j % 2], j, peaks_v.at[j % 2], key_side, grad_mixed, mixed, grad_proj, inner, grad_query, actions)
            cols = slice(j * CHUNK, (j + 1) * CHUNK)
            rows_v[0:1, cols] = col_sum(grad_proj[:, :CHUNK].astype(F32))
            rows_v[1:2, cols] = col_sum(grad_proj[:, 2 * CHUNK :].astype(F32))
            if j + 1 < CHUNKS:
                put(j, dot(x0[...], grad_proj[...], TN).astype(LOW))
                chunk_done(j)
            if j == 0:
                one.wait()
            total[...] += dot(grad_proj[...], flat(weight_v[j % 2]), NT) * features
        masked = key_side[:, 7:8].astype(F32)
        rows_v[6:7, :] = col_sum(total[...] * masked)
        put(CHUNKS - 1, dot(x0[...], grad_proj[...], TN).astype(LOW))
        put(CHUNKS, rows_v[...].T)
        chunk_done(CHUNKS - 1)
        total[...] = total[...] * (1.0 - masked)
        out.start()
        return out

    shape = jax.ShapeDtypeStruct
    operands = (codes, proj, peaks, key_side, grad_mixed, mixed, x0, grad_one) + tuple(chunk_full) + (sums, bias_sums)
    in_specs = [SM, HBM, HBM, VM, VM, VM, VM, HBM, HBM, HBM, VM, VM]

    def scratch(weight_shape):
        return [
            pltpu.VMEM((2, count, D), LOW),
            pltpu.VMEM((2, heads, count, 128), LOW),
            pltpu.VMEM((2,) + weight_shape, LOW),
            pltpu.VMEM((count, D), LOW),
            pltpu.VMEM((2, count, 128), LOW),
            pltpu.VMEM((count, 128), F32),
            pltpu.VMEM((count, D), F32),
            pltpu.VMEM((128, D), F32),
            pltpu.SemaphoreType.DMA((8,)),
        ]

    if not depth:

        def plain(codes, proj, peaks, key_side, grad_mixed, mixed, x0, grad_one, head, chunks, sums, bias_sums, frames_grad, parts, small, *rest):
            def put(j, value):
                if j < CHUNKS:
                    parts[j] = value
                else:
                    small[...] = value

            out = body(codes, proj, peaks, key_side, grad_mixed, mixed, x0, grad_one, None, sums, bias_sums, frames_grad, *rest,
                       lambda j: chunks.at[j - 1] if j else head.at[:, pl.ds(0, D)], put, {}, lambda j: None)
            out.wait()

        return pl.pallas_call(
            plain,
            out_shape=(shape((count, D), F32), shape((CHUNKS, D, D), LOW), shape((D, 128), F32)),
            in_specs=in_specs,
            out_specs=(HBM, VM, VM),
            scratch_shapes=scratch((D, D)),
            compiler_params=pltpu.CompilerParams(vmem_limit_bytes=62 * MIB),
            name="back_plain",
        )(*operands)

    rows, tall = wide_part.shape[4], down_part.shape[3]
    sizes = [(rows, D)] * 11 + [(rows, (D + SMALL) // 2)] * 2
    rooms = [reduce_room(depth, *size, cross) for size, cross in zip(sizes, SUM_CROSS)]
    starts = [sum(len(room) for room in rooms[:k]) for k in range(len(rooms) + 1)]

    def fused(codes, proj, peaks, key_side, grad_mixed, mixed, x0, grad_one, head, chunks, sums, bias_sums, wide_part, down_part,
              frames_grad, qkv_grad, out_grad, in_grad, down_grad, small_grad, *rest):
        inside, (send, recv, local, wide_kept, down_kept, chunk_part, last_part), rest = rest[:9], rest[9:16], rest[16:]
        room_refs, finals = rest[: starts[-1]], rest[starts[-1] :]
        here = Place(depth)
        c = here.c
        copies = Copies(send, recv)
        plans = []

        def plan(sibling, kept):
            k = len(plans)
            plans.append(reduce_part(here, copies, sibling, kept, room_refs[starts[k] : starts[k + 1]], finals[k], sizes[k][1], SUM_CROSS[k]))

        for k in range(5):
            plan(wide_part.at[k, :, :, 1 - c], lambda zz, xx, k=k: wide_kept[k, zz, xx])
        for k in range(4):
            cut = pl.ds(k * rows, rows)
            plan(down_part.at[:, :, 1 - c, cut], lambda zz, xx, cut=cut: down_kept[zz, xx, cut, :])
        for k in range(2):
            plan(chunk_part.at[k, :, :, 1 - c], lambda zz, xx, k=k: chunk_part[k, zz, xx, c])
        for k in range(2):
            cut = pl.ds(k * (D + SMALL) // 2, (D + SMALL) // 2)
            plan(last_part.at[:, :, 1 - c, :, cut], lambda zz, xx, cut=cut: last_part[zz, xx, c, :, cut])
        keep = [
            pltpu.make_async_copy(wide_part.at[:, :, :, c], wide_kept, local.at[0]),
            pltpu.make_async_copy(down_part.at[:, :, c], down_kept, local.at[1]),
        ]

        def put(j, value):
            if j < CHUNKS - 1:
                chunk_part[j] = value.reshape(depth, 2, 2, rows, D)
            elif j < CHUNKS:
                last_part[:, :, :, :, :D] = value.reshape(depth, 2, 2, rows, D)
            else:
                last_part[:, :, :, :, D : D + 128] = value.astype(LOW).reshape(depth, 2, 2, rows, 128)
                last_part[:, :, :, :, D + 128 :] = jnp.zeros((depth, 2, 2, rows, SMALL - 128), LOW)

        here.greet()
        run(plans, [(k, 0) for k in range(9)])
        for copy in keep:
            copy.start()
        first = SUM_THEN.get(0, [])

        def begin():
            for copy in keep:
                copy.wait()
            run(plans, first)

        actions = {k: functools.partial(run, plans, todo) for k, todo in SUM_THEN.items()}
        actions[0] = begin
        out = body(codes, proj, peaks, key_side, grad_mixed, mixed, x0, grad_one, None, sums, bias_sums, frames_grad, *inside,
                   lambda j: chunks.at[j - 1] if j else head.at[:, :, :, :, pl.ds(0, D)], put, actions,
                   lambda j: run(plans, SUM_CHUNK.get(j, [])))
        run(plans, SUM_LAST)
        out_grad[...] = finals[0][...].astype(F32)
        for k in range(4):
            in_grad[:, k * D : (k + 1) * D] = finals[1 + k][...].astype(F32)
            down_grad[k * rows : (k + 1) * rows, :] = finals[5 + k][...].astype(F32)
        last = jnp.concatenate([finals[11][...], finals[12][...]], axis=1).astype(F32)
        small_grad[...] = last[:, D : D + 128]
        for j in range(CHUNKS):
            value = last if j == CHUNKS - 1 else finals[9 + j][...].astype(F32)
            for k in range(3):
                qkv_grad[:, k * D + j * CHUNK : k * D + (j + 1) * CHUNK] = value[:, k * CHUNK : (k + 1) * CHUNK]
        out.wait()
        copies.finish()

    copies = reduce_copies(depth) * len(sizes)
    return pl.pallas_call(
        fused,
        out_shape=(
            shape((count, D), F32),
            shape((rows, 3 * D), F32),
            shape((rows, D), F32),
            shape((rows, FF), F32),
            shape((tall, D), F32),
            shape((rows, 128), F32),
        ),
        in_specs=in_specs + [HBM, HBM],
        out_specs=(HBM,) + (VM,) * 5,
        scratch_shapes=scratch((depth, 2, 2, rows, D))
        + [
            pltpu.SemaphoreType.DMA((copies,)),
            pltpu.SemaphoreType.DMA((copies,)),
            pltpu.SemaphoreType.DMA((2,)),
            pltpu.VMEM((5, depth, 2, rows, D), LOW),
            pltpu.VMEM((depth, 2, tall, D), LOW),
            pltpu.VMEM((2, depth, 2, 2, rows, D), LOW),
            pltpu.VMEM((depth, 2, 2, rows, D + SMALL), LOW),
        ]
        + [ref for room in rooms for ref in room]
        + [pltpu.VMEM(size, LOW) for size in sizes],
        compiler_params=pltpu.CompilerParams(collective_id=1, has_side_effects=True, vmem_limit_bytes=62 * MIB),
        name="back",
    )(*operands, wide_part, down_part)


def on_device(dp_size, frames, lengths, mask_starts, width_code, head_code, ffn_code, qkv_weight, out_weight, ffn_in_weight,
              ffn_out_weight, ffn_bias, norm_gains, shifts, cotangent):
    rows, tall = qkv_weight.shape[0], ffn_out_weight.shape[0]
    groups = D // rows
    fused = rows % 16 == 0 and groups % 4 == 0 and dp_size % 2 == 0
    depth = groups // 4 if fused else 0
    codes = jnp.concatenate([width_code, head_code, ffn_code])
    starts = mask_starts.reshape(frames.shape[0] // 128, 128)
    if fused:
        masters = (qkv_weight, out_weight, ffn_in_weight, ffn_out_weight, ffn_bias, norm_gains, shifts)
        proj, x0, mixed, peaks, key_side, small, head, chunks, wide, down = front(depth, codes, lengths, starts, frames, masters)
    else:
        tail = jnp.zeros((rows, SMALL - 13), F32)
        cols = [jnp.concatenate(chunk_cols(qkv_weight, j), axis=1) for j in range(CHUNKS)]
        head = jnp.concatenate([cols[0], shifts, norm_gains, ffn_bias.reshape(4, rows).T, tail], axis=1).astype(LOW)
        chunks = jnp.stack(cols[1:]).astype(LOW)
        wide = jnp.stack([out_weight] + [ffn_in_weight[:, k * D : (k + 1) * D] for k in range(4)]).astype(LOW)
        head = lax.all_gather(head, "group", axis=0, tiled=True)
        chunks = lax.all_gather(chunks, "group", axis=1, tiled=True)
        wide = lax.all_gather(wide, "group", axis=1, tiled=True)
        down = lax.all_gather(ffn_out_weight.astype(LOW), "group", axis=0, tiled=True)
        proj, x0, mixed, peaks, key_side, small = front(0, codes, lengths, starts, frames, (head, chunks))
    bias = small[9:13].reshape(4, groups, rows).transpose(1, 0, 2).reshape(4, D)
    layer_out, grad_mixed, grad_one, wide_part, down_part, sums, bias_sums = middle(
        codes, mixed, x0, cotangent, key_side, wide.reshape(5, D, D), down.reshape(4, D, D), small, bias
    )
    bias_sums = bias_sums.reshape(groups, 4, rows).transpose(1, 0, 2).reshape(4, D)
    shared = (codes, proj, peaks, key_side, grad_mixed, mixed, x0, grad_one, (head, chunks), sums, bias_sums)
    if fused:
        wide_part = wide_part.reshape(5, depth, 2, 2, rows, D)
        down_part = down_part.reshape(depth, 2, 2, tall, D)
        frames_grad, *owned = back(depth, *shared, wide_part, down_part)
        if dp_size > 2:
            owned = [0.5 * lax.psum(part.astype(LOW), "dp").astype(F32) for part in owned]
        qkv_grad, out_grad, ffn_in_grad, ffn_out_grad, small_grad = owned
    else:
        frames_grad, chunk_parts, small_part = back(0, *shared, None, None)
        parts = [chunk_parts[k] for k in range(CHUNKS)] + [small_part, down_part.reshape(FF, D)] + [wide_part[k] for k in range(5)]
        owned = [lax.psum_scatter(part.astype(F32), "group", scatter_dimension=0, tiled=True) for part in parts]
        owned = [lax.psum(part.astype(LOW), "dp").astype(F32) for part in owned]
        qkv_grad = jnp.concatenate([owned[j][:, k * CHUNK : (k + 1) * CHUNK] for k in range(3) for j in range(CHUNKS)], axis=1)
        small_grad, ffn_out_grad, out_grad, ffn_in_grad = owned[3], owned[4], owned[5], jnp.concatenate(owned[6:], axis=1)
    ffn_bias_grad = small_grad[:, 9:13].T.reshape(tall, 1)
    return (layer_out, frames_grad, qkv_grad, out_grad, ffn_in_grad, ffn_out_grad, ffn_bias_grad, small_grad[:, 7:9], small_grad[:, :7])


def solution(mesh):
    by_all, by_group = P(("group", "dp"), None), P("group", None)
    placed = (by_all, by_all, P(("group", "dp")), P("group"), P("group"), P("group")) + (by_group,) * 7 + (by_all,)
    return jax.shard_map(
        functools.partial(on_device, mesh.shape["dp"]),
        mesh=mesh,
        in_specs=placed,
        out_specs=(by_all, by_all) + (by_group,) * 7,
        check_vma=False,
    )
```

```python
import functools

import jax
import jax.numpy as jnp
from jax import lax
from jax.experimental import pallas as pl
from jax.experimental.pallas import tpu as pltpu
from jax.sharding import PartitionSpec as P

D = 768
HEADS = 12
FF = 3072
SPAN = 10
CHUNKS = 3
CHUNK = D // CHUNKS
CHUNK_PAIRS = HEADS // (2 * CHUNKS)
SMALL = 256
BLOCK = 512

norm_eps = 1e-05
far_score = -float(2**30)
root_half = 0.7071067811865476
inv_root_tau = 0.3989422804014327

F32, LOW = jnp.float32, jnp.bfloat16
NN = (((1,), (0,)), ((), ()))
NT = (((1,), (1,)), ((), ()))
TN = (((0,), (0,)), ((), ()))
MESH = pl.DeviceIdType.MESH
MIB = 2**20


def dot(a, b, dims=NN):
    return lax.dot_general(a, b, dims, preferred_element_type=F32)


def lane_row(n):
    return lax.broadcasted_iota(jnp.int32, (1, n), 1)


def row_sum(v):
    return jnp.sum(v, axis=1, keepdims=True)


def col_sum(v):
    return jnp.sum(v, axis=0, keepdims=True)


def subnet(codes):
    width = (D // 6) * (4 + codes[0])
    return width, (HEADS - HEADS // 3 + codes[1]) * (D // HEADS), (width * (6 + codes[2])) // 2


def bias_places(groups):
    tall = FF // groups
    for group in range(groups):
        for k in range(0, tall, 128):
            unit = group * tall + k
            yield group * (D // groups) + k // 128, min(128, tall - k), unit // D, unit % D


class Place:
    def __init__(self, depth):
        group, dp = lax.axis_index("group"), lax.axis_index("dp")
        self.depth = depth
        self.z, self.x, self.c, self.y = group // 4, (group // 2) % 2, group % 2, dp % 2
        self.dp = dp
        self.core_dev = (group + 1 - 2 * self.c, dp)
        self.x_dev = (group + 2 - 4 * self.x, dp)
        self.y_dev = (group, dp + 1 - 2 * self.y)

    def z_at(self, step):
        return lax.rem(self.z + step, self.depth)

    def z_from(self, step):
        return lax.rem(self.z - step + self.depth, self.depth)

    def z_dev(self, step):
        return ((self.z_at(step) * 2 + self.x) * 2 + self.c, self.dp)

    def greet(self):
        barrier = pltpu.get_barrier_semaphore()
        devs = [self.core_dev, self.x_dev, self.y_dev] + [self.z_dev(s) for s in range(1, self.depth)]
        for dev in devs:
            pl.semaphore_signal(barrier, inc=1, device_id=dev, device_id_type=MESH)
        pl.semaphore_wait(barrier, len(devs))


class Copies:
    def __init__(self, send_sems, recv_sems):
        self.send_sems, self.recv_sems, self.made = send_sems, recv_sems, []

    def to(self, src, dst, dev):
        spot = len(self.made)
        copy = pltpu.make_async_remote_copy(
            src_ref=src,
            dst_ref=dst,
            send_sem=self.send_sems.at[spot],
            recv_sem=self.recv_sems.at[spot],
            device_id=dev,
            device_id_type=MESH,
        )
        self.made.append(copy)
        return copy

    def finish(self):
        for copy in self.made:
            copy.wait_send()


def halves(width, y):
    half = width // 2
    mine = pl.ds(pl.multiple_of(y * half, 128), half)
    other = pl.ds(pl.multiple_of((1 - y) * half, 128), half)
    return mine, other


def gather_cross(here, copies, own, at, width):
    z, x, c = here.z, here.x, here.c
    mine, other = halves(width, here.y)
    full = slice(None)
    steps = range(1, here.depth)

    def same(zz, xx, cols, dev):
        return copies.to(at(zz, xx, c, cols), at(zz, xx, c, cols), dev)

    first = copies.to(own(mine), at(z, x, c, mine), here.x_dev)
    own_core = copies.to(own(full), at(z, x, c, full), here.core_dev)
    own_z = [copies.to(own(mine), at(z, x, c, mine), here.z_dev(s)) for s in steps]
    side_z = [same(z, 1 - x, mine, here.z_dev(s)) for s in steps]
    spots = [(z, 1 - x)] + [(here.z_from(s), x) for s in steps] + [(here.z_from(s), 1 - x) for s in steps]
    y_hops = [same(zz, xx, mine, here.y_dev) for zz, xx in spots]
    core_mine = [same(zz, xx, mine, here.core_dev) for zz, xx in spots]
    core_other = [same(zz, xx, other, here.core_dev) for zz, xx in spots]
    n = len(own_z)

    def stage0():
        first.start()
        for copy in own_z:
            copy.start()
        own_core.start()

    def stage1():
        first.wait_recv()
        for copy in side_z:
            copy.start()
        y_hops[0].start()
        core_mine[0].start()

    def stage2():
        for k in range(n):
            own_z[k].wait_recv()
            y_hops[1 + k].start()
            core_mine[1 + k].start()

    def stage3():
        for k in range(n):
            side_z[k].wait_recv()
            y_hops[1 + n + k].start()
            core_mine[1 + n + k].start()

    def stage4():
        for k in range(1 + 2 * n):
            y_hops[k].wait_recv()
            core_other[k].start()

    def stage5():
        own_core.wait_recv()
        for copy in core_mine + core_other:
            copy.wait_recv()

    return [stage0, stage1, stage2, stage3, stage4, stage5]


def gather_line(here, copies, own, at, width):
    z, x, c = here.z, here.x, here.c
    mine, other = halves(width, here.y)
    full = slice(None)
    steps = range(1, here.depth)

    def same(zz, xx, cols, dev):
        return copies.to(at(zz, xx, c, cols), at(zz, xx, c, cols), dev)

    own_z = [copies.to(own(mine), at(z, x, c, mine), here.z_dev(s)) for s in steps]
    own_x = copies.to(own(full), at(z, x, c, full), here.x_dev)
    own_core = copies.to(own(full), at(z, x, c, full), here.core_dev)
    froms = [here.z_from(s) for s in steps]
    y_hops = [same(zz, x, mine, here.y_dev) for zz in froms]
    x_mine = [same(zz, x, mine, here.x_dev) for zz in froms]
    x_other = [same(zz, x, other, here.x_dev) for zz in froms]
    core_side = same(z, 1 - x, full, here.core_dev)
    core_mine = [same(zz, x, mine, here.core_dev) for zz in froms]
    core_other = [same(zz, x, other, here.core_dev) for zz in froms]
    core_x_mine = [same(zz, 1 - x, mine, here.core_dev) for zz in froms]
    core_x_other = [same(zz, 1 - x, other, here.core_dev) for zz in froms]
    n = len(own_z)

    def stage0():
        for copy in own_z:
            copy.start()
        own_x.start()
        own_core.start()

    def stage1():
        for k in range(n):
            own_z[k].wait_recv()
            y_hops[k].start()
            x_mine[k].start()
            core_mine[k].start()

    def stage2():
        own_x.wait_recv()
        core_side.start()

    def stage3():
        for k in range(n):
            y_hops[k].wait_recv()
            x_other[k].start()
            core_other[k].start()

    def stage4():
        for k in range(n):
            x_mine[k].wait_recv()
            core_x_mine[k].start()
        for k in range(n):
            x_other[k].wait_recv()
            core_x_other[k].start()

    def stage5():
        own_core.wait_recv()
        core_side.wait_recv()
        for copy in core_mine + core_other + core_x_mine + core_x_other:
            copy.wait_recv()

    return [stage0, stage1, stage2, stage3, stage4, stage5]


def gather_cross_copies(depth):
    return 2 + (depth - 1) * 2 + 3 * (2 * depth - 1)


def gather_line_copies(depth):
    return (depth - 1) * 8 + 3


def plus(a, b):
    return (a.astype(F32) + b.astype(F32)).astype(LOW)


def reduce_part(here, copies, sibling, kept, room, final, width, cross):
    z, x, depth = here.z, here.x, here.depth
    mine, other = halves(width, here.y)
    steps = range(1, depth)
    if cross:
        first, second, third, fourth, fifth = room
        core = copies.to(sibling, first, here.core_dev)
        to_y = copies.to(first.at[:, :, :, other], second, here.y_dev)
        to_z = [copies.to(second.at[here.z_at(s)], third.at[s - 1], here.z_dev(s)) for s in steps]
        to_x = copies.to(fourth.at[1 - x], fifth, here.x_dev)
    else:
        first, second, third, fourth = room
        core = copies.to(sibling, first, here.core_dev)
        to_x = copies.to(first.at[:, 1 - x], second, here.x_dev)
        to_y = copies.to(second.at[:, :, other], third, here.y_dev)
        to_z = [copies.to(third.at[here.z_at(s)], fourth.at[s - 1], here.z_dev(s)) for s in steps]
    back = copies.to(final.at[:, mine], final.at[:, mine], here.y_dev)

    def stage0():
        core.start()

    def stage1():
        core.wait_recv()

        @pl.loop(0, depth)
        def _(zz):
            for xx in range(2):
                first[zz, xx] = plus(kept(zz, xx), first[zz, xx])

        if cross:
            to_y.start()
        else:
            to_x.start()

    def stage2():
        if cross:
            to_y.wait_recv()

            @pl.loop(0, depth)
            def _(zz):
                for xx in range(2):
                    second[zz, xx] = plus(first[zz, xx, :, mine], second[zz, xx])

            for copy in to_z:
                copy.start()
        else:
            to_x.wait_recv()

            @pl.loop(0, depth)
            def _(zz):
                second[zz] = plus(first[zz, x], second[zz])

            to_y.start()

    def stage3():
        if cross:
            for copy in to_z:
                copy.wait_recv()

            @pl.loop(0, 2)
            def _(xx):
                total = second[z, xx].astype(F32)
                for s in steps:
                    total += third[s - 1, xx].astype(F32)
                fourth[xx] = total.astype(LOW)

            to_x.start()
        else:
            to_y.wait_recv()

            @pl.loop(0, depth)
            def _(zz):
                third[zz] = plus(second[zz, :, mine], third[zz])

            for copy in to_z:
                copy.start()

    def stage4():
        if cross:
            to_x.wait_recv()
            final[:, mine] = plus(fourth[x], fifth[...])
        else:
            for copy in to_z:
                copy.wait_recv()
            total = third[z].astype(F32)
            for s in steps:
                total += fourth[s - 1].astype(F32)
            final[:, mine] = total.astype(LOW)
        back.start()

    def stage5():
        back.wait_recv()

    return [stage0, stage1, stage2, stage3, stage4, stage5]


def reduce_room(depth, rows, width, cross):
    half = width // 2
    if cross:
        shapes = [(depth, 2, rows, width), (depth, 2, rows, half), (depth - 1, 2, rows, half), (2, rows, half), (rows, half)]
    else:
        shapes = [(depth, 2, rows, width), (depth, rows, width), (depth, rows, half), (depth - 1, rows, half)]
    return [pltpu.VMEM(shape, LOW) for shape in shapes]


def reduce_copies(depth):
    return 4 + depth - 1


def run(plans, todo):
    for plan, stage in todo:
        plans[plan][stage]()


def hook(at, actions):
    for k, action in actions.items():
        pl.when(at == k)(action)


def split3(v):
    high = v.astype(LOW).astype(F32)
    rest = v - high
    middle = rest.astype(LOW).astype(F32)
    return high, middle, rest - middle


def frame_tables(lengths, starts, frames, edge, query_side, key_side):
    lane = lane_row(128)
    place = lax.broadcasted_iota(jnp.int32, (frames, 1), 0)
    first, second = lengths[0, 0], lengths[0, 0] + lengths[0, 1]
    segment = (place >= first).astype(jnp.int32) + (place >= second).astype(jnp.int32)
    spread = jnp.broadcast_to(starts[...][:, None, :], (frames // 128, 128, 128)).reshape(frames, 128)
    start = jnp.max(jnp.where(lane == lax.rem(place, 128), spread, 0), axis=1, keepdims=True)
    edge[0:16, :] = jnp.full((16, 1), -1, jnp.int32)
    edge[pl.ds(16, frames), :] = jnp.where(start == 1, segment, -1)
    masked = segment < 0
    for offset in range(SPAN):
        masked = masked | (edge[pl.ds(16 - offset, frames), :] == segment)
    live = segment < 2
    masked = masked & live
    query_side[...] = jnp.where((lane < 3) & (lane != segment), far_score, 0.0).astype(LOW)
    ones = (lane == segment) | ((lane >= 3) & (lane < 6)) | ((lane == 6) & live) | ((lane == 7) & masked)
    key_side[...] = jnp.where(ones, 1.0, 0.0).astype(LOW)


def attend(proj, chunk, query_side, key_side, mixed, peaks, actions):
    frames = mixed.shape[0]
    blocks = frames // BLOCK
    lane = lane_row(128)

    @pl.loop(0, CHUNK_PAIRS)
    def _(part):
        pair = chunk * CHUNK_PAIRS + part
        col = pl.multiple_of(part * 128, 128)

        @pl.loop(0, blocks)
        def _(block):
            hook(pair * blocks + block, actions)
            rows = pl.ds(pl.multiple_of(block * BLOCK, BLOCK), BLOCK)
            query = proj[rows, pl.ds(col, 128)]
            keys = jnp.concatenate([proj[:, pl.ds(pl.multiple_of(CHUNK + col, 128), 128)], key_side[...]], axis=1)
            values = proj[:, pl.ds(pl.multiple_of(2 * CHUNK + col, 128), 128)]
            values = jnp.concatenate([values, jnp.ones((frames, 128), LOW)], axis=1)
            side = query_side[rows, :]
            found = []
            for h in range(2):
                own = jnp.where((lane < 64) == (h == 0), query, jnp.zeros_like(query))
                scores = dot(jnp.concatenate([own, side], axis=1), keys, NT)
                peak = jnp.max(scores, axis=1, keepdims=True)
                weights = jnp.exp(scores - peak).astype(LOW)
                sums = dot(weights, values)
                total = sums[:, 128:]
                high, middle, low = split3(-(peak + jnp.log(total)))
                table = jnp.where(lane == 3, high, jnp.where(lane == 4, middle, jnp.where(lane == 5, low, side.astype(F32))))
                peaks[2 * pair + h, rows, :] = table.astype(LOW)
                found.append(sums[:, :128] / total)
            mixed[rows, pl.ds(pl.multiple_of(pair * 128, 128), 128)] = jnp.where(lane < 64, found[0], found[1]).astype(LOW)


def attend_back(proj, chunk, peaks, key_side, grad_mixed, mixed, grad_proj, inner, grad_query, actions):
    frames = mixed.shape[0]
    blocks = frames // BLOCK
    lane = lane_row(128)

    @pl.loop(0, CHUNK_PAIRS)
    def _(part):
        pair = chunk * CHUNK_PAIRS + part
        all_col = pl.ds(pl.multiple_of(pair * 128, 128), 128)
        query_cols = pl.ds(pl.multiple_of(part * 128, 128), 128)
        key_cols = pl.ds(pl.multiple_of(CHUNK + part * 128, 128), 128)
        value_cols = pl.ds(pl.multiple_of(2 * CHUNK + part * 128, 128), 128)
        prod = grad_mixed[:, all_col].astype(F32) * mixed[:, all_col].astype(F32)
        for h in range(2):
            high, middle, low = split3(-row_sum(jnp.where((lane < 64) == (h == 0), prod, 0.0)))
            table = jnp.where(lane == 3, high, jnp.where(lane == 4, middle, jnp.where(lane == 5, low, 0.0)))
            inner[h] = table.astype(LOW)

        @pl.loop(0, blocks)
        def _(block):
            hook(pair * blocks + block, actions)
            rows = pl.ds(pl.multiple_of(block * BLOCK, BLOCK), BLOCK)
            key, value, side = proj[rows, key_cols], proj[rows, value_cols], key_side[rows, :]
            keys = jnp.concatenate([key, side], axis=1)
            values = jnp.concatenate([value, side], axis=1)
            query, grad = proj[:, query_cols], grad_mixed[:, all_col]
            grad_v = grad_k = grad_q = 0.0
            for h in range(2):
                own = (lane < 64) == (h == 0)
                query_h = jnp.where(own, query, jnp.zeros_like(query))
                grad_h = jnp.where(own, grad, jnp.zeros_like(grad))
                key_h = jnp.where(own, key, jnp.zeros_like(key))
                probs = jnp.exp(dot(keys, jnp.concatenate([query_h, peaks[2 * part + h]], axis=1), NT))
                shifted = dot(values, jnp.concatenate([grad_h, inner[h]], axis=1), NT)
                grad_s = (probs * shifted).astype(LOW)
                grad_v += dot(probs.astype(LOW), grad_h)
                grad_k += dot(grad_s, query_h)
                grad_q += dot(grad_s, key_h, TN)
            grad_proj[rows, key_cols] = grad_k.astype(LOW)
            grad_proj[rows, value_cols] = grad_v.astype(LOW)

            @pl.when(block == 0)
            def _():
                grad_query[...] = grad_q

            @pl.when(block > 0)
            def _():
                grad_query[...] += grad_q

        grad_proj[:, query_cols] = (grad_query[...] * 0.125).astype(LOW)


VM = pl.BlockSpec(memory_space=pltpu.VMEM)
SM = pl.BlockSpec(memory_space=pltpu.SMEM)
HBM = pl.BlockSpec(memory_space=pl.ANY)


def flat(value):
    return value.reshape(D, value.shape[-1])


def chunk_cols(matrix, j):
    return [matrix[:, k * D + j * CHUNK : k * D + (j + 1) * CHUNK] for k in range(3)]


GATHER_FIRST = [(5, 0), (0, 0), (1, 0), (5, 1), (0, 1), (5, 2), (0, 2), (5, 3), (0, 3), (1, 1), (2, 0), (5, 4), (0, 4), (1, 2), (3, 0), (4, 0), (5, 5), (0, 5)]
GATHER_THEN = {
    0: [(1, 3), (2, 1), (2, 2), (3, 1)],
    1: [(1, 4)],
    2: [(2, 3), (3, 2)],
    3: [(4, 1), (4, 2), (2, 4)],
    6: [(3, 3)],
    7: [(4, 3)],
    11: [(3, 4), (4, 4)],
}
GATHER_CHUNK = {1: [(1, 5)], 2: [(2, 5)]}
GATHER_LAST = [(3, 5), (4, 5)]


def front(depth, groups, codes, lengths, starts, frames, weights):
    count = frames.shape[0]

    def body(codes, lengths, starts, frames, small_full, chunks, proj, x0, mixed, peaks, key_side, small, bias, query_side, edge, early, enter, actions):
        width, heads, _ = subnet(codes)
        features = (lane_row(D) < width).astype(F32)
        frame_tables(lengths, starts, count, edge, query_side, key_side)
        early()
        table = flat(small_full[...]).astype(F32)
        small[...] = table[:, :128].T[0:16, :]
        for row, n, at, col in bias_places(groups):
            bias[at : at + 1, col : col + n] = table[row : row + 1, 128 : 128 + n]
        masked = key_side[:, 7:8].astype(F32)
        start = jnp.where(masked > 0, small[6:7, :], frames[...].astype(F32)) * features
        x0[...] = start.astype(LOW)

        @pl.loop(0, CHUNKS)
        def _(j):
            enter(j)
            cols = pl.ds(pl.multiple_of(j * CHUNK, CHUNK), CHUNK)
            active = (lane_row(CHUNK) + j * CHUNK < heads).astype(F32)
            value = dot(x0[...], flat(chunks[j]))
            for k in range(3):
                piece = value[:, k * CHUNK : (k + 1) * CHUNK]
                if k != 1:
                    piece = piece + small[k // 2 : k // 2 + 1, cols]
                piece = (piece * active).astype(LOW)
                proj[j, :, k * CHUNK : (k + 1) * CHUNK] = piece * jnp.asarray(0.125, LOW) if k == 0 else piece
            attend(proj.at[j], j, query_side, key_side, mixed, peaks, actions)

    shape = jax.ShapeDtypeStruct
    found = (
        shape((CHUNKS, count, D), LOW),
        shape((count, D), LOW),
        shape((count, D), LOW),
        shape((HEADS, count, 128), LOW),
        shape((count, 128), LOW),
        shape((16, D), F32),
        shape((4, D), F32),
    )
    scratch = [pltpu.VMEM((count, 128), LOW), pltpu.VMEM((count + 16, 1), jnp.int32)]
    params = dict(has_side_effects=True, vmem_limit_bytes=62 * MIB)
    if not depth:

        def plain(codes, lengths, starts, frames, head, chunks, *rest):
            body(codes, lengths, starts, frames, head, chunks, *rest, lambda: None, lambda j: None, {})

        return pl.pallas_call(
            plain,
            out_shape=found,
            in_specs=[SM, SM, VM, VM, VM, VM],
            out_specs=(VM,) * 7,
            scratch_shapes=scratch,
            compiler_params=pltpu.CompilerParams(vmem_limit_bytes=62 * MIB),
            name="front_plain",
        )(codes, lengths, starts, frames, *weights)

    rows, tall = weights[0].shape[0], weights[3].shape[0]

    def fused(*refs):
        codes, lengths, starts, frames = refs[:4]
        qkv_own, out_own, in_own, down_own, bias_own, gains_own, shifts_own = refs[4:11]
        proj, x0, mixed, peaks, key_side, small, bias, head, chunks, wide, down = refs[11:22]
        query_side, edge, pad, square, head_low, chunks_low, wide_low, down_low, send, recv, local = refs[22:]
        here = Place(depth)
        z, x, c = here.z, here.x, here.c
        copies = Copies(send, recv)

        def flat_plan(gather, own, full, width):
            return gather(here, copies, lambda cols: own.at[:, cols], lambda zz, xx, cc, cols: full.at[zz, xx, cc, :, cols], width)

        plans = [
            flat_plan(gather_line, chunks_low.at[0], chunks.at[0], D),
            flat_plan(gather_cross, chunks_low.at[1], chunks.at[1], D),
            flat_plan(gather_line, chunks_low.at[2], chunks.at[2], D),
            flat_plan(gather_cross, down_low, down, D),
            gather_line(here, copies, lambda cols: wide_low.at[:, :, cols], lambda zz, xx, cc, cols: wide.at[:, zz, xx, cc, :, cols], D),
            flat_plan(gather_cross, head_low, head, SMALL),
        ]
        keep = [
            pltpu.make_async_copy(head_low, head.at[z, x, c], local.at[0]),
            pltpu.make_async_copy(chunks_low, chunks.at[:, z, x, c], local.at[1]),
            pltpu.make_async_copy(wide_low, wide.at[:, z, x, c], local.at[2]),
            pltpu.make_async_copy(down_low, down.at[z, x, c], local.at[3]),
        ]
        square[...] = jnp.zeros_like(square)
        square[0:7, 0:rows] = shifts_own[...]
        square[7:9, 0:rows] = gains_own[...]
        pad[...] = jnp.zeros_like(pad)
        pad[:, :128] = square[...].T[:rows, :]
        for k in range(0, tall, 128):
            n = min(128, tall - k)
            pad[k // 128 : k // 128 + 1, 128 : 128 + n] = bias_own[:, k : k + n]
        for j in range(CHUNKS):
            chunks_low[j] = jnp.concatenate(chunk_cols(qkv_own, j), axis=1).astype(LOW)
        head_low[...] = pad[...].astype(LOW)
        wide_low[0] = out_own[...].astype(LOW)
        for k in range(4):
            wide_low[1 + k] = in_own[:, k * D : (k + 1) * D].astype(LOW)
        down_low[...] = down_own[...].astype(LOW)
        here.greet()

        def early():
            for copy in keep:
                copy.start()
            run(plans, GATHER_FIRST)
            keep[0].wait()
            keep[1].wait()

        def enter(j):
            hook(j, {k: functools.partial(run, plans, todo) for k, todo in GATHER_CHUNK.items()})

        actions = {k: functools.partial(run, plans, todo) for k, todo in GATHER_THEN.items()}
        body(codes, lengths, starts, frames, head, chunks, proj, x0, mixed, peaks, key_side, small, bias, query_side, edge, early, enter, actions)
        run(plans, GATHER_LAST)
        keep[2].wait()
        keep[3].wait()
        copies.finish()

    copies = 3 * (gather_cross_copies(depth) + gather_line_copies(depth))
    return pl.pallas_call(
        fused,
        out_shape=found
        + (
            shape((depth, 2, 2, rows, SMALL), LOW),
            shape((CHUNKS, depth, 2, 2, rows, D), LOW),
            shape((5, depth, 2, 2, rows, D), LOW),
            shape((depth, 2, 2, tall, D), LOW),
        ),
        in_specs=[SM, SM] + [VM] * 9,
        out_specs=(VM,) * 9 + (HBM, HBM),
        scratch_shapes=scratch
        + [
            pltpu.VMEM((rows, SMALL), F32),
            pltpu.VMEM((128, 128), F32),
            pltpu.VMEM((rows, SMALL), LOW),
            pltpu.VMEM((CHUNKS, rows, D), LOW),
            pltpu.VMEM((5, rows, D), LOW),
            pltpu.VMEM((tall, D), LOW),
            pltpu.SemaphoreType.DMA((copies,)),
            pltpu.SemaphoreType.DMA((copies,)),
            pltpu.SemaphoreType.DMA((4,)),
        ],
        compiler_params=pltpu.CompilerParams(collective_id=0, **params),
        name="front",
    )(codes, lengths, starts, frames, *weights)


def normal_parts(v):
    bell = jnp.exp(v * v * -0.5)
    t = 1.0 / (1.0 + (0.3275911 * root_half) * jnp.abs(v))
    tail = t * (0.127414796 + t * (-0.142248368 + t * (0.7107068705 + t * (-0.7265760135 + t * 0.5307027145)))) * bell
    return jnp.where(v < 0, tail, 1.0 - tail), bell


def middle(codes, mixed, x0, cotangent, key_side, wide, down, small, bias):
    count = mixed.shape[0]
    size = BLOCK // 2
    steps = count // size

    def kernel(codes, mixed, x0, cotangent, key_side, wide, down, small, bias, out, grad_mixed, grad_one, wide_part, down_part,
               sums, bias_sums, wide_v, down_v, mixed_all, hidden_all, act_all, pre_all, ffn_all, branch_all, slope, stage, in_sems, out_sems):
        step = pl.program_id(0)
        width, heads, units = subnet(codes)
        features = (lane_row(D) < width).astype(F32)
        active = (lane_row(D) < heads).astype(F32)
        scale = 1.0 / width.astype(F32)
        rows = pl.ds(pl.multiple_of(step * size, size), size)
        loads = [pltpu.make_async_copy(wide.at[k], wide_v.at[k], in_sems.at[k]) for k in range(5)]
        loads += [pltpu.make_async_copy(down.at[k], down_v.at[k], in_sems.at[5 + k]) for k in range(4)]

        def ready(k):
            pl.when(step == 0)(loads[k].wait)

        @pl.when(step == 0)
        def _():
            for load in loads:
                load.start()
            sums[...] = jnp.zeros_like(sums)
            bias_sums[...] = jnp.zeros_like(bias_sums)

        def param(k):
            return small[k : k + 1, :]

        mixed_all[rows, :] = mixed[...]
        ready(0)
        resid = x0[...].astype(F32) + (dot(mixed[...], wide_v[0]) + param(2)) * features
        centered = (resid - row_sum(resid) * scale) * features
        inv_one = lax.rsqrt(row_sum(centered * centered) * scale + norm_eps)
        normed_one = centered * inv_one
        hidden = (normed_one * param(7) + param(4)) * features
        hidden_low = hidden.astype(LOW)
        hidden_all[rows, :] = hidden_low
        branch = 0.0
        for j in range(4):
            ready(1 + j)
            unit_mask = (lane_row(D) + j * D < units).astype(F32)
            pre = (dot(hidden_low, wide_v[1 + j]) + bias[j : j + 1, :]) * unit_mask
            share, bell = normal_parts(pre)
            act = (pre * share).astype(LOW)
            act_all[j, rows, :] = act
            slope[j] = (share + pre * bell * inv_root_tau) * unit_mask
            ready(5 + j)
            branch += dot(act, down_v[j])
        resid = hidden + (branch + param(3)) * features
        centered = (resid - row_sum(resid) * scale) * features
        inv_two = lax.rsqrt(row_sum(centered * centered) * scale + norm_eps)
        normed_two = centered * inv_two
        live = key_side[:, 6:7].astype(F32)
        out[...] = ((normed_two * param(8) + param(5)) * features * live).astype(LOW)
        grad_out = cotangent[...].astype(F32) * live
        grad_n = grad_out * (param(8) * features)
        grad_two = inv_two * features * (grad_n - row_sum(grad_n) * scale - normed_two * (row_sum(grad_n * normed_two) * scale))
        grad_ffn = grad_two.astype(LOW)
        ffn_all[rows, :] = grad_ffn
        back = 0.0
        for j in range(4):
            grad_pre = (dot(grad_ffn, down_v[j], NT) * slope[j]).astype(LOW)
            pre_all[j, rows, :] = grad_pre
            bias_sums[j : j + 1, :] += col_sum(grad_pre.astype(F32))
            back += dot(grad_pre, wide_v[1 + j], NT)
        grad_hidden = grad_two + back * features
        grad_n = grad_hidden * (param(7) * features)
        grad_res = inv_one * features * (grad_n - row_sum(grad_n) * scale - normed_one * (row_sum(grad_n * normed_one) * scale))
        grad_one[...] = grad_res
        grad_branch = grad_res.astype(LOW)
        branch_all[rows, :] = grad_branch
        grad_mixed[...] = (dot(grad_branch, wide_v[0], NT) * active).astype(LOW)
        sums[0:1, :] += col_sum(grad_branch.astype(F32))
        sums[1:2, :] += col_sum(grad_ffn.astype(F32))
        sums[2:3, :] += col_sum(grad_hidden) * features
        sums[3:4, :] += col_sum(grad_out) * features
        sums[4:5, :] += col_sum(grad_hidden * normed_one)
        sums[5:6, :] += col_sum(grad_out * normed_two)

        @pl.when(step == steps - 1)
        def _():
            def store(slot, value, place):
                stage[slot] = value.astype(LOW)
                pltpu.make_async_copy(stage.at[slot], place, out_sems.at[slot]).start()

            def stored(slot):
                pltpu.make_async_copy(stage.at[slot], down_part.at[0], out_sems.at[slot]).wait()

            @pl.loop(0, 4)
            def _(k):
                @pl.when(k > 0)
                def _():
                    stored(0)
                    stored(1)

                store(0, dot(act_all[k], ffn_all[...], TN), down_part.at[k])
                store(1, dot(hidden_all[...], pre_all[k], TN), wide_part.at[k + 1])

            stored(0)
            store(0, dot(mixed_all[...], branch_all[...], TN), wide_part.at[0])
            stored(1)
            stored(0)

    block = pl.BlockSpec((size, D), lambda i: (i, 0))
    shape = jax.ShapeDtypeStruct
    return pl.pallas_call(
        kernel,
        grid=(steps,),
        in_specs=[SM, block, block, block, pl.BlockSpec((size, 128), lambda i: (i, 0)), HBM, HBM]
        + [pl.BlockSpec((16, D), lambda i: (0, 0)), pl.BlockSpec((4, D), lambda i: (0, 0))],
        out_specs=(block, block, block, HBM, HBM, pl.BlockSpec((8, D), lambda i: (0, 0)), pl.BlockSpec((4, D), lambda i: (0, 0))),
        out_shape=(
            shape((count, D), LOW),
            shape((count, D), LOW),
            shape((count, D), F32),
            shape((5, D, D), LOW),
            shape((4, D, D), LOW),
            shape((8, D), F32),
            shape((4, D), F32),
        ),
        scratch_shapes=[
            pltpu.VMEM((5, D, D), LOW),
            pltpu.VMEM((4, D, D), LOW),
            pltpu.VMEM((count, D), LOW),
            pltpu.VMEM((count, D), LOW),
            pltpu.VMEM((4, count, D), LOW),
            pltpu.VMEM((4, count, D), LOW),
            pltpu.VMEM((count, D), LOW),
            pltpu.VMEM((count, D), LOW),
            pltpu.VMEM((4, size, D), F32),
            pltpu.VMEM((2, D, D), LOW),
            pltpu.SemaphoreType.DMA((9,)),
            pltpu.SemaphoreType.DMA((2,)),
        ],
        compiler_params=pltpu.CompilerParams(vmem_limit_bytes=62 * MIB),
        name="middle",
    )(codes, mixed, x0, cotangent, key_side, wide, down, small, bias)


SUM_CROSS = [False, True, False, False, False, False, False, False, False, False, True, False, True, True]
SUM_THEN = {
    2: [(0, 1), (1, 1), (2, 1)],
    3: [(3, 1), (4, 1), (5, 1)],
    5: [(2, 2), (9, 1), (0, 3)],
    6: [(3, 2), (1, 3)],
    7: [(2, 3), (0, 4), (4, 2)],
    9: [(10, 1), (6, 2), (3, 4), (5, 3), (2, 5)],
    10: [(4, 4), (7, 2)],
    11: [(5, 4), (10, 2), (8, 2)],
}
SUM_CHUNK = {
    0: [(9, 0), (6, 1), (7, 1), (8, 1), (0, 2), (1, 2)],
    1: [(10, 0), (3, 3), (0, 5), (5, 2), (2, 4), (4, 3)],
    2: [(11, 0), (12, 0)],
}
SUM_SMALL = [(13, 0)]
SUM_LAST = [
    (6, 3), (3, 5), (4, 5), (9, 2), (1, 4), (7, 3), (5, 5), (10, 3), (8, 3), (11, 1),
    (12, 1), (13, 1), (10, 4), (6, 4), (9, 3), (1, 5), (7, 4), (11, 2), (12, 2), (13, 2),
    (8, 4), (10, 5), (6, 5), (7, 5), (9, 4), (11, 3), (8, 5), (9, 5), (12, 3), (13, 3),
    (11, 4), (12, 4), (13, 4), (11, 5), (12, 5), (13, 5),
]


def back(depth, groups, codes, proj, peaks, key_side, grad_mixed, mixed, x0, grad_one, chunks, sums, bias_sums, wide_part, down_part):
    count = mixed.shape[0]
    heads = HEADS // CHUNKS

    def body(codes, proj, peaks, key_side, grad_mixed, mixed, x0, grad_one, chunks, sums, bias_sums, frames_grad,
             proj_v, peaks_v, weight_v, grad_proj, inner, grad_query, total, rows_v, small_v, loads, put, actions, chunk_done):
        width, _, _ = subnet(codes)
        features = (lane_row(D) < width).astype(F32)
        one = pltpu.make_async_copy(grad_one, total, loads.at[6])
        out = pltpu.make_async_copy(total, frames_grad, loads.at[7])

        def fetch(j):
            slot = lax.rem(j, 2)
            return [
                pltpu.make_async_copy(proj.at[j], proj_v.at[slot], loads.at[slot]),
                pltpu.make_async_copy(peaks.at[pl.ds(j * heads, heads)], peaks_v.at[slot], loads.at[2 + slot]),
                pltpu.make_async_copy(chunks.at[j], weight_v.at[slot], loads.at[4 + slot]),
            ]

        for copy in fetch(0):
            copy.start()
        one.start()
        rows_v[...] = jnp.zeros_like(rows_v)
        rows_v[2:6, :] = sums[0:4, :]
        rows_v[7:9, :] = sums[4:6, :]
        small_v[...] = jnp.zeros_like(small_v)
        for row, n, at, col in bias_places(groups):
            small_v[row : row + 1, 128 : 128 + n] = bias_sums[at : at + 1, col : col + n]

        @pl.loop(0, CHUNKS)
        def _(j):
            slot = lax.rem(j, 2)
            for copy in fetch(j):
                copy.wait()

            @pl.when(j + 1 < CHUNKS)
            def _():
                for copy in fetch(j + 1):
                    copy.start()

            attend_back(proj_v.at[slot], j, peaks_v.at[slot], key_side, grad_mixed, mixed, grad_proj, inner, grad_query, actions)
            cols = pl.ds(pl.multiple_of(j * CHUNK, CHUNK), CHUNK)
            rows_v[0:1, cols] = col_sum(grad_proj[:, :CHUNK].astype(F32))
            rows_v[1:2, cols] = col_sum(grad_proj[:, 2 * CHUNK :].astype(F32))
            put(j, dot(x0[...], grad_proj[...], TN).astype(LOW))
            chunk_done(j)

            @pl.when(j == 0)
            def _():
                one.wait()

            total[...] += dot(grad_proj[...], flat(weight_v[slot]), NT) * features

        out.start()
        rows_v[6:7, :] = col_sum(total[...] * key_side[:, 7:8].astype(F32))
        small_v[:, :128] = rows_v[...].T
        put(None, small_v[...])
        chunk_done(None)
        return out

    shape = jax.ShapeDtypeStruct
    operands = (codes, proj, peaks, key_side, grad_mixed, mixed, x0, grad_one, chunks, sums, bias_sums)
    in_specs = [SM, HBM, HBM, VM, VM, VM, VM, HBM, HBM, VM, VM]

    def scratch(weight_shape):
        return [
            pltpu.VMEM((2, count, D), LOW),
            pltpu.VMEM((2, heads, count, 128), LOW),
            pltpu.VMEM((2,) + weight_shape, LOW),
            pltpu.VMEM((count, D), LOW),
            pltpu.VMEM((2, count, 128), LOW),
            pltpu.VMEM((count, 128), F32),
            pltpu.VMEM((count, D), F32),
            pltpu.VMEM((128, D), F32),
            pltpu.VMEM((D, SMALL), F32),
            pltpu.SemaphoreType.DMA((8,)),
        ]

    if not depth:

        def plain(codes, proj, peaks, key_side, grad_mixed, mixed, x0, grad_one, chunks, sums, bias_sums, frames_grad, parts, small, *rest):
            def put(j, value):
                if j is None:
                    small[...] = value
                else:
                    parts[j] = value

            out = body(codes, proj, peaks, key_side, grad_mixed, mixed, x0, grad_one, chunks, sums, bias_sums, frames_grad, *rest,
                       put, {}, lambda j: None)
            out.wait()

        return pl.pallas_call(
            plain,
            out_shape=(shape((count, D), F32), shape((CHUNKS, D, D), LOW), shape((D, SMALL), F32)),
            in_specs=in_specs,
            out_specs=(HBM, VM, VM),
            scratch_shapes=scratch((D, D)),
            compiler_params=pltpu.CompilerParams(vmem_limit_bytes=62 * MIB),
            name="back_plain",
        )(*operands)

    rows, tall = wide_part.shape[4], down_part.shape[3]
    sizes = [(rows, D)] * 11 + [(rows, D - SMALL), (rows, SMALL), (rows, SMALL)]
    rooms = [reduce_room(depth, *size, cross) for size, cross in zip(sizes, SUM_CROSS)]
    starts = [sum(len(room) for room in rooms[:k]) for k in range(len(rooms) + 1)]

    def fused(codes, proj, peaks, key_side, grad_mixed, mixed, x0, grad_one, chunks, sums, bias_sums, wide_part, down_part,
              frames_grad, chunk_own, wide_own, down_own, small_own, *rest):
        inside, (send, recv, local, wide_kept, down_kept, chunk_part, small_part), rest = rest[:10], rest[10:17], rest[17:]
        room_refs, finals = rest[: starts[-1]], rest[starts[-1] :]
        here = Place(depth)
        c = here.c
        copies = Copies(send, recv)
        plans = []

        def plan(sibling, kept):
            k = len(plans)
            plans.append(reduce_part(here, copies, sibling, kept, room_refs[starts[k] : starts[k + 1]], finals[k], sizes[k][1], SUM_CROSS[k]))

        for k in range(5):
            plan(wide_part.at[k, :, :, 1 - c], lambda zz, xx, k=k: wide_kept[k, zz, xx])
        for k in range(4):
            cut = pl.ds(k * rows, rows)
            plan(down_part.at[:, :, 1 - c, cut], lambda zz, xx, cut=cut: down_kept[zz, xx, cut, :])
        for k in range(2):
            plan(chunk_part.at[k, :, :, 1 - c], lambda zz, xx, k=k: chunk_part[k, zz, xx, c])
        for cut in (pl.ds(0, D - SMALL), pl.ds(D - SMALL, SMALL)):
            plan(chunk_part.at[2, :, :, 1 - c, :, cut], lambda zz, xx, cut=cut: chunk_part[2, zz, xx, c, :, cut])
        plan(small_part.at[:, :, 1 - c], lambda zz, xx: small_part[zz, xx, c])
        keep = [
            pltpu.make_async_copy(wide_part.at[:, :, :, c], wide_kept, local.at[0]),
            pltpu.make_async_copy(down_part.at[:, :, c], down_kept, local.at[1]),
        ]

        def put(j, value):
            if j is None:
                small_part[...] = value.astype(LOW).reshape(depth, 2, 2, rows, SMALL)
            else:
                chunk_part[j] = value.reshape(depth, 2, 2, rows, D)

        here.greet()
        run(plans, [(k, 0) for k in range(9)])
        for copy in keep:
            copy.start()
        first = SUM_THEN.get(0, [])

        def begin():
            for copy in keep:
                copy.wait()
            run(plans, first)

        actions = {k: functools.partial(run, plans, todo) for k, todo in SUM_THEN.items()}
        actions[0] = begin
        def chunk_done(j):
            if j is None:
                run(plans, SUM_SMALL)
            else:
                hook(j, {k: functools.partial(run, plans, todo) for k, todo in SUM_CHUNK.items()})

        out = body(codes, proj, peaks, key_side, grad_mixed, mixed, x0, grad_one, chunks, sums, bias_sums, frames_grad, *inside,
                   put, actions, chunk_done)
        run(plans, SUM_LAST)
        for k in range(5):
            wide_own[k] = finals[k][...]
        for k in range(4):
            down_own[k * rows : (k + 1) * rows, :] = finals[5 + k][...]
        for k in range(2):
            chunk_own[k] = finals[9 + k][...]
        chunk_own[2, :, : D - SMALL] = finals[11][...]
        chunk_own[2, :, D - SMALL :] = finals[12][...]
        small_own[...] = finals[13][...]
        out.wait()
        copies.finish()

    copies = reduce_copies(depth) * len(sizes)
    return pl.pallas_call(
        fused,
        out_shape=(
            shape((count, D), F32),
            shape((CHUNKS, rows, D), LOW),
            shape((5, rows, D), LOW),
            shape((tall, D), LOW),
            shape((rows, SMALL), LOW),
        ),
        in_specs=in_specs + [HBM, HBM],
        out_specs=(HBM,) + (VM,) * 4,
        scratch_shapes=scratch((depth, 2, 2, rows, D))
        + [
            pltpu.SemaphoreType.DMA((copies,)),
            pltpu.SemaphoreType.DMA((copies,)),
            pltpu.SemaphoreType.DMA((2,)),
            pltpu.VMEM((5, depth, 2, rows, D), LOW),
            pltpu.VMEM((depth, 2, tall, D), LOW),
            pltpu.VMEM((CHUNKS, depth, 2, 2, rows, D), LOW),
            pltpu.VMEM((depth, 2, 2, rows, SMALL), LOW),
        ]
        + [ref for room in rooms for ref in room]
        + [pltpu.VMEM(size, LOW) for size in sizes],
        compiler_params=pltpu.CompilerParams(collective_id=1, has_side_effects=True, vmem_limit_bytes=62 * MIB),
        name="back",
    )(*operands, wide_part, down_part)


def finish(total, key_side, chunk_own, wide_own, down_own, small_own):
    count, (_, rows, _), tall = total.shape[0], chunk_own.shape, down_own.shape[0]
    size = count // 4

    def kernel(total, key_side, chunk_own, wide_own, down_own, small_own,
               frames_grad, qkv_grad, out_grad, in_grad, down_grad, bias_grad, gains_grad, shifts_grad, square):
        frames_grad[...] = total[...] * (1.0 - key_side[:, 7:8].astype(F32))

        @pl.when(pl.program_id(0) == 0)
        def _():
            for j in range(CHUNKS):
                for k in range(3):
                    piece = chunk_own[j, :, k * CHUNK : (k + 1) * CHUNK]
                    qkv_grad[:, k * D + j * CHUNK : k * D + (j + 1) * CHUNK] = piece.astype(F32)
            out_grad[...] = wide_own[0].astype(F32)
            for k in range(4):
                in_grad[:, k * D : (k + 1) * D] = wide_own[1 + k].astype(F32)
            down_grad[...] = down_own[...].astype(F32)
            table = small_own[...].astype(F32)
            square[...] = jnp.zeros_like(square)
            square[0:rows, :] = table[:, :128]
            turned = square[...].T
            shifts_grad[...] = turned[0:7, 0:rows]
            gains_grad[...] = turned[7:9, 0:rows]
            for k in range(0, tall, 128):
                n = min(128, tall - k)
                bias_grad[:, k : k + n] = table[k // 128 : k // 128 + 1, 128 : 128 + n]

    def whole(*dims):
        return pl.BlockSpec(dims, lambda i: (0,) * len(dims))

    block = pl.BlockSpec((size, D), lambda i: (i, 0))
    outs = [(rows, 3 * D), (rows, D), (rows, FF), (tall, D), (1, tall), (2, rows), (7, rows)]
    return pl.pallas_call(
        kernel,
        grid=(4,),
        in_specs=[block, pl.BlockSpec((size, 128), lambda i: (i, 0))]
        + [whole(*part.shape) for part in (chunk_own, wide_own, down_own, small_own)],
        out_specs=(block,) + tuple(whole(*dims) for dims in outs),
        out_shape=(jax.ShapeDtypeStruct((count, D), F32),) + tuple(jax.ShapeDtypeStruct(dims, F32) for dims in outs),
        scratch_shapes=[pltpu.VMEM((128, 128), F32)],
        name="finish",
    )(total, key_side, chunk_own, wide_own, down_own, small_own)


def on_device(dp_size, frames, lengths, mask_starts, width_code, head_code, ffn_code, qkv_weight, out_weight, ffn_in_weight,
              ffn_out_weight, ffn_bias, norm_gains, shifts, cotangent):
    rows, tall = qkv_weight.shape[0], ffn_out_weight.shape[0]
    groups = D // rows
    fused = rows % 16 == 0 and groups % 4 == 0 and dp_size % 2 == 0
    depth = groups // 4 if fused else 0
    codes = jnp.concatenate([width_code, head_code, ffn_code])
    starts = mask_starts.reshape(frames.shape[0] // 128, 128)
    if fused:
        masters = (qkv_weight, out_weight, ffn_in_weight, ffn_out_weight, ffn_bias.reshape(1, tall), norm_gains.T, shifts.T)
        found = front(depth, groups, codes, lengths, starts, frames, masters)
        proj, x0, mixed, peaks, key_side, small, bias, head, chunks, wide, down = found
    else:
        spread = jnp.zeros((rows, 128), F32).at[: -(-tall // 128), :].set(jnp.pad(ffn_bias[:, 0], (0, -tall % 128)).reshape(-1, 128))
        head = jnp.concatenate([shifts, norm_gains, jnp.zeros((rows, 119), F32), spread], axis=1).astype(LOW)
        chunks = jnp.stack([jnp.concatenate(chunk_cols(qkv_weight, j), axis=1) for j in range(CHUNKS)]).astype(LOW)
        wide = jnp.stack([out_weight] + [ffn_in_weight[:, k * D : (k + 1) * D] for k in range(4)]).astype(LOW)
        head = lax.all_gather(head, "group", axis=0, tiled=True)
        chunks = lax.all_gather(chunks, "group", axis=1, tiled=True)
        wide = lax.all_gather(wide, "group", axis=1, tiled=True)
        down = lax.all_gather(ffn_out_weight.astype(LOW), "group", axis=0, tiled=True)
        proj, x0, mixed, peaks, key_side, small, bias = front(0, groups, codes, lengths, starts, frames, (head, chunks))
    layer_out, grad_mixed, grad_one, wide_part, down_part, sums, bias_sums = middle(
        codes, mixed, x0, cotangent, key_side, wide.reshape(5, D, D), down.reshape(4, D, D), small, bias
    )
    shared = (codes, proj, peaks, key_side, grad_mixed, mixed, x0, grad_one, chunks, sums, bias_sums)
    if fused:
        wide_part = wide_part.reshape(5, depth, 2, 2, rows, D)
        down_part = down_part.reshape(depth, 2, 2, tall, D)
        total, *owned = back(depth, groups, *shared, wide_part, down_part)
        if dp_size > 2:
            owned = [0.5 * lax.psum(part, "dp") for part in owned]
    else:
        total, chunk_parts, small_part = back(0, groups, *shared, None, None)
        owned = [
            lax.psum_scatter(chunk_parts.astype(F32), "group", scatter_dimension=1, tiled=True),
            lax.psum_scatter(wide_part.astype(F32), "group", scatter_dimension=1, tiled=True),
            lax.psum_scatter(down_part.reshape(FF, D).astype(F32), "group", scatter_dimension=0, tiled=True),
            lax.psum_scatter(small_part, "group", scatter_dimension=0, tiled=True),
        ]
        owned = [lax.psum(part.astype(LOW), "dp") for part in owned]
    frames_grad, qkv_grad, out_grad, ffn_in_grad, ffn_out_grad, bias_row, gains_rows, shifts_rows = finish(total, key_side, *owned)
    return (layer_out, frames_grad, qkv_grad, out_grad, ffn_in_grad, ffn_out_grad, bias_row.reshape(tall, 1), gains_rows.T, shifts_rows.T)


def solution(mesh):
    by_all, by_group = P(("group", "dp"), None), P("group", None)
    placed = (by_all, by_all, P(("group", "dp")), P("group"), P("group"), P("group")) + (by_group,) * 7 + (by_all,)
    return jax.shard_map(
        functools.partial(on_device, mesh.shape["dp"]),
        mesh=mesh,
        in_specs=placed,
        out_specs=(by_all, by_all) + (by_group,) * 7,
        check_vma=False,
    )
```

```python
import functools

import jax
import jax.numpy as jnp
from jax import lax
from jax.experimental import pallas as pl
from jax.experimental.pallas import tpu as pltpu
from jax.sharding import PartitionSpec as P

D = 768
HEADS = 12
FF = 3072
SPAN = 10
CHUNKS = 3
CHUNK = D // CHUNKS
CHUNK_PAIRS = HEADS // (2 * CHUNKS)
SMALL = 256
BLOCK = 512

norm_eps = 1e-05
far_score = -float(2**30)
root_half = 0.7071067811865476
inv_root_tau = 0.3989422804014327

F32, LOW = jnp.float32, jnp.bfloat16
NN = (((1,), (0,)), ((), ()))
NT = (((1,), (1,)), ((), ()))
TN = (((0,), (0,)), ((), ()))
MESH = pl.DeviceIdType.MESH
MIB = 2**20


def dot(a, b, dims=NN):
    return lax.dot_general(a, b, dims, preferred_element_type=F32)


def lane_row(n):
    return lax.broadcasted_iota(jnp.int32, (1, n), 1)


def row_sum(v):
    return jnp.sum(v, axis=1, keepdims=True)


def col_sum(v):
    return jnp.sum(v, axis=0, keepdims=True)


def subnet(codes):
    width = (D // 6) * (4 + codes[0])
    return width, (HEADS - HEADS // 3 + codes[1]) * (D // HEADS), (width * (6 + codes[2])) // 2


def bias_places(groups):
    rows = D // groups
    for group in range(groups):
        for k in range(4):
            yield group * rows + k, k, group * rows


def unit_pieces(groups):
    rows = D // groups
    for k in range(4):
        for group in range(groups):
            yield k, group * rows, group * 4 * rows + k * rows


class Place:
    def __init__(self, depth):
        group, dp = lax.axis_index("group"), lax.axis_index("dp")
        self.depth = depth
        self.z, self.x, self.c, self.y = group // 4, (group // 2) % 2, group % 2, dp % 2
        self.dp = dp
        self.core_dev = (group + 1 - 2 * self.c, dp)
        self.x_dev = (group + 2 - 4 * self.x, dp)
        self.y_dev = (group, dp + 1 - 2 * self.y)

    def z_at(self, step):
        return lax.rem(self.z + step, self.depth)

    def z_from(self, step):
        return lax.rem(self.z - step + self.depth, self.depth)

    def z_dev(self, step):
        return ((self.z_at(step) * 2 + self.x) * 2 + self.c, self.dp)

    def greet(self):
        barrier = pltpu.get_barrier_semaphore()
        devs = [self.core_dev, self.x_dev, self.y_dev] + [self.z_dev(s) for s in range(1, self.depth)]
        for dev in devs:
            pl.semaphore_signal(barrier, inc=1, device_id=dev, device_id_type=MESH)
        pl.semaphore_wait(barrier, len(devs))


class Copies:
    def __init__(self, send_sems, recv_sems):
        self.send_sems, self.recv_sems, self.made, self.left = send_sems, recv_sems, [], set()

    def to(self, src, dst, dev):
        spot = len(self.made)
        copy = pltpu.make_async_remote_copy(
            src_ref=src,
            dst_ref=dst,
            send_sem=self.send_sems.at[spot],
            recv_sem=self.recv_sems.at[spot],
            device_id=dev,
            device_id_type=MESH,
        )
        self.made.append(copy)
        return copy

    def sent(self, copy):
        self.left.update(spot for spot, made in enumerate(self.made) if made is copy)
        copy.wait_send()

    def finish(self):
        for spot, copy in enumerate(self.made):
            if spot not in self.left:
                copy.wait_send()


def halves(width, y):
    half = width // 2
    mine = pl.ds(pl.multiple_of(y * half, 128), half)
    other = pl.ds(pl.multiple_of((1 - y) * half, 128), half)
    return mine, other


def gather_cross(here, copies, own, at, keep, width):
    z, x, c = here.z, here.x, here.c
    mine, other = halves(width, here.y)
    every = slice(None)
    steps = range(1, here.depth)

    def same(zz, xx, cols, dev):
        return copies.to(at(zz, xx, c, cols), at(zz, xx, c, cols), dev)

    first = copies.to(own(mine), at(z, x, c, mine), here.x_dev)
    own_z = [copies.to(own(mine), at(z, x, c, mine), here.z_dev(s)) for s in steps]
    side_z = [same(z, 1 - x, mine, here.z_dev(s)) for s in steps]
    side_y = same(z, 1 - x, mine, here.y_dev)
    far_y = [same(here.z_from(s), every, mine, here.y_dev) for s in steps]
    core = [same(every, every, cols, here.core_dev) for cols in (mine, other)]

    def stage0():
        keep.start()
        first.start()
        for copy in own_z:
            copy.start()

    def stage1():
        first.wait_recv()
        for copy in side_z:
            copy.start()
        side_y.start()

    def stage2():
        for k in range(len(own_z)):
            own_z[k].wait_recv()
            side_z[k].wait_recv()
            far_y[k].start()
        keep.wait()
        core[0].start()

    def stage3():
        for copy in [side_y] + far_y:
            copy.wait_recv()
        core[1].start()

    def stage4():
        for copy in core:
            copy.wait_recv()

    return [stage0, stage1, stage2, stage3, stage4]


def gather_line(here, copies, own, at, keep, width):
    z, x, c = here.z, here.x, here.c
    mine, other = halves(width, here.y)
    every = slice(None)
    steps = range(1, here.depth)

    def same(zz, xx, cols, dev):
        return copies.to(at(zz, xx, c, cols), at(zz, xx, c, cols), dev)

    own_z = [copies.to(own(mine), at(z, x, c, mine), here.z_dev(s)) for s in steps]
    own_x = copies.to(own(every), at(z, x, c, every), here.x_dev)
    froms = [here.z_from(s) for s in steps]
    y_hops = [same(zz, x, mine, here.y_dev) for zz in froms]
    x_mine = [same(zz, x, mine, here.x_dev) for zz in froms]
    x_other = [same(zz, x, other, here.x_dev) for zz in froms]
    core = [same(every, xx, every, here.core_dev) for xx in (x, 1 - x)]

    def stage0():
        keep.start()
        for copy in own_z:
            copy.start()
        own_x.start()

    def stage1():
        for k in range(len(own_z)):
            own_z[k].wait_recv()
            y_hops[k].start()
            x_mine[k].start()

    def stage2():
        for k in range(len(own_z)):
            y_hops[k].wait_recv()
            x_other[k].start()
        keep.wait()
        core[0].start()

    def stage3():
        for copy in [own_x] + x_mine + x_other:
            copy.wait_recv()
        core[1].start()

    def stage4():
        for copy in core:
            copy.wait_recv()

    return [stage0, stage1, stage2, stage3, stage4]


def gather_cross_copies(depth):
    return 4 + 3 * (depth - 1)


def gather_line_copies(depth):
    return 3 + 4 * (depth - 1)


def plus(a, b):
    return a + b


def reduce_part(here, copies, sibling, kept, room, final, width, cross):
    z, x, depth = here.z, here.x, here.depth
    mine, other = halves(width, here.y)
    steps = range(1, depth)
    if cross:
        first, second, third, fourth, fifth = room
        core = copies.to(sibling, first, here.core_dev)
        to_y = copies.to(first.at[:, :, :, other], second, here.y_dev)
        to_z = [copies.to(second.at[here.z_at(s)], third.at[s - 1], here.z_dev(s)) for s in steps]
        to_x = copies.to(fourth.at[1 - x], fifth, here.x_dev)
    else:
        first, second, third, fourth = room
        core = copies.to(sibling, first, here.core_dev)
        to_x = copies.to(first.at[:, 1 - x], second, here.x_dev)
        to_y = copies.to(second.at[:, :, other], third, here.y_dev)
        to_z = [copies.to(third.at[here.z_at(s)], fourth.at[s - 1], here.z_dev(s)) for s in steps]
    back = copies.to(final.at[:, mine], final.at[:, mine], here.y_dev)

    def stage0():
        core.start()

    def stage1():
        core.wait_recv()

        @pl.loop(0, depth)
        def _(zz):
            for xx in range(2):
                first[zz, xx] = plus(kept(zz, xx), first[zz, xx])

        if cross:
            to_y.start()
        else:
            to_x.start()

    def stage2():
        if cross:
            to_y.wait_recv()

            @pl.loop(0, depth)
            def _(zz):
                for xx in range(2):
                    second[zz, xx] = plus(first[zz, xx, :, mine], second[zz, xx])

            for copy in to_z:
                copy.start()
        else:
            to_x.wait_recv()

            @pl.loop(0, depth)
            def _(zz):
                second[zz] = plus(first[zz, x], second[zz])

            to_y.start()

    def stage3():
        if cross:
            for copy in to_z:
                copy.wait_recv()

            @pl.loop(0, 2)
            def _(xx):
                total = second[z, xx].astype(F32)
                for s in steps:
                    total += third[s - 1, xx].astype(F32)
                fourth[xx] = total.astype(LOW)

            to_x.start()
        else:
            to_y.wait_recv()

            @pl.loop(0, depth)
            def _(zz):
                third[zz] = plus(second[zz, :, mine], third[zz])

            for copy in to_z:
                copy.start()

    def stage4():
        if cross:
            to_x.wait_recv()
            final[:, mine] = plus(fourth[x], fifth[...])
        else:
            for copy in to_z:
                copy.wait_recv()
            total = third[z].astype(F32)
            for s in steps:
                total += fourth[s - 1].astype(F32)
            final[:, mine] = total.astype(LOW)
        back.start()

    def stage5():
        back.wait_recv()

    return [stage0, stage1, stage2, stage3, stage4, stage5, lambda: copies.sent(core)]


def reduce_room(depth, rows, width, cross):
    half = width // 2
    if cross:
        shapes = [(depth, 2, rows, width), (depth, 2, rows, half), (depth - 1, 2, rows, half), (2, rows, half), (rows, half)]
    else:
        shapes = [(depth, 2, rows, width), (depth, rows, width), (depth, rows, half), (depth - 1, rows, half)]
    return [pltpu.VMEM(shape, LOW) for shape in shapes]


def reduce_copies(depth):
    return 4 + depth - 1


def run(plans, todo):
    for plan, stage in todo:
        plans[plan][stage]()


def hook(at, actions):
    for k, action in actions.items():
        pl.when(at == k)(action)


def split3(v):
    high = v.astype(LOW).astype(F32)
    rest = v - high
    middle = rest.astype(LOW).astype(F32)
    return high, middle, rest - middle


def frame_tables(lengths, starts, frames, edge, query_side, key_side):
    lane = lane_row(128)
    place = lax.broadcasted_iota(jnp.int32, (frames, 1), 0)
    first, second = lengths[0, 0], lengths[0, 0] + lengths[0, 1]
    segment = (place >= first).astype(jnp.int32) + (place >= second).astype(jnp.int32)
    spread = jnp.broadcast_to(starts[...][:, None, :], (frames // 128, 128, 128)).reshape(frames, 128)
    start = jnp.max(jnp.where(lane == lax.rem(place, 128), spread, 0), axis=1, keepdims=True)
    edge[0:16, :] = jnp.full((16, 1), -1, jnp.int32)
    edge[pl.ds(16, frames), :] = jnp.where(start == 1, segment, -1)
    masked = segment < 0
    for offset in range(SPAN):
        masked = masked | (edge[pl.ds(16 - offset, frames), :] == segment)
    live = segment < 2
    masked = masked & live
    query_side[...] = jnp.where((lane < 3) & (lane != segment), far_score, 0.0).astype(LOW)
    ones = (lane == segment) | ((lane >= 3) & (lane < 6)) | ((lane == 6) & live) | ((lane == 7) & masked)
    key_side[...] = jnp.where(ones, 1.0, 0.0).astype(LOW)


def attend(proj, chunk, query_side, key_side, mixed, peaks, actions):
    frames = mixed.shape[0]
    blocks = frames // BLOCK
    lane = lane_row(128)

    @pl.loop(0, CHUNK_PAIRS)
    def _(part):
        pair = chunk * CHUNK_PAIRS + part
        col = pl.multiple_of(part * 128, 128)

        @pl.loop(0, blocks)
        def _(block):
            hook(pair * blocks + block, actions)
            rows = pl.ds(pl.multiple_of(block * BLOCK, BLOCK), BLOCK)
            query = proj[rows, pl.ds(col, 128)]
            keys = jnp.concatenate([proj[:, pl.ds(pl.multiple_of(CHUNK + col, 128), 128)], key_side[...]], axis=1)
            values = proj[:, pl.ds(pl.multiple_of(2 * CHUNK + col, 128), 128)]
            values = jnp.concatenate([values, jnp.ones((frames, 128), LOW)], axis=1)
            side = query_side[rows, :]
            found = []
            for h in range(2):
                own = jnp.where((lane < 64) == (h == 0), query, jnp.zeros_like(query))
                scores = dot(jnp.concatenate([own, side], axis=1), keys, NT)
                peak = jnp.max(scores, axis=1, keepdims=True)
                weights = jnp.exp(scores - peak).astype(LOW)
                sums = dot(weights, values)
                total = sums[:, 128:]
                high, middle, low = split3(-(peak + jnp.log(total)))
                table = jnp.where(lane == 3, high, jnp.where(lane == 4, middle, jnp.where(lane == 5, low, side.astype(F32))))
                peaks[2 * pair + h, rows, :] = table.astype(LOW)
                found.append(sums[:, :128] / total)
            mixed[rows, pl.ds(pl.multiple_of(pair * 128, 128), 128)] = jnp.where(lane < 64, found[0], found[1]).astype(LOW)


def attend_back(proj, chunk, peaks, key_side, grad_mixed, mixed, grad_proj, inner, grad_query, actions):
    frames = mixed.shape[0]
    blocks = frames // BLOCK
    lane = lane_row(128)

    @pl.loop(0, CHUNK_PAIRS)
    def _(part):
        pair = chunk * CHUNK_PAIRS + part
        all_col = pl.ds(pl.multiple_of(pair * 128, 128), 128)
        query_cols = pl.ds(pl.multiple_of(part * 128, 128), 128)
        key_cols = pl.ds(pl.multiple_of(CHUNK + part * 128, 128), 128)
        value_cols = pl.ds(pl.multiple_of(2 * CHUNK + part * 128, 128), 128)
        prod = grad_mixed[:, all_col].astype(F32) * mixed[:, all_col].astype(F32)
        for h in range(2):
            high, middle, low = split3(-row_sum(jnp.where((lane < 64) == (h == 0), prod, 0.0)))
            table = jnp.where(lane == 3, high, jnp.where(lane == 4, middle, jnp.where(lane == 5, low, 0.0)))
            inner[h] = table.astype(LOW)

        @pl.loop(0, blocks)
        def _(block):
            hook(pair * blocks + block, actions)
            rows = pl.ds(pl.multiple_of(block * BLOCK, BLOCK), BLOCK)
            key, value, side = proj[rows, key_cols], proj[rows, value_cols], key_side[rows, :]
            keys = jnp.concatenate([key, side], axis=1)
            values = jnp.concatenate([value, side], axis=1)
            query, grad = proj[:, query_cols], grad_mixed[:, all_col]
            grad_v = grad_k = grad_q = 0.0
            for h in range(2):
                own = (lane < 64) == (h == 0)
                query_h = jnp.where(own, query, jnp.zeros_like(query))
                grad_h = jnp.where(own, grad, jnp.zeros_like(grad))
                key_h = jnp.where(own, key, jnp.zeros_like(key))
                probs = jnp.exp(dot(keys, jnp.concatenate([query_h, peaks[2 * part + h]], axis=1), NT))
                shifted = dot(values, jnp.concatenate([grad_h, inner[h]], axis=1), NT)
                grad_s = (probs * shifted).astype(LOW)
                grad_v += dot(probs.astype(LOW), grad_h)
                grad_k += dot(grad_s, query_h)
                grad_q += dot(grad_s, key_h, TN)
            grad_proj[rows, key_cols] = grad_k.astype(LOW)
            grad_proj[rows, value_cols] = grad_v.astype(LOW)

            @pl.when(block == 0)
            def _():
                grad_query[...] = grad_q

            @pl.when(block > 0)
            def _():
                grad_query[...] += grad_q

        grad_proj[:, query_cols] = (grad_query[...] * 0.125).astype(LOW)


VM = pl.BlockSpec(memory_space=pltpu.VMEM)
SM = pl.BlockSpec(memory_space=pltpu.SMEM)
HBM = pl.BlockSpec(memory_space=pl.ANY)


def flat(value):
    return value.reshape(D, value.shape[-1])


def chunk_cols(matrix, j):
    return [matrix[:, k * D + j * CHUNK : k * D + (j + 1) * CHUNK] for k in range(3)]


GATHER_CROSS = [False, False, True, False, False, True, False, False]
GATHER_FIRST = [
    (3, 0), (0, 0), (1, 0), (2, 0), (6, 0), (7, 0), (5, 0), (3, 1), (4, 0), (3, 2),
    (0, 1), (2, 1), (1, 1), (0, 2), (1, 2), (5, 1), (6, 1), (3, 3), (3, 4), (6, 2),
    (0, 3), (7, 1), (1, 3), (0, 4),
]
GATHER_THEN = {
    0: [(1, 4)],
    2: [(7, 2)],
    3: [(4, 1), (6, 3)],
    4: [(2, 2), (6, 4)],
    5: [(4, 2)],
    6: [(5, 2)],
    7: [(2, 3)],
    9: [(7, 4)],
    10: [(4, 3), (5, 3)],
}
GATHER_CHUNK = {
    2: [(7, 3), (2, 4)],
}
GATHER_LAST = [
    (4, 4), (5, 4),
]


def front(depth, groups, codes, lengths, starts, frames, weights):
    count = frames.shape[0]

    def body(codes, lengths, starts, frames, small_full, chunks, proj, x0, mixed, peaks, key_side, small, bias, query_side, edge, early, enter, actions):
        width, heads, _ = subnet(codes)
        features = (lane_row(D) < width).astype(F32)
        frame_tables(lengths, starts, count, edge, query_side, key_side)
        early()
        table = flat(small_full[...]).astype(F32)
        small[...] = table[:, :128].T[0:16, :]
        for row, at, col in bias_places(groups):
            bias[at : at + 1, col : col + D // groups] = table[row : row + 1, 128 : 128 + D // groups]
        masked = key_side[:, 7:8].astype(F32)
        start = jnp.where(masked > 0, small[6:7, :], frames[...].astype(F32)) * features
        x0[...] = start.astype(LOW)

        @pl.loop(0, CHUNKS)
        def _(j):
            enter(j)
            cols = pl.ds(pl.multiple_of(j * CHUNK, CHUNK), CHUNK)
            active = (lane_row(CHUNK) + j * CHUNK < heads).astype(F32)
            value = dot(x0[...], flat(chunks[j]))
            for k in range(3):
                piece = value[:, k * CHUNK : (k + 1) * CHUNK]
                if k != 1:
                    piece = piece + small[k // 2 : k // 2 + 1, cols]
                piece = (piece * active).astype(LOW)
                proj[j, :, k * CHUNK : (k + 1) * CHUNK] = piece * jnp.asarray(0.125, LOW) if k == 0 else piece
            attend(proj.at[j], j, query_side, key_side, mixed, peaks, actions)

    shape = jax.ShapeDtypeStruct
    found = (
        shape((CHUNKS, count, D), LOW),
        shape((count, D), LOW),
        shape((count, D), LOW),
        shape((HEADS, count, 128), LOW),
        shape((count, 128), LOW),
        shape((16, D), F32),
        shape((4, D), F32),
    )
    scratch = [pltpu.VMEM((count, 128), LOW), pltpu.VMEM((count + 16, 1), jnp.int32)]
    params = dict(has_side_effects=True, vmem_limit_bytes=62 * MIB)
    if not depth:

        def plain(codes, lengths, starts, frames, head, chunks, *rest):
            body(codes, lengths, starts, frames, head, chunks, *rest, lambda: None, lambda j: None, {})

        return pl.pallas_call(
            plain,
            out_shape=found,
            in_specs=[SM, SM, VM, VM, VM, VM],
            out_specs=(VM,) * 7,
            scratch_shapes=scratch,
            compiler_params=pltpu.CompilerParams(vmem_limit_bytes=62 * MIB),
            name="front_plain",
        )(codes, lengths, starts, frames, *weights)

    rows = weights[0].shape[0]

    def fused(*refs):
        codes, lengths, starts, frames = refs[:4]
        qkv_own, out_own, in_own, down_own, bias_own, gains_own, shifts_own = refs[4:11]
        proj, x0, mixed, peaks, key_side, small, bias, head, chunks, wide, down = refs[11:22]
        query_side, edge, pad, square, in_v, head_low, chunks_low, wide_low, down_low, send, recv, local = refs[22:]
        here = Place(depth)
        z, x, c = here.z, here.x, here.c
        copies = Copies(send, recv)

        def plan(k, own, full, width):
            gather = gather_cross if GATHER_CROSS[k] else gather_line
            keep = pltpu.make_async_copy(own(slice(None)), full(z, x, c, slice(None)), local.at[k])
            return gather(here, copies, own, full, keep, width)

        def chunk_plan(k):
            return plan(k, lambda cols: chunks_low.at[k, :, cols], lambda zz, xx, cc, cols: chunks.at[k, zz, xx, cc, :, cols], D)

        def blocks_plan(k, first, count, own, full):
            cut = pl.ds(first, count)
            return plan(k, lambda cols: own.at[cut, :, cols], lambda zz, xx, cc, cols: full.at[cut, zz, xx, cc, :, cols], D)

        plans = [chunk_plan(j) for j in range(CHUNKS)]
        plans.append(plan(3, lambda cols: head_low.at[:, cols], lambda zz, xx, cc, cols: head.at[zz, xx, cc, :, cols], SMALL))
        plans += [blocks_plan(4 + k, 2 * k, 2, down_low, down) for k in range(2)]
        plans += [blocks_plan(6 + k, 2 * k, 2 + k, wide_low, wide) for k in range(2)]
        square[...] = jnp.zeros_like(square)
        square[0:7, 0:rows] = shifts_own[...]
        square[7:9, 0:rows] = gains_own[...]
        pad[...] = jnp.zeros_like(pad)
        pad[:, :128] = square[...].T[:rows, :]
        for k in range(4):
            pad[k : k + 1, 128 : 128 + rows] = bias_own[:, k * rows : (k + 1) * rows]
        for j in range(CHUNKS):
            chunks_low[j] = jnp.concatenate(chunk_cols(qkv_own, j), axis=1).astype(LOW)
        head_low[...] = pad[...].astype(LOW)
        here.greet()

        def early():
            cut = min(k for k, (plan, _) in enumerate(GATHER_FIRST) if plan > 3)
            run(plans, GATHER_FIRST[:cut])
            wide_low[0] = out_own[...].astype(LOW)
            for k, col, unit in unit_pieces(groups):
                in_v[k, :, col : col + rows] = in_own[:, unit : unit + rows]
            for k in range(4):
                wide_low[1 + k] = in_v[k].astype(LOW)
                down_low[k] = down_own[k * rows : (k + 1) * rows, :].astype(LOW)
            run(plans, GATHER_FIRST[cut:])

        def enter(j):
            hook(j, {k: functools.partial(run, plans, todo) for k, todo in GATHER_CHUNK.items()})

        actions = {k: functools.partial(run, plans, todo) for k, todo in GATHER_THEN.items()}
        body(codes, lengths, starts, frames, head, chunks, proj, x0, mixed, peaks, key_side, small, bias, query_side, edge, early, enter, actions)
        run(plans, GATHER_LAST)
        copies.finish()

    copies = sum(gather_cross_copies(depth) if cross else gather_line_copies(depth) for cross in GATHER_CROSS)
    return pl.pallas_call(
        fused,
        out_shape=found
        + (
            shape((depth, 2, 2, rows, SMALL), LOW),
            shape((CHUNKS, depth, 2, 2, rows, D), LOW),
            shape((5, depth, 2, 2, rows, D), LOW),
            shape((4, depth, 2, 2, rows, D), LOW),
        ),
        in_specs=[SM, SM] + [VM] * 9,
        out_specs=(VM,) * 9 + (HBM, HBM),
        scratch_shapes=scratch
        + [
            pltpu.VMEM((rows, SMALL), F32),
            pltpu.VMEM((128, 128), F32),
            pltpu.VMEM((4, rows, D), F32),
            pltpu.VMEM((rows, SMALL), LOW),
            pltpu.VMEM((CHUNKS, rows, D), LOW),
            pltpu.VMEM((5, rows, D), LOW),
            pltpu.VMEM((4, rows, D), LOW),
            pltpu.SemaphoreType.DMA((copies,)),
            pltpu.SemaphoreType.DMA((copies,)),
            pltpu.SemaphoreType.DMA((8,)),
        ],
        compiler_params=pltpu.CompilerParams(collective_id=0, **params),
        name="front",
    )(codes, lengths, starts, frames, *weights)


def normal_parts(v):
    bell = jnp.exp(v * v * -0.5)
    t = 1.0 / (1.0 + (0.3275911 * root_half) * jnp.abs(v))
    tail = t * (0.127414796 + t * (-0.142248368 + t * (0.7107068705 + t * (-0.7265760135 + t * 0.5307027145)))) * bell
    return jnp.where(v < 0, tail, 1.0 - tail), bell


def middle(groups, codes, mixed, x0, cotangent, key_side, wide, down, small, bias):
    count = mixed.shape[0]
    size = BLOCK // 2
    steps = count // size
    numbers = jnp.arange(FF, dtype=jnp.int32).reshape(groups, 4, D // groups).transpose(1, 0, 2).reshape(4, D)

    def kernel(codes, mixed, x0, cotangent, key_side, wide, down, small, bias, numbers, out, grad_mixed, grad_one, act_all, pre_all, hidden_all,
               ffn_all, branch_all, sums, bias_sums, wide_v, down_v, slope, in_sems):
        step = pl.program_id(0)
        width, heads, units = subnet(codes)
        features = (lane_row(D) < width).astype(F32)
        active = (lane_row(D) < heads).astype(F32)
        scale = 1.0 / width.astype(F32)
        loads = [pltpu.make_async_copy(wide.at[k], wide_v.at[k], in_sems.at[k]) for k in range(5)]
        loads += [pltpu.make_async_copy(down.at[k], down_v.at[k], in_sems.at[5 + k]) for k in range(4)]

        def ready(k):
            pl.when(step == 0)(loads[k].wait)

        @pl.when(step == 0)
        def _():
            for load in loads:
                load.start()
            sums[...] = jnp.zeros_like(sums)
            bias_sums[...] = jnp.zeros_like(bias_sums)

        def param(k):
            return small[k : k + 1, :]

        ready(0)
        resid = x0[...].astype(F32) + (dot(mixed[...], wide_v[0]) + param(2)) * features
        centered = (resid - row_sum(resid) * scale) * features
        inv_one = lax.rsqrt(row_sum(centered * centered) * scale + norm_eps)
        normed_one = centered * inv_one
        hidden = (normed_one * param(7) + param(4)) * features
        hidden_low = hidden.astype(LOW)
        hidden_all[...] = hidden_low
        branch = 0.0
        for j in range(4):
            ready(1 + j)
            unit_mask = (numbers[j : j + 1, :] < units).astype(F32)
            pre = (dot(hidden_low, wide_v[1 + j]) + bias[j : j + 1, :]) * unit_mask
            share, bell = normal_parts(pre)
            act = (pre * share).astype(LOW)
            act_all[j] = act
            slope[j] = (share + pre * bell * inv_root_tau) * unit_mask
            ready(5 + j)
            branch += dot(act, down_v[j])
        resid = hidden + (branch + param(3)) * features
        centered = (resid - row_sum(resid) * scale) * features
        inv_two = lax.rsqrt(row_sum(centered * centered) * scale + norm_eps)
        normed_two = centered * inv_two
        live = key_side[:, 6:7].astype(F32)
        out[...] = ((normed_two * param(8) + param(5)) * features * live).astype(LOW)
        grad_out = cotangent[...].astype(F32) * live
        grad_n = grad_out * (param(8) * features)
        grad_two = inv_two * features * (grad_n - row_sum(grad_n) * scale - normed_two * (row_sum(grad_n * normed_two) * scale))
        grad_ffn = grad_two.astype(LOW)
        ffn_all[...] = grad_ffn
        back = 0.0
        for j in range(4):
            grad_pre = (dot(grad_ffn, down_v[j], NT) * slope[j]).astype(LOW)
            pre_all[j] = grad_pre
            bias_sums[j : j + 1, :] += col_sum(grad_pre.astype(F32))
            back += dot(grad_pre, wide_v[1 + j], NT)
        grad_hidden = grad_two + back * features
        grad_n = grad_hidden * (param(7) * features)
        grad_res = inv_one * features * (grad_n - row_sum(grad_n) * scale - normed_one * (row_sum(grad_n * normed_one) * scale))
        grad_one[...] = grad_res
        grad_branch = grad_res.astype(LOW)
        branch_all[...] = grad_branch
        grad_mixed[...] = (dot(grad_branch, wide_v[0], NT) * active).astype(LOW)
        sums[0:1, :] += col_sum(grad_branch.astype(F32))
        sums[1:2, :] += col_sum(grad_ffn.astype(F32))
        sums[2:3, :] += col_sum(grad_hidden) * features
        sums[3:4, :] += col_sum(grad_out) * features
        sums[4:5, :] += col_sum(grad_hidden * normed_one)
        sums[5:6, :] += col_sum(grad_out * normed_two)

    block = pl.BlockSpec((size, D), lambda i: (i, 0))
    four = pl.BlockSpec((4, size, D), lambda i: (0, i, 0))
    shape = jax.ShapeDtypeStruct
    return pl.pallas_call(
        kernel,
        grid=(steps,),
        in_specs=[SM, block, block, block, pl.BlockSpec((size, 128), lambda i: (i, 0)), HBM, HBM]
        + [pl.BlockSpec((16, D), lambda i: (0, 0)), pl.BlockSpec((4, D), lambda i: (0, 0)), pl.BlockSpec((4, D), lambda i: (0, 0))],
        out_specs=(block, block, block, four, four, block, block, block, pl.BlockSpec((8, D), lambda i: (0, 0)), pl.BlockSpec((4, D), lambda i: (0, 0))),
        out_shape=(
            shape((count, D), LOW),
            shape((count, D), LOW),
            shape((count, D), F32),
            shape((4, count, D), LOW),
            shape((4, count, D), LOW),
            shape((count, D), LOW),
            shape((count, D), LOW),
            shape((count, D), LOW),
            shape((8, D), F32),
            shape((4, D), F32),
        ),
        scratch_shapes=[
            pltpu.VMEM((5, D, D), LOW),
            pltpu.VMEM((4, D, D), LOW),
            pltpu.VMEM((4, size, D), F32),
            pltpu.SemaphoreType.DMA((9,)),
        ],
        compiler_params=pltpu.CompilerParams(vmem_limit_bytes=62 * MIB),
        name="middle",
    )(codes, mixed, x0, cotangent, key_side, wide, down, small, bias, numbers)


SUM_CROSS = [False, False, True, True, True, True, False, True, True, True, False, False, True, True]
SUM_EARLY = {
    0: [(0, 0)],
    1: [(1, 0)],
    2: [(2, 0), (0, 1)],
    3: [(3, 0), (1, 1)],
    4: [(4, 0), (2, 1)],
    5: [(5, 0), (3, 1)],
    6: [(6, 0), (4, 1), (0, 2)],
    7: [(7, 0), (5, 1)],
    8: [(8, 0), (6, 1), (2, 2), (1, 2)],
}
SUM_THEN = {
    0: [(7, 1), (8, 1)],
    1: [(3, 2)],
    2: [(6, 2), (2, 3)],
    3: [(4, 2), (2, 4), (0, 3)],
    4: [(5, 2)],
    5: [(4, 3), (3, 4), (1, 3), (9, 1), (0, 4)],
    6: [(4, 4), (7, 2)],
    7: [(5, 3)],
    8: [(3, 5), (7, 3)],
    9: [(10, 1), (7, 4)],
    10: [(9, 2), (0, 5), (4, 5), (8, 3), (1, 5), (5, 5)],
    11: [(7, 5), (6, 4)],
}
SUM_CHUNK = {
    0: [(9, 0), (3, 3)],
    1: [(10, 0), (1, 4), (8, 2), (5, 4), (6, 3), (2, 5)],
    2: [(11, 0), (12, 0), (10, 2), (8, 4), (6, 5), (9, 3)],
}
SUM_SMALL = [
    (13, 0),
]
SUM_LAST = [
    (11, 1), (9, 4), (12, 1), (10, 3), (13, 1), (8, 5), (9, 5), (12, 2), (11, 2), (13, 2),
    (10, 4), (12, 3), (11, 3), (10, 5), (13, 3), (12, 4), (13, 4), (11, 4), (12, 5), (13, 5),
    (11, 5),
]


def back(depth, groups, codes, proj, peaks, key_side, grad_mixed, mixed, x0, grad_one, chunks, sums, bias_sums, saved):
    count = mixed.shape[0]
    heads = HEADS // CHUNKS
    act, pre, hidden, ffn, branch = saved

    def weight_grads(mixed, act, pre, hidden, ffn, branch, lanes_v, left_v, right_v, loads, step):
        def fetch(k, source):
            return pltpu.make_async_copy(source, lanes_v.at[lax.rem(k, 2)], loads.at[lax.rem(k, 2)])

        right = pltpu.make_async_copy(ffn, right_v, loads.at[2])
        left = pltpu.make_async_copy(hidden, left_v, loads.at[3])
        last = pltpu.make_async_copy(branch, right_v, loads.at[2])
        fetch(0, act.at[0]).start()
        right.start()
        left.start()
        right.wait()

        @pl.loop(0, 4)
        def _(k):
            fetch(k, act.at[0]).wait()

            @pl.when(k < 3)
            def _():
                fetch(k + 1, act.at[k + 1]).start()

            @pl.when(k == 3)
            def _():
                fetch(0, pre.at[0]).start()

            step(k, dot(lanes_v[lax.rem(k, 2)], right_v[...], TN))

        left.wait()
        last.start()

        @pl.loop(0, 4)
        def _(k):
            fetch(k, pre.at[0]).wait()

            @pl.when(k < 3)
            def _():
                fetch(k + 1, pre.at[k + 1]).start()

            step(4 + k, dot(left_v[...], lanes_v[lax.rem(k, 2)], TN))

        last.wait()
        step(8, dot(mixed[...], right_v[...], TN))

    def body(codes, proj, peaks, key_side, grad_mixed, mixed, x0, grad_one, chunks, sums, bias_sums, act, pre, hidden, ffn, branch, frames_grad,
             proj_v, peaks_v, weight_v, grad_proj, left_v, inner, grad_query, total, rows_v, small_v, loads, step, put, actions, chunk_done):
        width, _, _ = subnet(codes)
        features = (lane_row(D) < width).astype(F32)
        one = pltpu.make_async_copy(grad_one, total, loads.at[6])
        out = pltpu.make_async_copy(total, frames_grad, loads.at[7])

        def fetch(j):
            slot = lax.rem(j, 2)
            return [
                pltpu.make_async_copy(proj.at[j], proj_v.at[slot], loads.at[slot]),
                pltpu.make_async_copy(peaks.at[pl.ds(j * heads, heads)], peaks_v.at[slot], loads.at[2 + slot]),
                pltpu.make_async_copy(chunks.at[j], weight_v.at[slot], loads.at[4 + slot]),
            ]

        one.start()
        rows_v[...] = jnp.zeros_like(rows_v)
        rows_v[2:6, :] = sums[0:4, :]
        rows_v[7:9, :] = sums[4:6, :]
        small_v[...] = jnp.zeros_like(small_v)
        for row, at, col in bias_places(groups):
            small_v[row : row + 1, 128 : 128 + D // groups] = bias_sums[at : at + 1, col : col + D // groups]

        weight_grads(mixed, act, pre, hidden, ffn, branch, proj_v, left_v, grad_proj, loads, step)
        for copy in fetch(0):
            copy.start()

        @pl.loop(0, CHUNKS)
        def _(j):
            slot = lax.rem(j, 2)
            for copy in fetch(j):
                copy.wait()

            @pl.when(j + 1 < CHUNKS)
            def _():
                for copy in fetch(j + 1):
                    copy.start()

            attend_back(proj_v.at[slot], j, peaks_v.at[slot], key_side, grad_mixed, mixed, grad_proj, inner, grad_query, actions)
            cols = pl.ds(pl.multiple_of(j * CHUNK, CHUNK), CHUNK)
            rows_v[0:1, cols] = col_sum(grad_proj[:, :CHUNK].astype(F32))
            rows_v[1:2, cols] = col_sum(grad_proj[:, 2 * CHUNK :].astype(F32))
            put(j, dot(x0[...], grad_proj[...], TN).astype(LOW))
            chunk_done(j)

            @pl.when(j == 0)
            def _():
                one.wait()

            total[...] += dot(grad_proj[...], flat(weight_v[slot]), NT) * features

        out.start()
        rows_v[6:7, :] = col_sum(total[...] * key_side[:, 7:8].astype(F32))
        small_v[:, :128] = rows_v[...].T
        put(None, small_v[...])
        chunk_done(None)
        return out

    shape = jax.ShapeDtypeStruct
    operands = (codes, proj, peaks, key_side, grad_mixed, mixed, x0, grad_one, chunks, sums, bias_sums, act, pre, hidden, ffn, branch)
    in_specs = [SM, HBM, HBM, VM, VM, VM, VM, HBM, HBM, VM, VM] + [HBM] * 5

    def scratch(weight_shape):
        return [
            pltpu.VMEM((2, count, D), LOW),
            pltpu.VMEM((2, heads, count, 128), LOW),
            pltpu.VMEM((2,) + weight_shape, LOW),
            pltpu.VMEM((count, D), LOW),
            pltpu.VMEM((count, D), LOW),
            pltpu.VMEM((2, count, 128), LOW),
            pltpu.VMEM((count, 128), F32),
            pltpu.VMEM((count, D), F32),
            pltpu.VMEM((128, D), F32),
            pltpu.VMEM((D, SMALL), F32),
            pltpu.SemaphoreType.DMA((8,)),
        ]

    if not depth:

        def plain(*refs):
            inputs, parts, small, weight_parts, rest = refs[:17], refs[17], refs[18], refs[19], refs[20:]

            def step(k, value):
                weight_parts[k] = value.astype(LOW)

            def put(j, value):
                if j is None:
                    small[...] = value
                else:
                    parts[j] = value

            body(*inputs, *rest, step, put, {}, lambda j: None).wait()

        return pl.pallas_call(
            plain,
            out_shape=(shape((count, D), F32), shape((CHUNKS, D, D), LOW), shape((D, SMALL), F32), shape((9, D, D), LOW)),
            in_specs=in_specs,
            out_specs=(HBM, VM, VM, VM),
            scratch_shapes=scratch((D, D)),
            compiler_params=pltpu.CompilerParams(vmem_limit_bytes=62 * MIB),
            name="back_plain",
        )(*operands)

    rows, tall = D // groups, FF // groups
    sizes = [(rows, D)] * 11 + [(rows, D - SMALL), (rows, SMALL), (rows, SMALL)]
    rooms = [reduce_room(depth, *size, cross) for size, cross in zip(sizes, SUM_CROSS)]
    starts = [sum(len(room) for room in rooms[:k]) for k in range(len(rooms) + 1)]

    def fused(*refs):
        inputs, chunk_own, wide_own, down_own, small_own = refs[:17], *refs[17:21]
        inside, (send, recv, ring, chunk_part, small_part), rest = refs[21:32], refs[32:37], refs[37:]
        room_refs, finals = rest[: starts[-1]], rest[starts[-1] :]
        here = Place(depth)
        c = here.c
        copies = Copies(send, recv)
        plans = []

        def plan(sibling, kept):
            k = len(plans)
            plans.append(reduce_part(here, copies, sibling, kept, room_refs[starts[k] : starts[k + 1]], finals[k], sizes[k][1], SUM_CROSS[k]))

        for k in range(9):
            plan(ring.at[k % 3, :, :, 1 - c], lambda zz, xx, k=k: ring[k % 3, zz, xx, c])
        for k in range(2):
            plan(chunk_part.at[k, :, :, 1 - c], lambda zz, xx, k=k: chunk_part[k, zz, xx, c])
        for cut in (pl.ds(0, D - SMALL), pl.ds(D - SMALL, SMALL)):
            plan(chunk_part.at[2, :, :, 1 - c, :, cut], lambda zz, xx, cut=cut: chunk_part[2, zz, xx, c, :, cut])
        plan(small_part.at[:, :, 1 - c], lambda zz, xx: small_part[zz, xx, c])
        def step(k, value):
            hook(k, {at: plans[at - 3][6] for at in range(3, 9)})
            ring[lax.rem(k, 3)] = value.astype(LOW).reshape(depth, 2, 2, rows, D)
            hook(k, {at: functools.partial(run, plans, todo) for at, todo in SUM_EARLY.items()})

        def put(j, value):
            if j is None:
                small_part[...] = value.astype(LOW).reshape(depth, 2, 2, rows, SMALL)
            else:
                chunk_part[j] = value.reshape(depth, 2, 2, rows, D)

        here.greet()
        actions = {k: functools.partial(run, plans, todo) for k, todo in SUM_THEN.items()}

        def chunk_done(j):
            if j is None:
                run(plans, SUM_SMALL)
            else:
                hook(j, {k: functools.partial(run, plans, todo) for k, todo in SUM_CHUNK.items()})

        out = body(*inputs, *inside, step, put, actions, chunk_done)
        run(plans, SUM_LAST)
        for k in range(4):
            down_own[k * rows : (k + 1) * rows, :] = finals[k][...]
            wide_own[1 + k] = finals[4 + k][...]
        wide_own[0] = finals[8][...]
        for k in range(2):
            chunk_own[k] = finals[9 + k][...]
        chunk_own[2, :, : D - SMALL] = finals[11][...]
        chunk_own[2, :, D - SMALL :] = finals[12][...]
        small_own[...] = finals[13][...]
        out.wait()
        copies.finish()

    copies = reduce_copies(depth) * len(sizes)
    return pl.pallas_call(
        fused,
        out_shape=(
            shape((count, D), F32),
            shape((CHUNKS, rows, D), LOW),
            shape((5, rows, D), LOW),
            shape((tall, D), LOW),
            shape((rows, SMALL), LOW),
        ),
        in_specs=in_specs,
        out_specs=(HBM,) + (VM,) * 4,
        scratch_shapes=scratch((depth, 2, 2, rows, D))
        + [
            pltpu.SemaphoreType.DMA((copies,)),
            pltpu.SemaphoreType.DMA((copies,)),
            pltpu.VMEM((3, depth, 2, 2, rows, D), LOW),
            pltpu.VMEM((CHUNKS, depth, 2, 2, rows, D), LOW),
            pltpu.VMEM((depth, 2, 2, rows, SMALL), LOW),
        ]
        + [ref for room in rooms for ref in room]
        + [pltpu.VMEM(size, LOW) for size in sizes],
        compiler_params=pltpu.CompilerParams(collective_id=1, has_side_effects=True, vmem_limit_bytes=62 * MIB),
        name="back",
    )(*operands)


def finish(total, key_side, chunk_own, wide_own, down_own, small_own):
    count, (_, rows, _), tall = total.shape[0], chunk_own.shape, down_own.shape[0]
    size = count // 4

    def kernel(total, key_side, chunk_own, wide_own, down_own, small_own,
               frames_grad, qkv_grad, out_grad, in_grad, down_grad, bias_grad, gains_grad, shifts_grad, square, in_v):
        frames_grad[...] = total[...] * (1.0 - key_side[:, 7:8].astype(F32))

        @pl.when(pl.program_id(0) == 0)
        def _():
            for j in range(CHUNKS):
                for k in range(3):
                    piece = chunk_own[j, :, k * CHUNK : (k + 1) * CHUNK]
                    qkv_grad[:, k * D + j * CHUNK : k * D + (j + 1) * CHUNK] = piece.astype(F32)
            out_grad[...] = wide_own[0].astype(F32)
            for k in range(4):
                in_v[k] = wide_own[1 + k].astype(F32)
            for k, col, unit in unit_pieces(D // rows):
                in_grad[:, unit : unit + rows] = in_v[k, :, col : col + rows]
            down_grad[...] = down_own[...].astype(F32)
            table = small_own[...].astype(F32)
            square[...] = jnp.zeros_like(square)
            square[0:rows, :] = table[:, :128]
            turned = square[...].T
            shifts_grad[...] = turned[0:7, 0:rows]
            gains_grad[...] = turned[7:9, 0:rows]
            for k in range(4):
                bias_grad[:, k * rows : (k + 1) * rows] = table[k : k + 1, 128 : 128 + rows]

    def whole(*dims):
        return pl.BlockSpec(dims, lambda i: (0,) * len(dims))

    block = pl.BlockSpec((size, D), lambda i: (i, 0))
    outs = [(rows, 3 * D), (rows, D), (rows, FF), (tall, D), (1, tall), (2, rows), (7, rows)]
    return pl.pallas_call(
        kernel,
        grid=(4,),
        in_specs=[block, pl.BlockSpec((size, 128), lambda i: (i, 0))]
        + [whole(*part.shape) for part in (chunk_own, wide_own, down_own, small_own)],
        out_specs=(block,) + tuple(whole(*dims) for dims in outs),
        out_shape=(jax.ShapeDtypeStruct((count, D), F32),) + tuple(jax.ShapeDtypeStruct(dims, F32) for dims in outs),
        scratch_shapes=[pltpu.VMEM((128, 128), F32), pltpu.VMEM((4, rows, D), F32)],
        name="finish",
    )(total, key_side, chunk_own, wide_own, down_own, small_own)


def on_device(dp_size, frames, lengths, mask_starts, width_code, head_code, ffn_code, qkv_weight, out_weight, ffn_in_weight,
              ffn_out_weight, ffn_bias, norm_gains, shifts, cotangent):
    rows, tall = qkv_weight.shape[0], ffn_out_weight.shape[0]
    groups = D // rows
    fused = rows % 16 == 0 and groups % 4 == 0 and dp_size % 2 == 0
    depth = groups // 4 if fused else 0
    codes = jnp.concatenate([width_code, head_code, ffn_code])
    starts = mask_starts.reshape(frames.shape[0] // 128, 128)
    if fused:
        masters = (qkv_weight, out_weight, ffn_in_weight, ffn_out_weight, ffn_bias.reshape(1, tall), norm_gains.T, shifts.T)
        found = front(depth, groups, codes, lengths, starts, frames, masters)
        proj, x0, mixed, peaks, key_side, small, bias, head, chunks, wide, down = found
    else:
        spread = jnp.zeros((rows, 128), F32).at[:4, :rows].set(ffn_bias.reshape(4, rows))
        head = jnp.concatenate([shifts, norm_gains, jnp.zeros((rows, 119), F32), spread], axis=1).astype(LOW)
        chunks = jnp.stack([jnp.concatenate(chunk_cols(qkv_weight, j), axis=1) for j in range(CHUNKS)]).astype(LOW)
        blocks = ffn_in_weight.reshape(rows, groups, 4, rows).transpose(2, 0, 1, 3).reshape(4, rows, D)
        wide = jnp.concatenate([out_weight[None], blocks]).astype(LOW)
        head = lax.all_gather(head, "group", axis=0, tiled=True)
        chunks = lax.all_gather(chunks, "group", axis=1, tiled=True)
        wide = lax.all_gather(wide, "group", axis=1, tiled=True)
        down = lax.all_gather(ffn_out_weight.astype(LOW).reshape(4, rows, D), "group", axis=1, tiled=True)
        proj, x0, mixed, peaks, key_side, small, bias = front(0, groups, codes, lengths, starts, frames, (head, chunks))
    layer_out, grad_mixed, grad_one, *saved, sums, bias_sums = middle(
        groups, codes, mixed, x0, cotangent, key_side, wide.reshape(5, D, D), down.reshape(4, D, D), small, bias
    )
    shared = (codes, proj, peaks, key_side, grad_mixed, mixed, x0, grad_one, chunks, sums, bias_sums, saved)
    if fused:
        total, *owned = back(depth, groups, *shared)
        if dp_size > 2:
            owned = [0.5 * lax.psum(part, "dp") for part in owned]
    else:
        total, chunk_parts, small_part, weight_parts = back(0, groups, *shared)
        wide_part, down_part = weight_parts[jnp.array([8, 4, 5, 6, 7])], weight_parts[:4]
        owned = [
            lax.psum_scatter(chunk_parts.astype(F32), "group", scatter_dimension=1, tiled=True),
            lax.psum_scatter(wide_part.astype(F32), "group", scatter_dimension=1, tiled=True),
            lax.psum_scatter(down_part.astype(F32), "group", scatter_dimension=1, tiled=True).reshape(tall, D),
            lax.psum_scatter(small_part, "group", scatter_dimension=0, tiled=True),
        ]
        owned = [lax.psum(part.astype(LOW), "dp") for part in owned]
    frames_grad, qkv_grad, out_grad, ffn_in_grad, ffn_out_grad, bias_row, gains_rows, shifts_rows = finish(total, key_side, *owned)
    return (layer_out, frames_grad, qkv_grad, out_grad, ffn_in_grad, ffn_out_grad, bias_row.reshape(tall, 1), gains_rows.T, shifts_rows.T)


def solution(mesh):
    by_all, by_group = P(("group", "dp"), None), P("group", None)
    placed = (by_all, by_all, P(("group", "dp")), P("group"), P("group"), P("group")) + (by_group,) * 7 + (by_all,)
    return jax.shard_map(
        functools.partial(on_device, mesh.shape["dp"]),
        mesh=mesh,
        in_specs=placed,
        out_specs=(by_all, by_all) + (by_group,) * 7,
        check_vma=False,
    )
```

```python
import functools

import jax
import jax.numpy as jnp
from jax import lax
from jax.experimental import pallas as pl
from jax.experimental.pallas import tpu as pltpu
from jax.sharding import PartitionSpec as P

D = 768
HEADS = 12
FF = 3072
SPAN = 10
CHUNKS = 3
CHUNK = D // CHUNKS
CHUNK_PAIRS = HEADS // (2 * CHUNKS)
SMALL = 256
BLOCK = 512

norm_eps = 1e-05
far_score = -float(2**30)
root_half = 0.7071067811865476
inv_root_tau = 0.3989422804014327

F32, LOW = jnp.float32, jnp.bfloat16
NN = (((1,), (0,)), ((), ()))
NT = (((1,), (1,)), ((), ()))
TN = (((0,), (0,)), ((), ()))
MESH = pl.DeviceIdType.MESH
MIB = 2**20


def dot(a, b, dims=NN):
    return lax.dot_general(a, b, dims, preferred_element_type=F32)


def lane_row(n):
    return lax.broadcasted_iota(jnp.int32, (1, n), 1)


def row_sum(v):
    return jnp.sum(v, axis=1, keepdims=True)


def col_sum(v):
    return jnp.sum(v, axis=0, keepdims=True)


def subnet(codes):
    width = (D // 6) * (4 + codes[0])
    return width, (HEADS - HEADS // 3 + codes[1]) * (D // HEADS), (width * (6 + codes[2])) // 2


def bias_places(groups):
    rows = D // groups
    for group in range(groups):
        for k in range(4):
            yield group * rows + k, k, group * rows


def unit_pieces(groups):
    rows = D // groups
    for k in range(4):
        for group in range(groups):
            yield k, group * rows, group * 4 * rows + k * rows


class Place:
    def __init__(self, depth):
        group, dp = lax.axis_index("group"), lax.axis_index("dp")
        self.depth = depth
        self.z, self.x, self.c, self.y = group // 4, (group // 2) % 2, group % 2, dp % 2
        self.dp = dp
        self.core_dev = (group + 1 - 2 * self.c, dp)
        self.x_dev = (group + 2 - 4 * self.x, dp)
        self.y_dev = (group, dp + 1 - 2 * self.y)

    def z_at(self, step):
        return lax.rem(self.z + step, self.depth)

    def z_from(self, step):
        return lax.rem(self.z - step + self.depth, self.depth)

    def z_dev(self, step):
        return ((self.z_at(step) * 2 + self.x) * 2 + self.c, self.dp)

    def greet(self):
        barrier = pltpu.get_barrier_semaphore()
        devs = [self.core_dev, self.x_dev, self.y_dev] + [self.z_dev(s) for s in range(1, self.depth)]
        for dev in devs:
            pl.semaphore_signal(barrier, inc=1, device_id=dev, device_id_type=MESH)
        pl.semaphore_wait(barrier, len(devs))


class Copies:
    def __init__(self, send_sems, recv_sems):
        self.send_sems, self.recv_sems, self.made, self.left = send_sems, recv_sems, [], set()

    def to(self, src, dst, dev):
        spot = len(self.made)
        copy = pltpu.make_async_remote_copy(
            src_ref=src,
            dst_ref=dst,
            send_sem=self.send_sems.at[spot],
            recv_sem=self.recv_sems.at[spot],
            device_id=dev,
            device_id_type=MESH,
        )
        self.made.append(copy)
        return copy

    def sent(self, copy):
        self.left.update(spot for spot, made in enumerate(self.made) if made is copy)
        copy.wait_send()

    def finish(self):
        for spot, copy in enumerate(self.made):
            if spot not in self.left:
                copy.wait_send()


def halves(width, y):
    half = width // 2
    mine = pl.ds(pl.multiple_of(y * half, 128), half)
    other = pl.ds(pl.multiple_of((1 - y) * half, 128), half)
    return mine, other


def gather_cross(here, copies, own, at, keep, width):
    z, x, c = here.z, here.x, here.c
    mine, other = halves(width, here.y)
    every = slice(None)
    steps = range(1, here.depth)

    def same(zz, xx, cols, dev):
        return copies.to(at(zz, xx, c, cols), at(zz, xx, c, cols), dev)

    first = copies.to(own(mine), at(z, x, c, mine), here.x_dev)
    own_z = [copies.to(own(mine), at(z, x, c, mine), here.z_dev(s)) for s in steps]
    side_z = [same(z, 1 - x, mine, here.z_dev(s)) for s in steps]
    side_y = same(z, 1 - x, mine, here.y_dev)
    far_y = [same(here.z_from(s), every, mine, here.y_dev) for s in steps]
    core = [same(every, every, cols, here.core_dev) for cols in (mine, other)]

    def stage0():
        keep.start()
        first.start()
        for copy in own_z:
            copy.start()

    def stage1():
        first.wait_recv()
        for copy in side_z:
            copy.start()
        side_y.start()

    def stage2():
        for k in range(len(own_z)):
            own_z[k].wait_recv()
            side_z[k].wait_recv()
            far_y[k].start()
        keep.wait()
        core[0].start()

    def stage3():
        for copy in [side_y] + far_y:
            copy.wait_recv()
        core[1].start()

    def stage4():
        for copy in core:
            copy.wait_recv()

    return [stage0, stage1, stage2, stage3, stage4]


def gather_line(here, copies, own, at, keep, width):
    z, x, c = here.z, here.x, here.c
    mine, other = halves(width, here.y)
    every = slice(None)
    steps = range(1, here.depth)

    def same(zz, xx, cols, dev):
        return copies.to(at(zz, xx, c, cols), at(zz, xx, c, cols), dev)

    own_z = [copies.to(own(mine), at(z, x, c, mine), here.z_dev(s)) for s in steps]
    own_x = copies.to(own(every), at(z, x, c, every), here.x_dev)
    froms = [here.z_from(s) for s in steps]
    y_hops = [same(zz, x, mine, here.y_dev) for zz in froms]
    x_mine = [same(zz, x, mine, here.x_dev) for zz in froms]
    x_other = [same(zz, x, other, here.x_dev) for zz in froms]
    core = [same(every, xx, every, here.core_dev) for xx in (x, 1 - x)]

    def stage0():
        keep.start()
        for copy in own_z:
            copy.start()
        own_x.start()

    def stage1():
        for k in range(len(own_z)):
            own_z[k].wait_recv()
            y_hops[k].start()
            x_mine[k].start()

    def stage2():
        for k in range(len(own_z)):
            y_hops[k].wait_recv()
            x_other[k].start()
        keep.wait()
        core[0].start()

    def stage3():
        for copy in [own_x] + x_mine + x_other:
            copy.wait_recv()
        core[1].start()

    def stage4():
        for copy in core:
            copy.wait_recv()

    return [stage0, stage1, stage2, stage3, stage4]


def gather_cross_copies(depth):
    return 4 + 3 * (depth - 1)


def gather_line_copies(depth):
    return 3 + 4 * (depth - 1)


def plus(a, b):
    return a + b


def reduce_part(here, copies, sibling, kept, room, final, width, cross):
    z, x, depth = here.z, here.x, here.depth
    mine, other = halves(width, here.y)
    steps = range(1, depth)
    if cross:
        first, second, third, fourth, fifth = room
        core = copies.to(sibling, first, here.core_dev)
        to_y = copies.to(first.at[:, :, :, other], second, here.y_dev)
        to_z = [copies.to(second.at[here.z_at(s)], third.at[s - 1], here.z_dev(s)) for s in steps]
        to_x = copies.to(fourth.at[1 - x], fifth, here.x_dev)
    else:
        first, second, third, fourth = room
        core = copies.to(sibling, first, here.core_dev)
        to_x = copies.to(first.at[:, 1 - x], second, here.x_dev)
        to_y = copies.to(second.at[:, :, other], third, here.y_dev)
        to_z = [copies.to(third.at[here.z_at(s)], fourth.at[s - 1], here.z_dev(s)) for s in steps]
    back = copies.to(final.at[:, mine], final.at[:, mine], here.y_dev)

    def stage0():
        core.start()

    def stage1():
        core.wait_recv()

        @pl.loop(0, depth)
        def _(zz):
            for xx in range(2):
                first[zz, xx] = plus(kept(zz, xx), first[zz, xx])

        if cross:
            to_y.start()
        else:
            to_x.start()

    def stage2():
        if cross:
            to_y.wait_recv()

            @pl.loop(0, depth)
            def _(zz):
                for xx in range(2):
                    second[zz, xx] = plus(first[zz, xx, :, mine], second[zz, xx])

            for copy in to_z:
                copy.start()
        else:
            to_x.wait_recv()

            @pl.loop(0, depth)
            def _(zz):
                second[zz] = plus(first[zz, x], second[zz])

            to_y.start()

    def stage3():
        if cross:
            for copy in to_z:
                copy.wait_recv()

            @pl.loop(0, 2)
            def _(xx):
                total = second[z, xx].astype(F32)
                for s in steps:
                    total += third[s - 1, xx].astype(F32)
                fourth[xx] = total.astype(LOW)

            to_x.start()
        else:
            to_y.wait_recv()

            @pl.loop(0, depth)
            def _(zz):
                third[zz] = plus(second[zz, :, mine], third[zz])

            for copy in to_z:
                copy.start()

    def stage4():
        if cross:
            to_x.wait_recv()
            final[:, mine] = plus(fourth[x], fifth[...])
        else:
            for copy in to_z:
                copy.wait_recv()
            total = third[z].astype(F32)
            for s in steps:
                total += fourth[s - 1].astype(F32)
            final[:, mine] = total.astype(LOW)
        back.start()

    def stage5():
        back.wait_recv()

    return [stage0, stage1, stage2, stage3, stage4, stage5, lambda: copies.sent(core)]


def reduce_room(depth, rows, width, cross):
    half = width // 2
    if cross:
        shapes = [(depth, 2, rows, width), (depth, 2, rows, half), (depth - 1, 2, rows, half), (2, rows, half), (rows, half)]
    else:
        shapes = [(depth, 2, rows, width), (depth, rows, width), (depth, rows, half), (depth - 1, rows, half)]
    return [pltpu.VMEM(shape, LOW) for shape in shapes]


def reduce_copies(depth):
    return 4 + depth - 1


def run(plans, todo):
    for plan, stage in todo:
        plans[plan][stage]()


def hook(at, actions):
    for k, action in actions.items():
        pl.when(at == k)(action)


def split3(v):
    high = v.astype(LOW).astype(F32)
    rest = v - high
    middle = rest.astype(LOW).astype(F32)
    return high, middle, rest - middle


def frame_tables(lengths, starts, frames, edge, query_side, key_side):
    lane = lane_row(128)
    place = lax.broadcasted_iota(jnp.int32, (frames, 1), 0)
    first, second = lengths[0, 0], lengths[0, 0] + lengths[0, 1]
    segment = (place >= first).astype(jnp.int32) + (place >= second).astype(jnp.int32)
    spread = jnp.broadcast_to(starts[...][:, None, :], (frames // 128, 128, 128)).reshape(frames, 128)
    start = jnp.max(jnp.where(lane == lax.rem(place, 128), spread, 0), axis=1, keepdims=True)
    edge[0:16, :] = jnp.full((16, 1), -1, jnp.int32)
    edge[pl.ds(16, frames), :] = jnp.where(start == 1, segment, -1)
    masked = segment < 0
    for offset in range(SPAN):
        masked = masked | (edge[pl.ds(16 - offset, frames), :] == segment)
    live = segment < 2
    masked = masked & live
    query_side[...] = jnp.where((lane < 3) & (lane != segment), far_score, 0.0).astype(LOW)
    ones = (lane == segment) | ((lane >= 3) & (lane < 6)) | ((lane == 6) & live) | ((lane == 7) & masked)
    key_side[...] = jnp.where(ones, 1.0, 0.0).astype(LOW)


def attend(proj, chunk, query_side, key_side, mixed, peaks, actions):
    frames = mixed.shape[0]
    blocks = frames // BLOCK
    lane = lane_row(128)

    @pl.loop(0, CHUNK_PAIRS)
    def _(part):
        pair = chunk * CHUNK_PAIRS + part
        col = pl.multiple_of(part * 128, 128)

        @pl.loop(0, blocks)
        def _(block):
            hook(pair * blocks + block, actions)
            rows = pl.ds(pl.multiple_of(block * BLOCK, BLOCK), BLOCK)
            query = proj[rows, pl.ds(col, 128)]
            keys = jnp.concatenate([proj[:, pl.ds(pl.multiple_of(CHUNK + col, 128), 128)], key_side[...]], axis=1)
            values = proj[:, pl.ds(pl.multiple_of(2 * CHUNK + col, 128), 128)]
            values = jnp.concatenate([values, jnp.ones((frames, 128), LOW)], axis=1)
            side = query_side[rows, :]
            found = []
            for h in range(2):
                own = jnp.where((lane < 64) == (h == 0), query, jnp.zeros_like(query))
                scores = dot(jnp.concatenate([own, side], axis=1), keys, NT)
                peak = jnp.max(scores, axis=1, keepdims=True)
                weights = jnp.exp(scores - peak).astype(LOW)
                sums = dot(weights, values)
                total = sums[:, 128:]
                high, middle, low = split3(-(peak + jnp.log(total)))
                table = jnp.where(lane == 3, high, jnp.where(lane == 4, middle, jnp.where(lane == 5, low, side.astype(F32))))
                peaks[2 * pair + h, rows, :] = table.astype(LOW)
                found.append(sums[:, :128] / total)
            mixed[rows, pl.ds(pl.multiple_of(pair * 128, 128), 128)] = jnp.where(lane < 64, found[0], found[1]).astype(LOW)


def attend_back(proj, chunk, peaks, key_side, grad_mixed, mixed, grad_proj, inner, grad_query, actions):
    frames = mixed.shape[0]
    blocks = frames // BLOCK
    lane = lane_row(128)

    @pl.loop(0, CHUNK_PAIRS)
    def _(part):
        pair = chunk * CHUNK_PAIRS + part
        all_col = pl.ds(pl.multiple_of(pair * 128, 128), 128)
        query_cols = pl.ds(pl.multiple_of(part * 128, 128), 128)
        key_cols = pl.ds(pl.multiple_of(CHUNK + part * 128, 128), 128)
        value_cols = pl.ds(pl.multiple_of(2 * CHUNK + part * 128, 128), 128)
        prod = grad_mixed[:, all_col].astype(F32) * mixed[:, all_col].astype(F32)
        for h in range(2):
            high, middle, low = split3(-row_sum(jnp.where((lane < 64) == (h == 0), prod, 0.0)))
            table = jnp.where(lane == 3, high, jnp.where(lane == 4, middle, jnp.where(lane == 5, low, 0.0)))
            inner[h] = table.astype(LOW)

        @pl.loop(0, blocks)
        def _(block):
            hook(pair * blocks + block, actions)
            rows = pl.ds(pl.multiple_of(block * BLOCK, BLOCK), BLOCK)
            key, value, side = proj[rows, key_cols], proj[rows, value_cols], key_side[rows, :]
            keys = jnp.concatenate([key, side], axis=1)
            values = jnp.concatenate([value, side], axis=1)
            query, grad = proj[:, query_cols], grad_mixed[:, all_col]
            grad_v = grad_k = grad_q = 0.0
            for h in range(2):
                own = (lane < 64) == (h == 0)
                query_h = jnp.where(own, query, jnp.zeros_like(query))
                grad_h = jnp.where(own, grad, jnp.zeros_like(grad))
                key_h = jnp.where(own, key, jnp.zeros_like(key))
                probs = jnp.exp(dot(keys, jnp.concatenate([query_h, peaks[2 * part + h]], axis=1), NT))
                shifted = dot(values, jnp.concatenate([grad_h, inner[h]], axis=1), NT)
                grad_s = (probs * shifted).astype(LOW)
                grad_v += dot(probs.astype(LOW), grad_h)
                grad_k += dot(grad_s, query_h)
                grad_q += dot(grad_s, key_h, TN)
            grad_proj[rows, key_cols] = grad_k.astype(LOW)
            grad_proj[rows, value_cols] = grad_v.astype(LOW)

            @pl.when(block == 0)
            def _():
                grad_query[...] = grad_q

            @pl.when(block > 0)
            def _():
                grad_query[...] += grad_q

        grad_proj[:, query_cols] = (grad_query[...] * 0.125).astype(LOW)


VM = pl.BlockSpec(memory_space=pltpu.VMEM)
SM = pl.BlockSpec(memory_space=pltpu.SMEM)
HBM = pl.BlockSpec(memory_space=pl.ANY)


def flat(value):
    return value.reshape(D, value.shape[-1])


def chunk_cols(matrix, j):
    return [matrix[:, k * D + j * CHUNK : k * D + (j + 1) * CHUNK] for k in range(3)]


GATHER_CROSS = [False, True, False, True, False, False, True, False]
GATHER_FIRST = [
    (3, 0), (0, 0), (1, 0), (2, 0), (3, 1), (5, 0), (1, 1), (0, 1), (7, 0), (0, 2),
    (2, 1), (3, 2), (4, 0), (2, 2), (0, 3), (3, 3), (5, 1), (6, 0), (0, 4), (3, 4),
]
GATHER_THEN = {
    0: [(1, 2)],
    1: [(2, 3), (5, 2)],
    3: [(2, 4), (6, 1), (1, 3), (7, 1)],
    4: [(5, 3), (4, 1)],
    6: [(5, 4)],
    7: [(7, 2)],
    8: [(6, 2), (4, 2)],
    11: [(7, 3)],
}
GATHER_CHUNK = {
    1: [(1, 4)],
}
GATHER_LAST = [
    (4, 3), (7, 4), (6, 3), (4, 4), (6, 4),
]


def front(depth, groups, codes, lengths, starts, frames, weights):
    count = frames.shape[0]

    def body(codes, lengths, starts, frames, small_full, chunks, proj, x0, mixed, peaks, key_side, small, bias, query_side, edge, proj_v, peaks_v, out_sems, early, enter, actions):
        width, heads, _ = subnet(codes)
        features = (lane_row(D) < width).astype(F32)
        frame_tables(lengths, starts, count, edge, query_side, key_side)
        early()
        table = flat(small_full[...]).astype(F32)
        small[...] = table[:, :128].T[0:16, :]
        for row, at, col in bias_places(groups):
            bias[at : at + 1, col : col + D // groups] = table[row : row + 1, 128 : 128 + D // groups]
        masked = key_side[:, 7:8].astype(F32)
        start = jnp.where(masked > 0, small[6:7, :], frames[...].astype(F32)) * features
        x0[...] = start.astype(LOW)

        @pl.loop(0, CHUNKS)
        def _(j):
            enter(j)
            cols = pl.ds(pl.multiple_of(j * CHUNK, CHUNK), CHUNK)
            active = (lane_row(CHUNK) + j * CHUNK < heads).astype(F32)
            value = dot(x0[...], flat(chunks[j]))
            for k in range(3):
                piece = value[:, k * CHUNK : (k + 1) * CHUNK]
                if k != 1:
                    piece = piece + small[k // 2 : k // 2 + 1, cols]
                piece = (piece * active).astype(LOW)
                proj_v[j, :, k * CHUNK : (k + 1) * CHUNK] = piece * jnp.asarray(0.125, LOW) if k == 0 else piece
            pltpu.make_async_copy(proj_v.at[j], proj.at[j], out_sems.at[j]).start()
            attend(proj_v.at[j], j, query_side, key_side, mixed, peaks_v, actions)
            quarter = pl.ds(j * (HEADS // CHUNKS), HEADS // CHUNKS)
            pltpu.make_async_copy(peaks_v.at[quarter], peaks.at[quarter], out_sems.at[CHUNKS + j]).start()

        def leave():
            for j in range(CHUNKS):
                pltpu.make_async_copy(proj_v.at[j], proj.at[j], out_sems.at[j]).wait()
                quarter = pl.ds(j * (HEADS // CHUNKS), HEADS // CHUNKS)
                pltpu.make_async_copy(peaks_v.at[quarter], peaks.at[quarter], out_sems.at[CHUNKS + j]).wait()

        return leave

    shape = jax.ShapeDtypeStruct
    found = (
        shape((CHUNKS, count, D), LOW),
        shape((count, D), LOW),
        shape((count, D), LOW),
        shape((HEADS, count, 128), LOW),
        shape((count, 128), LOW),
        shape((16, D), F32),
        shape((4, D), F32),
    )
    scratch = [
        pltpu.VMEM((count, 128), LOW),
        pltpu.VMEM((count + 16, 1), jnp.int32),
        pltpu.VMEM((CHUNKS, count, D), LOW),
        pltpu.VMEM((HEADS, count, 128), LOW),
        pltpu.SemaphoreType.DMA((2 * CHUNKS,)),
    ]
    places = (HBM, VM, VM, HBM, VM, VM, VM)
    params = dict(has_side_effects=True, vmem_limit_bytes=62 * MIB)
    if not depth:

        def plain(codes, lengths, starts, frames, head, chunks, *rest):
            body(codes, lengths, starts, frames, head, chunks, *rest, lambda: None, lambda j: None, {})()

        return pl.pallas_call(
            plain,
            out_shape=found,
            in_specs=[SM, SM, VM, VM, VM, VM],
            out_specs=places,
            scratch_shapes=scratch,
            compiler_params=pltpu.CompilerParams(vmem_limit_bytes=62 * MIB),
            name="front_plain",
        )(codes, lengths, starts, frames, *weights)

    rows = weights[0].shape[0]

    def fused(*refs):
        codes, lengths, starts, frames = refs[:4]
        qkv_own, out_own, in_own, down_own, bias_own, gains_own, shifts_own = refs[4:11]
        proj, x0, mixed, peaks, key_side, small, bias, chunks_out, wide, down = refs[11:21]
        query_side, edge, proj_v, peaks_v, out_sems, head, chunks = refs[21:28]
        pad, square, in_v, head_low, chunks_low, wide_low, down_low, send, recv, local = refs[28:]
        here = Place(depth)
        z, x, c = here.z, here.x, here.c
        copies = Copies(send, recv)

        def plan(k, own, full, width):
            gather = gather_cross if GATHER_CROSS[k] else gather_line
            keep = pltpu.make_async_copy(own(slice(None)), full(z, x, c, slice(None)), local.at[k])
            return gather(here, copies, own, full, keep, width)

        def chunk_plan(k):
            return plan(k, lambda cols: chunks_low.at[k, :, cols], lambda zz, xx, cc, cols: chunks.at[k, zz, xx, cc, :, cols], D)

        def blocks_plan(k, first, count, own, full):
            cut = pl.ds(first, count)
            return plan(k, lambda cols: own.at[cut, :, cols], lambda zz, xx, cc, cols: full.at[cut, zz, xx, cc, :, cols], D)

        plans = [chunk_plan(j) for j in range(CHUNKS)]
        plans.append(plan(3, lambda cols: head_low.at[:, cols], lambda zz, xx, cc, cols: head.at[zz, xx, cc, :, cols], SMALL))
        plans += [blocks_plan(4 + k, 2 * k, 2, down_low, down) for k in range(2)]
        plans += [blocks_plan(6 + k, 2 * k, 2 + k, wide_low, wide) for k in range(2)]
        square[...] = jnp.zeros_like(square)
        square[0:7, 0:rows] = shifts_own[...]
        square[7:9, 0:rows] = gains_own[...]
        pad[...] = jnp.zeros_like(pad)
        pad[:, :128] = square[...].T[:rows, :]
        for k in range(4):
            pad[k : k + 1, 128 : 128 + rows] = bias_own[:, k * rows : (k + 1) * rows]
        for j in range(CHUNKS):
            chunks_low[j] = jnp.concatenate(chunk_cols(qkv_own, j), axis=1).astype(LOW)
        head_low[...] = pad[...].astype(LOW)
        here.greet()

        def early():
            cut = min(k for k, (plan, _) in enumerate(GATHER_FIRST) if plan > 3)
            run(plans, GATHER_FIRST[:cut])
            wide_low[0] = out_own[...].astype(LOW)
            for k, col, unit in unit_pieces(groups):
                in_v[k, :, col : col + rows] = in_own[:, unit : unit + rows]
            for k in range(4):
                wide_low[1 + k] = in_v[k].astype(LOW)
                down_low[k] = down_own[k * rows : (k + 1) * rows, :].astype(LOW)
            run(plans, GATHER_FIRST[cut:])

        def enter(j):
            hook(j, {k: functools.partial(run, plans, todo) for k, todo in GATHER_CHUNK.items()})

        actions = {k: functools.partial(run, plans, todo) for k, todo in GATHER_THEN.items()}
        leave = body(codes, lengths, starts, frames, head, chunks, proj, x0, mixed, peaks, key_side, small, bias,
                     query_side, edge, proj_v, peaks_v, out_sems, early, enter, actions)
        pass_on = pltpu.make_async_copy(chunks, chunks_out, local.at[8])
        pass_on.start()
        run(plans, GATHER_LAST)
        pass_on.wait()
        leave()
        copies.finish()

    copies = sum(gather_cross_copies(depth) if cross else gather_line_copies(depth) for cross in GATHER_CROSS)
    return pl.pallas_call(
        fused,
        out_shape=found
        + (
            shape((CHUNKS, depth, 2, 2, rows, D), LOW),
            shape((5, depth, 2, 2, rows, D), LOW),
            shape((4, depth, 2, 2, rows, D), LOW),
        ),
        in_specs=[SM, SM] + [VM] * 9,
        out_specs=places + (HBM,) * 3,
        scratch_shapes=scratch
        + [
            pltpu.VMEM((depth, 2, 2, rows, SMALL), LOW),
            pltpu.VMEM((CHUNKS, depth, 2, 2, rows, D), LOW),
            pltpu.VMEM((rows, SMALL), F32),
            pltpu.VMEM((128, 128), F32),
            pltpu.VMEM((4, rows, D), F32),
            pltpu.VMEM((rows, SMALL), LOW),
            pltpu.VMEM((CHUNKS, rows, D), LOW),
            pltpu.VMEM((5, rows, D), LOW),
            pltpu.VMEM((4, rows, D), LOW),
            pltpu.SemaphoreType.DMA((copies,)),
            pltpu.SemaphoreType.DMA((copies,)),
            pltpu.SemaphoreType.DMA((9,)),
        ],
        compiler_params=pltpu.CompilerParams(collective_id=0, **params),
        name="front",
    )(codes, lengths, starts, frames, *weights)


def normal_parts(v):
    bell = jnp.exp(v * v * -0.5)
    t = 1.0 / (1.0 + (0.3275911 * root_half) * jnp.abs(v))
    tail = t * (0.127414796 + t * (-0.142248368 + t * (0.7107068705 + t * (-0.7265760135 + t * 0.5307027145)))) * bell
    return jnp.where(v < 0, tail, 1.0 - tail), bell


def middle(groups, codes, mixed, x0, cotangent, key_side, wide, down, small, bias):
    count = mixed.shape[0]
    size = BLOCK // 2
    steps = count // size
    numbers = jnp.arange(FF, dtype=jnp.int32).reshape(groups, 4, D // groups).transpose(1, 0, 2).reshape(4, D)

    def kernel(codes, mixed, x0, cotangent, key_side, wide, down, small, bias, numbers, out, grad_mixed, grad_one, act_all, pre_all, hidden_all,
               ffn_all, branch_all, sums, bias_sums, wide_v, down_v, slope, in_sems):
        step = pl.program_id(0)
        width, heads, units = subnet(codes)
        features = (lane_row(D) < width).astype(F32)
        active = (lane_row(D) < heads).astype(F32)
        scale = 1.0 / width.astype(F32)
        loads = [pltpu.make_async_copy(wide.at[k], wide_v.at[k], in_sems.at[k]) for k in range(5)]
        loads += [pltpu.make_async_copy(down.at[k], down_v.at[k], in_sems.at[5 + k]) for k in range(4)]

        def ready(k):
            pl.when(step == 0)(loads[k].wait)

        @pl.when(step == 0)
        def _():
            for load in loads:
                load.start()
            sums[...] = jnp.zeros_like(sums)
            bias_sums[...] = jnp.zeros_like(bias_sums)

        def param(k):
            return small[k : k + 1, :]

        ready(0)
        resid = x0[...].astype(F32) + (dot(mixed[...], wide_v[0]) + param(2)) * features
        centered = (resid - row_sum(resid) * scale) * features
        inv_one = lax.rsqrt(row_sum(centered * centered) * scale + norm_eps)
        normed_one = centered * inv_one
        hidden = (normed_one * param(7) + param(4)) * features
        hidden_low = hidden.astype(LOW)
        hidden_all[...] = hidden_low
        branch = 0.0
        for j in range(4):
            ready(1 + j)
            unit_mask = (numbers[j : j + 1, :] < units).astype(F32)
            pre = (dot(hidden_low, wide_v[1 + j]) + bias[j : j + 1, :]) * unit_mask
            share, bell = normal_parts(pre)
            act = (pre * share).astype(LOW)
            act_all[j] = act
            slope[j] = (share + pre * bell * inv_root_tau) * unit_mask
            ready(5 + j)
            branch += dot(act, down_v[j])
        resid = hidden + (branch + param(3)) * features
        centered = (resid - row_sum(resid) * scale) * features
        inv_two = lax.rsqrt(row_sum(centered * centered) * scale + norm_eps)
        normed_two = centered * inv_two
        live = key_side[:, 6:7].astype(F32)
        out[...] = ((normed_two * param(8) + param(5)) * features * live).astype(LOW)
        grad_out = cotangent[...].astype(F32) * live
        grad_n = grad_out * (param(8) * features)
        grad_two = inv_two * features * (grad_n - row_sum(grad_n) * scale - normed_two * (row_sum(grad_n * normed_two) * scale))
        grad_ffn = grad_two.astype(LOW)
        ffn_all[...] = grad_ffn
        back = 0.0
        for j in range(4):
            grad_pre = (dot(grad_ffn, down_v[j], NT) * slope[j]).astype(LOW)
            pre_all[j] = grad_pre
            bias_sums[j : j + 1, :] += col_sum(grad_pre.astype(F32))
            back += dot(grad_pre, wide_v[1 + j], NT)
        grad_hidden = grad_two + back * features
        grad_n = grad_hidden * (param(7) * features)
        grad_res = inv_one * features * (grad_n - row_sum(grad_n) * scale - normed_one * (row_sum(grad_n * normed_one) * scale))
        grad_one[...] = grad_res
        grad_branch = grad_res.astype(LOW)
        branch_all[...] = grad_branch
        grad_mixed[...] = (dot(grad_branch, wide_v[0], NT) * active).astype(LOW)
        sums[0:1, :] += col_sum(grad_branch.astype(F32))
        sums[1:2, :] += col_sum(grad_ffn.astype(F32))
        sums[2:3, :] += col_sum(grad_hidden) * features
        sums[3:4, :] += col_sum(grad_out) * features
        sums[4:5, :] += col_sum(grad_hidden * normed_one)
        sums[5:6, :] += col_sum(grad_out * normed_two)

    block = pl.BlockSpec((size, D), lambda i: (i, 0))
    four = pl.BlockSpec((4, size, D), lambda i: (0, i, 0))
    shape = jax.ShapeDtypeStruct
    return pl.pallas_call(
        kernel,
        grid=(steps,),
        in_specs=[SM, block, block, block, pl.BlockSpec((size, 128), lambda i: (i, 0)), HBM, HBM]
        + [pl.BlockSpec((16, D), lambda i: (0, 0)), pl.BlockSpec((4, D), lambda i: (0, 0)), pl.BlockSpec((4, D), lambda i: (0, 0))],
        out_specs=(block, block, block, four, four, block, block, block, pl.BlockSpec((8, D), lambda i: (0, 0)), pl.BlockSpec((4, D), lambda i: (0, 0))),
        out_shape=(
            shape((count, D), LOW),
            shape((count, D), LOW),
            shape((count, D), F32),
            shape((4, count, D), LOW),
            shape((4, count, D), LOW),
            shape((count, D), LOW),
            shape((count, D), LOW),
            shape((count, D), LOW),
            shape((8, D), F32),
            shape((4, D), F32),
        ),
        scratch_shapes=[
            pltpu.VMEM((5, D, D), LOW),
            pltpu.VMEM((4, D, D), LOW),
            pltpu.VMEM((4, size, D), F32),
            pltpu.SemaphoreType.DMA((9,)),
        ],
        compiler_params=pltpu.CompilerParams(vmem_limit_bytes=62 * MIB),
        name="middle",
    )(codes, mixed, x0, cotangent, key_side, wide, down, small, bias, numbers)


SUM_CROSS = [True, False, False, True, False, False, False, False, False, False, True, False, True, True]
SUM_EARLY = {
    0: [(0, 0)],
    1: [(1, 0)],
    2: [(2, 0), (0, 1)],
    3: [(3, 0), (1, 1)],
    4: [(4, 0), (2, 1)],
    5: [(5, 0), (3, 1)],
    6: [(6, 0), (4, 1), (0, 2)],
    7: [(7, 0), (5, 1), (1, 2)],
    8: [(8, 0), (6, 1)],
}
SUM_THEN = {
    0: [(7, 1), (8, 1), (3, 2), (2, 2)],
    1: [(0, 3), (1, 3)],
    2: [(2, 3), (4, 2)],
    3: [(3, 3)],
    4: [(6, 2)],
    5: [(1, 5), (9, 1), (4, 4)],
    6: [(5, 3), (2, 5), (7, 2)],
    7: [(6, 3), (4, 5)],
    9: [(9, 2), (10, 1), (8, 3), (7, 4)],
    10: [(0, 5), (5, 5), (3, 5), (6, 5)],
    11: [(9, 3), (8, 4)],
}
SUM_CHUNK = {
    0: [(9, 0), (1, 4), (5, 2), (4, 3), (2, 4)],
    1: [(10, 0), (8, 2), (0, 4), (5, 4), (3, 4), (7, 3), (6, 4)],
    2: [(11, 0), (12, 0), (10, 2), (7, 5), (9, 4)],
}
SUM_SMALL = [
    (13, 0), (8, 5),
]
SUM_LAST = [
    (11, 1), (9, 5), (12, 1), (13, 1), (12, 2), (10, 3), (11, 2), (13, 2), (10, 4), (12, 3),
    (11, 3), (13, 3), (10, 5), (12, 4), (13, 4), (12, 5), (11, 4), (13, 5), (11, 5),
]


def back(depth, groups, codes, proj, peaks, key_side, grad_mixed, mixed, x0, grad_one, chunks, sums, bias_sums, saved):
    count = mixed.shape[0]
    heads = HEADS // CHUNKS
    act, pre, hidden, ffn, branch = saved

    def weight_grads(mixed, act, pre, hidden, ffn, branch, lanes_v, left_v, right_v, loads, step):
        def fetch(k, source):
            return pltpu.make_async_copy(source, lanes_v.at[lax.rem(k, 2)], loads.at[lax.rem(k, 2)])

        right = pltpu.make_async_copy(ffn, right_v, loads.at[2])
        left = pltpu.make_async_copy(hidden, left_v, loads.at[3])
        last = pltpu.make_async_copy(branch, right_v, loads.at[2])
        fetch(0, act.at[0]).start()
        right.start()
        left.start()
        right.wait()

        @pl.loop(0, 4)
        def _(k):
            fetch(k, act.at[0]).wait()

            @pl.when(k < 3)
            def _():
                fetch(k + 1, act.at[k + 1]).start()

            @pl.when(k == 3)
            def _():
                fetch(0, pre.at[0]).start()

            step(k, dot(lanes_v[lax.rem(k, 2)], right_v[...], TN))

        left.wait()
        last.start()

        @pl.loop(0, 4)
        def _(k):
            fetch(k, pre.at[0]).wait()

            @pl.when(k < 3)
            def _():
                fetch(k + 1, pre.at[k + 1]).start()

            step(4 + k, dot(left_v[...], lanes_v[lax.rem(k, 2)], TN))

        last.wait()
        step(8, dot(mixed[...], right_v[...], TN))

    def body(codes, proj, peaks, key_side, grad_mixed, mixed, x0, grad_one, chunks, sums, bias_sums, act, pre, hidden, ffn, branch, frames_grad,
             proj_v, peaks_v, weight_v, grad_proj, left_v, inner, grad_query, total, rows_v, small_v, loads, step, put, actions, chunk_done):
        width, _, _ = subnet(codes)
        features = (lane_row(D) < width).astype(F32)
        one = pltpu.make_async_copy(grad_one, total, loads.at[6])
        out = pltpu.make_async_copy(total, frames_grad, loads.at[7])

        def fetch(j):
            slot = lax.rem(j, 2)
            return [
                pltpu.make_async_copy(proj.at[j], proj_v.at[slot], loads.at[slot]),
                pltpu.make_async_copy(peaks.at[pl.ds(j * heads, heads)], peaks_v.at[slot], loads.at[2 + slot]),
                pltpu.make_async_copy(chunks.at[j], weight_v.at[slot], loads.at[4 + slot]),
            ]

        one.start()
        rows_v[...] = jnp.zeros_like(rows_v)
        rows_v[2:6, :] = sums[0:4, :]
        rows_v[7:9, :] = sums[4:6, :]
        small_v[...] = jnp.zeros_like(small_v)
        for row, at, col in bias_places(groups):
            small_v[row : row + 1, 128 : 128 + D // groups] = bias_sums[at : at + 1, col : col + D // groups]

        weight_grads(mixed, act, pre, hidden, ffn, branch, proj_v, left_v, grad_proj, loads, step)
        for copy in fetch(0):
            copy.start()

        @pl.loop(0, CHUNKS)
        def _(j):
            slot = lax.rem(j, 2)
            for copy in fetch(j):
                copy.wait()

            @pl.when(j + 1 < CHUNKS)
            def _():
                for copy in fetch(j + 1):
                    copy.start()

            attend_back(proj_v.at[slot], j, peaks_v.at[slot], key_side, grad_mixed, mixed, grad_proj, inner, grad_query, actions)
            cols = pl.ds(pl.multiple_of(j * CHUNK, CHUNK), CHUNK)
            masked = key_side[:, 7:8].astype(F32)
            grads = grad_proj[...].astype(F32)
            totals = col_sum(grads)
            rows_v[0:1, cols] = totals[:, :CHUNK]
            rows_v[1:2, cols] = totals[:, 2 * CHUNK :]
            put(j, dot(x0[...], grad_proj[...], TN).astype(LOW))
            chunk_done(j)

            @pl.when(j == 0)
            def _():
                one.wait()
                rows_v[6:7, :] = col_sum(total[...] * masked)

            rows_v[16:24, :] = jnp.zeros((8, D), F32)
            for k, part in enumerate(split3(col_sum(grads * masked))):
                rows_v[16 + k : 17 + k, :] = part
            spread = dot(rows_v[16:32, :].astype(LOW), flat(weight_v[slot]), NT)
            rows_v[6:7, :] += col_sum(spread) * features

            @pl.when(j + 1 < CHUNKS)
            def _():
                total[...] += dot(grad_proj[...], flat(weight_v[slot]), NT) * features

        small_v[:, :128] = rows_v[...].T
        put(None, small_v[...])
        chunk_done(None)
        total[...] += dot(grad_proj[...], flat(weight_v[(CHUNKS - 1) % 2]), NT) * features
        out.start()
        return out

    shape = jax.ShapeDtypeStruct
    operands = (codes, proj, peaks, key_side, grad_mixed, mixed, x0, grad_one, chunks, sums, bias_sums, act, pre, hidden, ffn, branch)
    in_specs = [SM, HBM, HBM, VM, VM, VM, VM, HBM, HBM, VM, VM] + [HBM] * 5

    def scratch(weight_shape):
        return [
            pltpu.VMEM((2, count, D), LOW),
            pltpu.VMEM((2, heads, count, 128), LOW),
            pltpu.VMEM((2,) + weight_shape, LOW),
            pltpu.VMEM((count, D), LOW),
            pltpu.VMEM((count, D), LOW),
            pltpu.VMEM((2, count, 128), LOW),
            pltpu.VMEM((count, 128), F32),
            pltpu.VMEM((count, D), F32),
            pltpu.VMEM((128, D), F32),
            pltpu.VMEM((D, SMALL), F32),
            pltpu.SemaphoreType.DMA((8,)),
        ]

    if not depth:

        def plain(*refs):
            inputs, parts, small, weight_parts, rest = refs[:17], refs[17], refs[18], refs[19], refs[20:]

            def step(k, value):
                weight_parts[k] = value.astype(LOW)

            def put(j, value):
                if j is None:
                    small[...] = value
                else:
                    parts[j] = value

            body(*inputs, *rest, step, put, {}, lambda j: None).wait()

        return pl.pallas_call(
            plain,
            out_shape=(shape((count, D), F32), shape((CHUNKS, D, D), LOW), shape((D, SMALL), F32), shape((9, D, D), LOW)),
            in_specs=in_specs,
            out_specs=(HBM, VM, VM, VM),
            scratch_shapes=scratch((D, D)),
            compiler_params=pltpu.CompilerParams(vmem_limit_bytes=62 * MIB),
            name="back_plain",
        )(*operands)

    rows, tall = D // groups, FF // groups
    sizes = [(rows, D)] * 11 + [(rows, D - SMALL), (rows, SMALL), (rows, SMALL)]
    rooms = [reduce_room(depth, *size, cross) for size, cross in zip(sizes, SUM_CROSS)]
    starts = [sum(len(room) for room in rooms[:k]) for k in range(len(rooms) + 1)]

    def fused(*refs):
        inputs, chunk_own, wide_own, down_own, small_own = refs[:17], *refs[17:21]
        inside, (send, recv, ring, chunk_part, small_part), rest = refs[21:32], refs[32:37], refs[37:]
        room_refs, finals = rest[: starts[-1]], rest[starts[-1] :]
        here = Place(depth)
        c = here.c
        copies = Copies(send, recv)
        plans = []

        def plan(sibling, kept):
            k = len(plans)
            plans.append(reduce_part(here, copies, sibling, kept, room_refs[starts[k] : starts[k + 1]], finals[k], sizes[k][1], SUM_CROSS[k]))

        for k in range(9):
            plan(ring.at[k % 3, :, :, 1 - c], lambda zz, xx, k=k: ring[k % 3, zz, xx, c])
        for k in range(2):
            plan(chunk_part.at[k, :, :, 1 - c], lambda zz, xx, k=k: chunk_part[k, zz, xx, c])
        for cut in (pl.ds(0, D - SMALL), pl.ds(D - SMALL, SMALL)):
            plan(chunk_part.at[2, :, :, 1 - c, :, cut], lambda zz, xx, cut=cut: chunk_part[2, zz, xx, c, :, cut])
        plan(small_part.at[:, :, 1 - c], lambda zz, xx: small_part[zz, xx, c])
        def step(k, value):
            hook(k, {at: plans[at - 3][6] for at in range(3, 9)})
            ring[lax.rem(k, 3)] = value.astype(LOW).reshape(depth, 2, 2, rows, D)
            hook(k, {at: functools.partial(run, plans, todo) for at, todo in SUM_EARLY.items()})

        def put(j, value):
            if j is None:
                small_part[...] = value.astype(LOW).reshape(depth, 2, 2, rows, SMALL)
            else:
                chunk_part[j] = value.reshape(depth, 2, 2, rows, D)

        here.greet()
        actions = {k: functools.partial(run, plans, todo) for k, todo in SUM_THEN.items()}

        def chunk_done(j):
            if j is None:
                run(plans, SUM_SMALL)
            else:
                hook(j, {k: functools.partial(run, plans, todo) for k, todo in SUM_CHUNK.items()})

        out = body(*inputs, *inside, step, put, actions, chunk_done)
        run(plans, SUM_LAST)
        for k in range(4):
            down_own[k * rows : (k + 1) * rows, :] = finals[k][...]
            wide_own[1 + k] = finals[4 + k][...]
        wide_own[0] = finals[8][...]
        for k in range(2):
            chunk_own[k] = finals[9 + k][...]
        chunk_own[2, :, : D - SMALL] = finals[11][...]
        chunk_own[2, :, D - SMALL :] = finals[12][...]
        small_own[...] = finals[13][...]
        out.wait()
        copies.finish()

    copies = reduce_copies(depth) * len(sizes)
    return pl.pallas_call(
        fused,
        out_shape=(
            shape((count, D), F32),
            shape((CHUNKS, rows, D), LOW),
            shape((5, rows, D), LOW),
            shape((tall, D), LOW),
            shape((rows, SMALL), LOW),
        ),
        in_specs=in_specs,
        out_specs=(HBM,) + (VM,) * 4,
        scratch_shapes=scratch((depth, 2, 2, rows, D))
        + [
            pltpu.SemaphoreType.DMA((copies,)),
            pltpu.SemaphoreType.DMA((copies,)),
            pltpu.VMEM((3, depth, 2, 2, rows, D), LOW),
            pltpu.VMEM((CHUNKS, depth, 2, 2, rows, D), LOW),
            pltpu.VMEM((depth, 2, 2, rows, SMALL), LOW),
        ]
        + [ref for room in rooms for ref in room]
        + [pltpu.VMEM(size, LOW) for size in sizes],
        compiler_params=pltpu.CompilerParams(collective_id=1, has_side_effects=True, vmem_limit_bytes=62 * MIB),
        name="back",
    )(*operands)


def finish(total, key_side, chunk_own, wide_own, down_own, small_own):
    count, (_, rows, _), tall = total.shape[0], chunk_own.shape, down_own.shape[0]
    size = count // 4

    def kernel(total, key_side, chunk_own, wide_own, down_own, small_own,
               frames_grad, qkv_grad, out_grad, in_grad, down_grad, bias_grad, gains_grad, shifts_grad, square, in_v):
        frames_grad[...] = total[...] * (1.0 - key_side[:, 7:8].astype(F32))

        @pl.when(pl.program_id(0) == 0)
        def _():
            for j in range(CHUNKS):
                for k in range(3):
                    piece = chunk_own[j, :, k * CHUNK : (k + 1) * CHUNK]
                    qkv_grad[:, k * D + j * CHUNK : k * D + (j + 1) * CHUNK] = piece.astype(F32)
            out_grad[...] = wide_own[0].astype(F32)
            for k in range(4):
                in_v[k] = wide_own[1 + k].astype(F32)
            for k, col, unit in unit_pieces(D // rows):
                in_grad[:, unit : unit + rows] = in_v[k, :, col : col + rows]
            down_grad[...] = down_own[...].astype(F32)
            table = small_own[...].astype(F32)
            square[...] = jnp.zeros_like(square)
            square[0:rows, :] = table[:, :128]
            turned = square[...].T
            shifts_grad[...] = turned[0:7, 0:rows]
            gains_grad[...] = turned[7:9, 0:rows]
            for k in range(4):
                bias_grad[:, k * rows : (k + 1) * rows] = table[k : k + 1, 128 : 128 + rows]

    def whole(*dims):
        return pl.BlockSpec(dims, lambda i: (0,) * len(dims))

    block = pl.BlockSpec((size, D), lambda i: (i, 0))
    outs = [(rows, 3 * D), (rows, D), (rows, FF), (tall, D), (1, tall), (2, rows), (7, rows)]
    return pl.pallas_call(
        kernel,
        grid=(4,),
        in_specs=[block, pl.BlockSpec((size, 128), lambda i: (i, 0))]
        + [whole(*part.shape) for part in (chunk_own, wide_own, down_own, small_own)],
        out_specs=(block,) + tuple(whole(*dims) for dims in outs),
        out_shape=(jax.ShapeDtypeStruct((count, D), F32),) + tuple(jax.ShapeDtypeStruct(dims, F32) for dims in outs),
        scratch_shapes=[pltpu.VMEM((128, 128), F32), pltpu.VMEM((4, rows, D), F32)],
        name="finish",
    )(total, key_side, chunk_own, wide_own, down_own, small_own)


def on_device(dp_size, frames, lengths, mask_starts, width_code, head_code, ffn_code, qkv_weight, out_weight, ffn_in_weight,
              ffn_out_weight, ffn_bias, norm_gains, shifts, cotangent):
    rows, tall = qkv_weight.shape[0], ffn_out_weight.shape[0]
    groups = D // rows
    fused = rows % 16 == 0 and groups % 4 == 0 and dp_size % 2 == 0
    depth = groups // 4 if fused else 0
    codes = jnp.concatenate([width_code, head_code, ffn_code])
    starts = mask_starts.reshape(frames.shape[0] // 128, 128)
    if fused:
        masters = (qkv_weight, out_weight, ffn_in_weight, ffn_out_weight, ffn_bias.reshape(1, tall), norm_gains.T, shifts.T)
        found = front(depth, groups, codes, lengths, starts, frames, masters)
        proj, x0, mixed, peaks, key_side, small, bias, chunks, wide, down = found
    else:
        spread = jnp.zeros((rows, 128), F32).at[:4, :rows].set(ffn_bias.reshape(4, rows))
        head = jnp.concatenate([shifts, norm_gains, jnp.zeros((rows, 119), F32), spread], axis=1).astype(LOW)
        chunks = jnp.stack([jnp.concatenate(chunk_cols(qkv_weight, j), axis=1) for j in range(CHUNKS)]).astype(LOW)
        blocks = ffn_in_weight.reshape(rows, groups, 4, rows).transpose(2, 0, 1, 3).reshape(4, rows, D)
        wide = jnp.concatenate([out_weight[None], blocks]).astype(LOW)
        head = lax.all_gather(head, "group", axis=0, tiled=True)
        chunks = lax.all_gather(chunks, "group", axis=1, tiled=True)
        wide = lax.all_gather(wide, "group", axis=1, tiled=True)
        down = lax.all_gather(ffn_out_weight.astype(LOW).reshape(4, rows, D), "group", axis=1, tiled=True)
        proj, x0, mixed, peaks, key_side, small, bias = front(0, groups, codes, lengths, starts, frames, (head, chunks))
    layer_out, grad_mixed, grad_one, *saved, sums, bias_sums = middle(
        groups, codes, mixed, x0, cotangent, key_side, wide.reshape(5, D, D), down.reshape(4, D, D), small, bias
    )
    shared = (codes, proj, peaks, key_side, grad_mixed, mixed, x0, grad_one, chunks, sums, bias_sums, saved)
    if fused:
        total, *owned = back(depth, groups, *shared)
        if dp_size > 2:
            owned = [0.5 * lax.psum(part, "dp") for part in owned]
    else:
        total, chunk_parts, small_part, weight_parts = back(0, groups, *shared)
        wide_part, down_part = weight_parts[jnp.array([8, 4, 5, 6, 7])], weight_parts[:4]
        owned = [
            lax.psum_scatter(chunk_parts.astype(F32), "group", scatter_dimension=1, tiled=True),
            lax.psum_scatter(wide_part.astype(F32), "group", scatter_dimension=1, tiled=True),
            lax.psum_scatter(down_part.astype(F32), "group", scatter_dimension=1, tiled=True).reshape(tall, D),
            lax.psum_scatter(small_part, "group", scatter_dimension=0, tiled=True),
        ]
        owned = [lax.psum(part.astype(LOW), "dp") for part in owned]
    frames_grad, qkv_grad, out_grad, ffn_in_grad, ffn_out_grad, bias_row, gains_rows, shifts_rows = finish(total, key_side, *owned)
    return (layer_out, frames_grad, qkv_grad, out_grad, ffn_in_grad, ffn_out_grad, bias_row.reshape(tall, 1), gains_rows.T, shifts_rows.T)


def solution(mesh):
    by_all, by_group = P(("group", "dp"), None), P("group", None)
    placed = (by_all, by_all, P(("group", "dp")), P("group"), P("group"), P("group")) + (by_group,) * 7 + (by_all,)
    return jax.shard_map(
        functools.partial(on_device, mesh.shape["dp"]),
        mesh=mesh,
        in_specs=placed,
        out_specs=(by_all, by_all) + (by_group,) * 7,
        check_vma=False,
    )
```

```python
import functools

import jax
import jax.numpy as jnp
from jax import lax
from jax.experimental import pallas as pl
from jax.experimental.pallas import tpu as pltpu
from jax.sharding import PartitionSpec as P

D = 768
HEADS = 12
FF = 3072
SPAN = 10
CHUNKS = 3
CHUNK = D // CHUNKS
CHUNK_PAIRS = HEADS // (2 * CHUNKS)
SMALL = 256
BLOCK = 512

norm_eps = 1e-05
far_score = -float(2**30)
root_half = 0.7071067811865476
inv_root_tau = 0.3989422804014327

F32, LOW = jnp.float32, jnp.bfloat16
NN = (((1,), (0,)), ((), ()))
NT = (((1,), (1,)), ((), ()))
TN = (((0,), (0,)), ((), ()))
MESH = pl.DeviceIdType.MESH
MIB = 2**20


def dot(a, b, dims=NN):
    return lax.dot_general(a, b, dims, preferred_element_type=F32)


def lane_row(n):
    return lax.broadcasted_iota(jnp.int32, (1, n), 1)


def row_sum(v):
    return jnp.sum(v, axis=1, keepdims=True)


def col_sum(v):
    return jnp.sum(v, axis=0, keepdims=True)


def subnet(codes):
    width = (D // 6) * (4 + codes[0])
    return width, (HEADS - HEADS // 3 + codes[1]) * (D // HEADS), (width * (6 + codes[2])) // 2


def bias_places(groups):
    rows = D // groups
    for group in range(groups):
        for k in range(4):
            yield group * rows + k, k, group * rows


def unit_pieces(groups):
    rows = D // groups
    for k in range(4):
        for group in range(groups):
            yield k, group * rows, group * 4 * rows + k * rows


class Place:
    def __init__(self, depth):
        group, dp = lax.axis_index("group"), lax.axis_index("dp")
        self.depth = depth
        self.z, self.x, self.c, self.y = group // 4, (group // 2) % 2, group % 2, dp % 2
        self.dp = dp
        self.core_dev = (group + 1 - 2 * self.c, dp)
        self.x_dev = (group + 2 - 4 * self.x, dp)
        self.y_dev = (group, dp + 1 - 2 * self.y)

    def z_at(self, step):
        return lax.rem(self.z + step, self.depth)

    def z_from(self, step):
        return lax.rem(self.z - step + self.depth, self.depth)

    def z_dev(self, step):
        return ((self.z_at(step) * 2 + self.x) * 2 + self.c, self.dp)

    def greet(self):
        barrier = pltpu.get_barrier_semaphore()
        devs = [self.core_dev, self.x_dev, self.y_dev] + [self.z_dev(s) for s in range(1, self.depth)]
        for dev in devs:
            pl.semaphore_signal(barrier, inc=1, device_id=dev, device_id_type=MESH)
        pl.semaphore_wait(barrier, len(devs))


class Copies:
    def __init__(self, send_sems, recv_sems):
        self.send_sems, self.recv_sems, self.made, self.left = send_sems, recv_sems, [], set()

    def to(self, src, dst, dev):
        spot = len(self.made)
        copy = pltpu.make_async_remote_copy(
            src_ref=src,
            dst_ref=dst,
            send_sem=self.send_sems.at[spot],
            recv_sem=self.recv_sems.at[spot],
            device_id=dev,
            device_id_type=MESH,
        )
        self.made.append(copy)
        return copy

    def sent(self, copy):
        self.left.update(spot for spot, made in enumerate(self.made) if made is copy)
        copy.wait_send()

    def finish(self):
        for spot, copy in enumerate(self.made):
            if spot not in self.left:
                copy.wait_send()


def halves(width, y):
    half = width // 2
    mine = pl.ds(pl.multiple_of(y * half, 128), half)
    other = pl.ds(pl.multiple_of((1 - y) * half, 128), half)
    return mine, other


def gather_cross(here, copies, own, at, keep, width):
    z, x, c = here.z, here.x, here.c
    mine, other = halves(width, here.y)
    every = slice(None)
    steps = range(1, here.depth)

    def same(zz, xx, cols, dev):
        return copies.to(at(zz, xx, c, cols), at(zz, xx, c, cols), dev)

    first = copies.to(own(mine), at(z, x, c, mine), here.x_dev)
    own_z = [copies.to(own(mine), at(z, x, c, mine), here.z_dev(s)) for s in steps]
    side_z = [same(z, 1 - x, mine, here.z_dev(s)) for s in steps]
    side_y = same(z, 1 - x, mine, here.y_dev)
    far_y = [same(here.z_from(s), every, mine, here.y_dev) for s in steps]
    core = [same(every, every, cols, here.core_dev) for cols in (mine, other)]

    def stage0():
        keep.start()
        first.start()
        for copy in own_z:
            copy.start()

    def stage1():
        first.wait_recv()
        for copy in side_z:
            copy.start()
        side_y.start()

    def stage2():
        for k in range(len(own_z)):
            own_z[k].wait_recv()
            side_z[k].wait_recv()
            far_y[k].start()
        keep.wait()
        core[0].start()

    def stage3():
        for copy in [side_y] + far_y:
            copy.wait_recv()
        core[1].start()

    def stage4():
        for copy in core:
            copy.wait_recv()

    return [stage0, stage1, stage2, stage3, stage4]


def gather_line(here, copies, own, at, keep, width):
    z, x, c = here.z, here.x, here.c
    mine, other = halves(width, here.y)
    every = slice(None)
    steps = range(1, here.depth)

    def same(zz, xx, cols, dev):
        return copies.to(at(zz, xx, c, cols), at(zz, xx, c, cols), dev)

    own_z = [copies.to(own(mine), at(z, x, c, mine), here.z_dev(s)) for s in steps]
    own_x = copies.to(own(every), at(z, x, c, every), here.x_dev)
    froms = [here.z_from(s) for s in steps]
    y_hops = [same(zz, x, mine, here.y_dev) for zz in froms]
    x_mine = [same(zz, x, mine, here.x_dev) for zz in froms]
    x_other = [same(zz, x, other, here.x_dev) for zz in froms]
    core = [same(every, xx, every, here.core_dev) for xx in (x, 1 - x)]

    def stage0():
        keep.start()
        for copy in own_z:
            copy.start()
        own_x.start()

    def stage1():
        for k in range(len(own_z)):
            own_z[k].wait_recv()
            y_hops[k].start()
            x_mine[k].start()

    def stage2():
        for k in range(len(own_z)):
            y_hops[k].wait_recv()
            x_other[k].start()
        keep.wait()
        core[0].start()

    def stage3():
        for copy in [own_x] + x_mine + x_other:
            copy.wait_recv()
        core[1].start()

    def stage4():
        for copy in core:
            copy.wait_recv()

    return [stage0, stage1, stage2, stage3, stage4]


def gather_cross_copies(depth):
    return 4 + 3 * (depth - 1)


def gather_line_copies(depth):
    return 3 + 4 * (depth - 1)


def plus(a, b):
    return a + b


def reduce_part(here, copies, sibling, kept, room, final, width, cross):
    z, x, depth = here.z, here.x, here.depth
    mine, other = halves(width, here.y)
    steps = range(1, depth)
    if cross:
        first, second, third, fourth, fifth = room
        core = copies.to(sibling, first, here.core_dev)
        to_y = copies.to(first.at[:, :, :, other], second, here.y_dev)
        to_z = [copies.to(second.at[here.z_at(s)], third.at[s - 1], here.z_dev(s)) for s in steps]
        to_x = copies.to(fourth.at[1 - x], fifth, here.x_dev)
    else:
        first, second, third, fourth = room
        core = copies.to(sibling, first, here.core_dev)
        to_x = copies.to(first.at[:, 1 - x], second, here.x_dev)
        to_y = copies.to(second.at[:, :, other], third, here.y_dev)
        to_z = [copies.to(third.at[here.z_at(s)], fourth.at[s - 1], here.z_dev(s)) for s in steps]
    back = copies.to(final.at[:, mine], final.at[:, mine], here.y_dev)

    def stage0():
        core.start()

    def stage1():
        core.wait_recv()

        @pl.loop(0, depth)
        def _(zz):
            for xx in range(2):
                first[zz, xx] = plus(kept(zz, xx), first[zz, xx])

        if cross:
            to_y.start()
        else:
            to_x.start()

    def stage2():
        if cross:
            to_y.wait_recv()

            @pl.loop(0, depth)
            def _(zz):
                for xx in range(2):
                    second[zz, xx] = plus(first[zz, xx, :, mine], second[zz, xx])

            for copy in to_z:
                copy.start()
        else:
            to_x.wait_recv()

            @pl.loop(0, depth)
            def _(zz):
                second[zz] = plus(first[zz, x], second[zz])

            to_y.start()

    def stage3():
        if cross:
            for copy in to_z:
                copy.wait_recv()

            @pl.loop(0, 2)
            def _(xx):
                total = second[z, xx].astype(F32)
                for s in steps:
                    total += third[s - 1, xx].astype(F32)
                fourth[xx] = total.astype(LOW)

            to_x.start()
        else:
            to_y.wait_recv()

            @pl.loop(0, depth)
            def _(zz):
                third[zz] = plus(second[zz, :, mine], third[zz])

            for copy in to_z:
                copy.start()

    def stage4():
        if cross:
            to_x.wait_recv()
            final[:, mine] = plus(fourth[x], fifth[...])
        else:
            for copy in to_z:
                copy.wait_recv()
            total = third[z].astype(F32)
            for s in steps:
                total += fourth[s - 1].astype(F32)
            final[:, mine] = total.astype(LOW)
        back.start()

    def stage5():
        back.wait_recv()

    return [stage0, stage1, stage2, stage3, stage4, stage5, lambda: copies.sent(core)]


def reduce_room(depth, rows, width, cross):
    half = width // 2
    if cross:
        shapes = [(depth, 2, rows, width), (depth, 2, rows, half), (depth - 1, 2, rows, half), (2, rows, half), (rows, half)]
    else:
        shapes = [(depth, 2, rows, width), (depth, rows, width), (depth, rows, half), (depth - 1, rows, half)]
    return [pltpu.VMEM(shape, LOW) for shape in shapes]


def reduce_copies(depth):
    return 4 + depth - 1


def run(plans, todo):
    for plan, stage in todo:
        plans[plan][stage]()


def hook(at, actions):
    for k, action in actions.items():
        pl.when(at == k)(action)


def split3(v):
    high = v.astype(LOW).astype(F32)
    rest = v - high
    middle = rest.astype(LOW).astype(F32)
    return high, middle, rest - middle


def frame_tables(lengths, starts, frames, edge, query_side, key_side):
    lane = lane_row(128)
    place = lax.broadcasted_iota(jnp.int32, (frames, 1), 0)
    first, second = lengths[0, 0], lengths[0, 0] + lengths[0, 1]
    segment = (place >= first).astype(jnp.int32) + (place >= second).astype(jnp.int32)
    spread = jnp.broadcast_to(starts[...][:, None, :], (frames // 128, 128, 128)).reshape(frames, 128)
    start = jnp.max(jnp.where(lane == lax.rem(place, 128), spread, 0), axis=1, keepdims=True)
    edge[0:16, :] = jnp.full((16, 1), -1, jnp.int32)
    edge[pl.ds(16, frames), :] = jnp.where(start == 1, segment, -1)
    masked = segment < 0
    for offset in range(SPAN):
        masked = masked | (edge[pl.ds(16 - offset, frames), :] == segment)
    live = segment < 2
    masked = masked & live
    query_side[...] = jnp.where((lane < 3) & (lane != segment), far_score, 0.0).astype(LOW)
    ones = (lane == segment) | ((lane >= 3) & (lane < 6)) | ((lane == 6) & live) | ((lane == 7) & masked)
    key_side[...] = jnp.where(ones, 1.0, 0.0).astype(LOW)


def attend(proj, chunk, query_side, key_side, mixed, peaks, actions):
    frames = mixed.shape[0]
    blocks = frames // BLOCK
    lane = lane_row(128)

    @pl.loop(0, CHUNK_PAIRS)
    def _(part):
        pair = chunk * CHUNK_PAIRS + part
        col = pl.multiple_of(part * 128, 128)

        @pl.loop(0, blocks)
        def _(block):
            hook(pair * blocks + block, actions)
            rows = pl.ds(pl.multiple_of(block * BLOCK, BLOCK), BLOCK)
            query = proj[rows, pl.ds(col, 128)]
            keys = jnp.concatenate([proj[:, pl.ds(pl.multiple_of(CHUNK + col, 128), 128)], key_side[...]], axis=1)
            values = proj[:, pl.ds(pl.multiple_of(2 * CHUNK + col, 128), 128)]
            values = jnp.concatenate([values, jnp.ones((frames, 128), LOW)], axis=1)
            side = query_side[rows, :]
            found = []
            for h in range(2):
                own = jnp.where((lane < 64) == (h == 0), query, jnp.zeros_like(query))
                scores = dot(jnp.concatenate([own, side], axis=1), keys, NT)
                peak = jnp.max(scores, axis=1, keepdims=True)
                weights = jnp.exp(scores - peak).astype(LOW)
                sums = dot(weights, values)
                total = sums[:, 128:]
                high, middle, low = split3(-(peak + jnp.log(total)))
                table = jnp.where(lane == 3, high, jnp.where(lane == 4, middle, jnp.where(lane == 5, low, side.astype(F32))))
                peaks[2 * pair + h, rows, :] = table.astype(LOW)
                found.append(sums[:, :128] / total)
            mixed[rows, pl.ds(pl.multiple_of(pair * 128, 128), 128)] = jnp.where(lane < 64, found[0], found[1]).astype(LOW)


def attend_back(proj, chunk, peaks, key_side, grad_mixed, mixed, grad_proj, inner, grad_query, actions):
    frames = mixed.shape[0]
    blocks = frames // BLOCK
    lane = lane_row(128)

    @pl.loop(0, CHUNK_PAIRS)
    def _(part):
        pair = chunk * CHUNK_PAIRS + part
        all_col = pl.ds(pl.multiple_of(pair * 128, 128), 128)
        query_cols = pl.ds(pl.multiple_of(part * 128, 128), 128)
        key_cols = pl.ds(pl.multiple_of(CHUNK + part * 128, 128), 128)
        value_cols = pl.ds(pl.multiple_of(2 * CHUNK + part * 128, 128), 128)
        prod = grad_mixed[:, all_col].astype(F32) * mixed[:, all_col].astype(F32)
        for h in range(2):
            high, middle, low = split3(-row_sum(jnp.where((lane < 64) == (h == 0), prod, 0.0)))
            table = jnp.where(lane == 3, high, jnp.where(lane == 4, middle, jnp.where(lane == 5, low, 0.0)))
            inner[h] = table.astype(LOW)

        @pl.loop(0, blocks)
        def _(block):
            hook(pair * blocks + block, actions)
            rows = pl.ds(pl.multiple_of(block * BLOCK, BLOCK), BLOCK)
            key, value, side = proj[rows, key_cols], proj[rows, value_cols], key_side[rows, :]
            keys = jnp.concatenate([key, side], axis=1)
            values = jnp.concatenate([value, side], axis=1)
            query, grad = proj[:, query_cols], grad_mixed[:, all_col]
            grad_v = grad_k = grad_q = 0.0
            for h in range(2):
                own = (lane < 64) == (h == 0)
                query_h = jnp.where(own, query, jnp.zeros_like(query))
                grad_h = jnp.where(own, grad, jnp.zeros_like(grad))
                key_h = jnp.where(own, key, jnp.zeros_like(key))
                probs = jnp.exp(dot(keys, jnp.concatenate([query_h, peaks[2 * part + h]], axis=1), NT))
                shifted = dot(values, jnp.concatenate([grad_h, inner[h]], axis=1), NT)
                grad_s = (probs * shifted).astype(LOW)
                grad_v += dot(probs.astype(LOW), grad_h)
                grad_k += dot(grad_s, query_h)
                grad_q += dot(grad_s, key_h, TN)
            grad_proj[rows, key_cols] = grad_k.astype(LOW)
            grad_proj[rows, value_cols] = grad_v.astype(LOW)

            @pl.when(block == 0)
            def _():
                grad_query[...] = grad_q

            @pl.when(block > 0)
            def _():
                grad_query[...] += grad_q

        grad_proj[:, query_cols] = (grad_query[...] * 0.125).astype(LOW)


VM = pl.BlockSpec(memory_space=pltpu.VMEM)
SM = pl.BlockSpec(memory_space=pltpu.SMEM)
HBM = pl.BlockSpec(memory_space=pl.ANY)


def flat(value):
    return value.reshape(D, value.shape[-1])


def chunk_cols(matrix, j):
    return [matrix[:, k * D + j * CHUNK : k * D + (j + 1) * CHUNK] for k in range(3)]


GATHER_CROSS = [False, True, False, True, False, False, True, False]
GATHER_FIRST = [
    (3, 0), (0, 0), (1, 0), (2, 0), (3, 1), (5, 0), (1, 1), (0, 1), (7, 0), (0, 2),
    (2, 1), (3, 2), (4, 0), (2, 2), (0, 3), (3, 3), (5, 1), (6, 0), (0, 4), (3, 4),
]
GATHER_THEN = {
    0: [(1, 2)],
    1: [(2, 3), (5, 2)],
    3: [(2, 4), (6, 1), (1, 3), (7, 1)],
    4: [(5, 3), (4, 1)],
    6: [(5, 4)],
    7: [(7, 2)],
    8: [(6, 2), (4, 2)],
    11: [(7, 3)],
}
GATHER_CHUNK = {
    1: [(1, 4)],
}
GATHER_LAST = [
    (4, 3), (7, 4), (6, 3), (4, 4), (6, 4),
]


def front(depth, groups, codes, lengths, starts, frames, weights):
    count = frames.shape[0]

    def body(codes, lengths, starts, frames, small_full, chunks, proj, x0, mixed, peaks, key_side, small, bias, query_side, edge, proj_v, peaks_v, out_sems, early, enter, actions):
        width, heads, _ = subnet(codes)
        features = (lane_row(D) < width).astype(F32)
        frame_tables(lengths, starts, count, edge, query_side, key_side)
        early()
        table = flat(small_full[...]).astype(F32)
        small[...] = table[:, :128].T[0:16, :]
        for row, at, col in bias_places(groups):
            bias[at : at + 1, col : col + D // groups] = table[row : row + 1, 128 : 128 + D // groups]
        masked = key_side[:, 7:8].astype(F32)
        start = jnp.where(masked > 0, small[6:7, :], frames[...].astype(F32)) * features
        x0[...] = start.astype(LOW)

        @pl.loop(0, CHUNKS)
        def _(j):
            enter(j)
            cols = pl.ds(pl.multiple_of(j * CHUNK, CHUNK), CHUNK)
            active = (lane_row(CHUNK) + j * CHUNK < heads).astype(F32)
            value = dot(x0[...], flat(chunks[j]))
            for k in range(3):
                piece = value[:, k * CHUNK : (k + 1) * CHUNK]
                if k != 1:
                    piece = piece + small[k // 2 : k // 2 + 1, cols]
                piece = (piece * active).astype(LOW)
                proj_v[j, :, k * CHUNK : (k + 1) * CHUNK] = piece * jnp.asarray(0.125, LOW) if k == 0 else piece
            pltpu.make_async_copy(proj_v.at[j], proj.at[j], out_sems.at[j]).start()
            attend(proj_v.at[j], j, query_side, key_side, mixed, peaks_v, actions)
            quarter = pl.ds(j * (HEADS // CHUNKS), HEADS // CHUNKS)
            pltpu.make_async_copy(peaks_v.at[quarter], peaks.at[quarter], out_sems.at[CHUNKS + j]).start()

        def leave():
            for j in range(CHUNKS):
                pltpu.make_async_copy(proj_v.at[j], proj.at[j], out_sems.at[j]).wait()
                quarter = pl.ds(j * (HEADS // CHUNKS), HEADS // CHUNKS)
                pltpu.make_async_copy(peaks_v.at[quarter], peaks.at[quarter], out_sems.at[CHUNKS + j]).wait()

        return leave

    shape = jax.ShapeDtypeStruct
    found = (
        shape((CHUNKS, count, D), LOW),
        shape((count, D), LOW),
        shape((count, D), LOW),
        shape((HEADS, count, 128), LOW),
        shape((count, 128), LOW),
        shape((16, D), F32),
        shape((4, D), F32),
    )
    scratch = [
        pltpu.VMEM((count, 128), LOW),
        pltpu.VMEM((count + 16, 1), jnp.int32),
        pltpu.VMEM((CHUNKS, count, D), LOW),
        pltpu.VMEM((HEADS, count, 128), LOW),
        pltpu.SemaphoreType.DMA((2 * CHUNKS,)),
    ]
    places = (HBM, VM, VM, HBM, VM, VM, VM)
    params = dict(has_side_effects=True, vmem_limit_bytes=62 * MIB)
    if not depth:

        def plain(codes, lengths, starts, frames, head, chunks, *rest):
            body(codes, lengths, starts, frames, head, chunks, *rest, lambda: None, lambda j: None, {})()

        return pl.pallas_call(
            plain,
            out_shape=found,
            in_specs=[SM, SM, VM, VM, VM, VM],
            out_specs=places,
            scratch_shapes=scratch,
            compiler_params=pltpu.CompilerParams(vmem_limit_bytes=62 * MIB),
            name="front_plain",
        )(codes, lengths, starts, frames, *weights)

    rows = weights[0].shape[0]

    def fused(*refs):
        codes, lengths, starts, frames = refs[:4]
        qkv_own, out_own, in_own, down_own, bias_own, gains_own, shifts_own = refs[4:11]
        proj, x0, mixed, peaks, key_side, small, bias, chunks_out, wide, down = refs[11:21]
        query_side, edge, proj_v, peaks_v, out_sems, head, chunks = refs[21:28]
        pad, square, in_v, head_low, chunks_low, wide_low, down_low, send, recv, local = refs[28:]
        here = Place(depth)
        z, x, c = here.z, here.x, here.c
        copies = Copies(send, recv)

        def plan(k, own, full, width):
            gather = gather_cross if GATHER_CROSS[k] else gather_line
            keep = pltpu.make_async_copy(own(slice(None)), full(z, x, c, slice(None)), local.at[k])
            return gather(here, copies, own, full, keep, width)

        def chunk_plan(k):
            return plan(k, lambda cols: chunks_low.at[k, :, cols], lambda zz, xx, cc, cols: chunks.at[k, zz, xx, cc, :, cols], D)

        def blocks_plan(k, first, count, own, full):
            cut = pl.ds(first, count)
            return plan(k, lambda cols: own.at[cut, :, cols], lambda zz, xx, cc, cols: full.at[cut, zz, xx, cc, :, cols], D)

        plans = [chunk_plan(j) for j in range(CHUNKS)]
        plans.append(plan(3, lambda cols: head_low.at[:, cols], lambda zz, xx, cc, cols: head.at[zz, xx, cc, :, cols], SMALL))
        plans += [blocks_plan(4 + k, 2 * k, 2, down_low, down) for k in range(2)]
        plans += [blocks_plan(6 + k, 2 * k, 2 + k, wide_low, wide) for k in range(2)]
        square[...] = jnp.zeros_like(square)
        square[0:7, 0:rows] = shifts_own[...]
        square[7:9, 0:rows] = gains_own[...]
        pad[...] = jnp.zeros_like(pad)
        pad[:, :128] = square[...].T[:rows, :]
        for k in range(4):
            pad[k : k + 1, 128 : 128 + rows] = bias_own[:, k * rows : (k + 1) * rows]
        for j in range(CHUNKS):
            chunks_low[j] = jnp.concatenate(chunk_cols(qkv_own, j), axis=1).astype(LOW)
        head_low[...] = pad[...].astype(LOW)
        here.greet()

        def early():
            cut = min(k for k, (plan, _) in enumerate(GATHER_FIRST) if plan > 3)
            run(plans, GATHER_FIRST[:cut])
            wide_low[0] = out_own[...].astype(LOW)
            for k, col, unit in unit_pieces(groups):
                in_v[k, :, col : col + rows] = in_own[:, unit : unit + rows]
            for k in range(4):
                wide_low[1 + k] = in_v[k].astype(LOW)
                down_low[k] = down_own[k * rows : (k + 1) * rows, :].astype(LOW)
            run(plans, GATHER_FIRST[cut:])

        def enter(j):
            hook(j, {k: functools.partial(run, plans, todo) for k, todo in GATHER_CHUNK.items()})

        actions = {k: functools.partial(run, plans, todo) for k, todo in GATHER_THEN.items()}
        leave = body(codes, lengths, starts, frames, head, chunks, proj, x0, mixed, peaks, key_side, small, bias,
                     query_side, edge, proj_v, peaks_v, out_sems, early, enter, actions)
        pass_on = pltpu.make_async_copy(chunks, chunks_out, local.at[8])
        pass_on.start()
        run(plans, GATHER_LAST)
        pass_on.wait()
        leave()
        copies.finish()

    copies = sum(gather_cross_copies(depth) if cross else gather_line_copies(depth) for cross in GATHER_CROSS)
    return pl.pallas_call(
        fused,
        out_shape=found
        + (
            shape((CHUNKS, depth, 2, 2, rows, D), LOW),
            shape((5, depth, 2, 2, rows, D), LOW),
            shape((4, depth, 2, 2, rows, D), LOW),
        ),
        in_specs=[SM, SM] + [VM] * 9,
        out_specs=places + (HBM,) * 3,
        scratch_shapes=scratch
        + [
            pltpu.VMEM((depth, 2, 2, rows, SMALL), LOW),
            pltpu.VMEM((CHUNKS, depth, 2, 2, rows, D), LOW),
            pltpu.VMEM((rows, SMALL), F32),
            pltpu.VMEM((128, 128), F32),
            pltpu.VMEM((4, rows, D), F32),
            pltpu.VMEM((rows, SMALL), LOW),
            pltpu.VMEM((CHUNKS, rows, D), LOW),
            pltpu.VMEM((5, rows, D), LOW),
            pltpu.VMEM((4, rows, D), LOW),
            pltpu.SemaphoreType.DMA((copies,)),
            pltpu.SemaphoreType.DMA((copies,)),
            pltpu.SemaphoreType.DMA((9,)),
        ],
        compiler_params=pltpu.CompilerParams(collective_id=0, **params),
        name="front",
    )(codes, lengths, starts, frames, *weights)


def normal_parts(v):
    bell = jnp.exp(v * v * -0.5)
    t = 1.0 / (1.0 + (0.3275911 * root_half) * jnp.abs(v))
    tail = t * (0.127414796 + t * (-0.142248368 + t * (0.7107068705 + t * (-0.7265760135 + t * 0.5307027145)))) * bell
    return jnp.where(v < 0, tail, 1.0 - tail), bell


def middle(groups, codes, mixed, x0, cotangent, key_side, wide, down, small, bias):
    count = mixed.shape[0]
    size = BLOCK // 2
    steps = count // size
    numbers = jnp.arange(FF, dtype=jnp.int32).reshape(groups, 4, D // groups).transpose(1, 0, 2).reshape(4, D)

    def kernel(codes, mixed, x0, cotangent, key_side, wide, down, small, bias, numbers, out, grad_mixed, grad_one, act_all, pre_all, hidden_all,
               ffn_all, branch_all, sums, bias_sums, wide_v, down_v, slope, in_sems):
        step = pl.program_id(0)
        width, heads, units = subnet(codes)
        features = (lane_row(D) < width).astype(F32)
        active = (lane_row(D) < heads).astype(F32)
        scale = 1.0 / width.astype(F32)
        loads = [pltpu.make_async_copy(wide.at[k], wide_v.at[k], in_sems.at[k]) for k in range(5)]
        loads += [pltpu.make_async_copy(down.at[k], down_v.at[k], in_sems.at[5 + k]) for k in range(4)]

        def ready(k):
            pl.when(step == 0)(loads[k].wait)

        @pl.when(step == 0)
        def _():
            for load in loads:
                load.start()
            sums[...] = jnp.zeros_like(sums)
            bias_sums[...] = jnp.zeros_like(bias_sums)

        def param(k):
            return small[k : k + 1, :]

        ready(0)
        resid = x0[...].astype(F32) + (dot(mixed[...], wide_v[0]) + param(2)) * features
        centered = (resid - row_sum(resid) * scale) * features
        inv_one = lax.rsqrt(row_sum(centered * centered) * scale + norm_eps)
        normed_one = centered * inv_one
        hidden = (normed_one * param(7) + param(4)) * features
        hidden_low = hidden.astype(LOW)
        hidden_all[...] = hidden_low
        branch = 0.0
        for j in range(4):
            ready(1 + j)
            unit_mask = (numbers[j : j + 1, :] < units).astype(F32)
            pre = (dot(hidden_low, wide_v[1 + j]) + bias[j : j + 1, :]) * unit_mask
            share, bell = normal_parts(pre)
            act = (pre * share).astype(LOW)
            act_all[j] = act
            slope[j] = (share + pre * bell * inv_root_tau) * unit_mask
            ready(5 + j)
            branch += dot(act, down_v[j])
        resid = hidden + (branch + param(3)) * features
        centered = (resid - row_sum(resid) * scale) * features
        inv_two = lax.rsqrt(row_sum(centered * centered) * scale + norm_eps)
        normed_two = centered * inv_two
        live = key_side[:, 6:7].astype(F32)
        out[...] = ((normed_two * param(8) + param(5)) * features * live).astype(LOW)
        grad_out = cotangent[...].astype(F32) * live
        grad_n = grad_out * (param(8) * features)
        grad_two = inv_two * features * (grad_n - row_sum(grad_n) * scale - normed_two * (row_sum(grad_n * normed_two) * scale))
        grad_ffn = grad_two.astype(LOW)
        ffn_all[...] = grad_ffn
        back = 0.0
        for j in range(4):
            grad_pre = (dot(grad_ffn, down_v[j], NT) * slope[j]).astype(LOW)
            pre_all[j] = grad_pre
            bias_sums[j : j + 1, :] += col_sum(grad_pre.astype(F32))
            back += dot(grad_pre, wide_v[1 + j], NT)
        grad_hidden = grad_two + back * features
        grad_n = grad_hidden * (param(7) * features)
        grad_res = inv_one * features * (grad_n - row_sum(grad_n) * scale - normed_one * (row_sum(grad_n * normed_one) * scale))
        grad_one[...] = grad_res
        grad_branch = grad_res.astype(LOW)
        branch_all[...] = grad_branch
        grad_mixed[...] = (dot(grad_branch, wide_v[0], NT) * active).astype(LOW)
        sums[0:1, :] += col_sum(grad_branch.astype(F32))
        sums[1:2, :] += col_sum(grad_ffn.astype(F32))
        sums[2:3, :] += col_sum(grad_hidden) * features
        sums[3:4, :] += col_sum(grad_out) * features
        sums[4:5, :] += col_sum(grad_hidden * normed_one)
        sums[5:6, :] += col_sum(grad_out * normed_two)

    block = pl.BlockSpec((size, D), lambda i: (i, 0))
    four = pl.BlockSpec((4, size, D), lambda i: (0, i, 0))
    shape = jax.ShapeDtypeStruct
    return pl.pallas_call(
        kernel,
        grid=(steps,),
        in_specs=[SM, block, block, block, pl.BlockSpec((size, 128), lambda i: (i, 0)), HBM, HBM]
        + [pl.BlockSpec((16, D), lambda i: (0, 0)), pl.BlockSpec((4, D), lambda i: (0, 0)), pl.BlockSpec((4, D), lambda i: (0, 0))],
        out_specs=(block, block, block, four, four, block, block, block, pl.BlockSpec((8, D), lambda i: (0, 0)), pl.BlockSpec((4, D), lambda i: (0, 0))),
        out_shape=(
            shape((count, D), LOW),
            shape((count, D), LOW),
            shape((count, D), F32),
            shape((4, count, D), LOW),
            shape((4, count, D), LOW),
            shape((count, D), LOW),
            shape((count, D), LOW),
            shape((count, D), LOW),
            shape((8, D), F32),
            shape((4, D), F32),
        ),
        scratch_shapes=[
            pltpu.VMEM((5, D, D), LOW),
            pltpu.VMEM((4, D, D), LOW),
            pltpu.VMEM((4, size, D), F32),
            pltpu.SemaphoreType.DMA((9,)),
        ],
        compiler_params=pltpu.CompilerParams(vmem_limit_bytes=62 * MIB),
        name="middle",
    )(codes, mixed, x0, cotangent, key_side, wide, down, small, bias, numbers)


SUM_CROSS = [True, False, False, True, False, False, False, False, False, False, True, False, True, True]
SUM_EARLY = {
    0: [(0, 0)],
    1: [(1, 0)],
    2: [(2, 0), (0, 1)],
    3: [(3, 0), (1, 1)],
    4: [(4, 0), (2, 1)],
    5: [(5, 0), (3, 1)],
    6: [(6, 0), (4, 1), (0, 2)],
    7: [(7, 0), (5, 1), (1, 2)],
    8: [(8, 0), (6, 1)],
}
SUM_THEN = {
    0: [(7, 1), (8, 1), (3, 2), (2, 2)],
    1: [(0, 3), (1, 3)],
    2: [(2, 3), (4, 2)],
    3: [(3, 3)],
    4: [(6, 2)],
    5: [(1, 5), (9, 1), (4, 4)],
    6: [(5, 3), (2, 5), (7, 2)],
    7: [(6, 3), (4, 5)],
    9: [(9, 2), (10, 1), (8, 3), (7, 4)],
    10: [(0, 5), (5, 5), (3, 5), (6, 5)],
    11: [(9, 3), (8, 4)],
}
SUM_CHUNK = {
    0: [(9, 0), (1, 4), (5, 2), (4, 3), (2, 4)],
    1: [(10, 0), (8, 2), (0, 4), (5, 4), (3, 4), (7, 3), (6, 4)],
    2: [(11, 0), (12, 0), (10, 2), (7, 5), (9, 4)],
}
SUM_SMALL = [
    (13, 0), (8, 5),
]
SUM_LAST = [
    (11, 1), (9, 5), (12, 1), (13, 1), (12, 2), (10, 3), (11, 2), (13, 2), (10, 4), (12, 3),
    (11, 3), (13, 3), (10, 5), (12, 4), (13, 4), (12, 5), (11, 4), (13, 5), (11, 5),
]


def back(depth, groups, codes, proj, peaks, key_side, grad_mixed, mixed, x0, grad_one, chunks, sums, bias_sums, saved):
    count = mixed.shape[0]
    heads = HEADS // CHUNKS
    act, pre, hidden, ffn, branch = saved

    def weight_grads(mixed, act, pre, hidden, ffn, branch, lanes_v, left_v, right_v, loads, greet, step):
        def fetch(k, source):
            return pltpu.make_async_copy(source, lanes_v.at[lax.rem(k, 2)], loads.at[lax.rem(k, 2)])

        right = pltpu.make_async_copy(ffn, right_v, loads.at[2])
        left = pltpu.make_async_copy(hidden, left_v, loads.at[3])
        last = pltpu.make_async_copy(branch, right_v, loads.at[2])
        fetch(0, act.at[0]).start()
        right.start()
        left.start()
        greet()
        right.wait()

        @pl.loop(0, 4)
        def _(k):
            fetch(k, act.at[0]).wait()

            @pl.when(k < 3)
            def _():
                fetch(k + 1, act.at[k + 1]).start()

            @pl.when(k == 3)
            def _():
                fetch(0, pre.at[0]).start()

            step(k, dot(lanes_v[lax.rem(k, 2)], right_v[...], TN))

        left.wait()
        last.start()

        @pl.loop(0, 4)
        def _(k):
            fetch(k, pre.at[0]).wait()

            @pl.when(k < 3)
            def _():
                fetch(k + 1, pre.at[k + 1]).start()

            step(4 + k, dot(left_v[...], lanes_v[lax.rem(k, 2)], TN))

        last.wait()
        step(8, dot(mixed[...], right_v[...], TN))

    def body(codes, proj, peaks, key_side, grad_mixed, mixed, x0, grad_one, chunks, sums, bias_sums, act, pre, hidden, ffn, branch, frames_grad,
             proj_v, peaks_v, weight_v, grad_proj, left_v, inner, grad_query, total, rows_v, small_v, loads, greet, step, put, actions, chunk_done):
        width, _, _ = subnet(codes)
        features = (lane_row(D) < width).astype(F32)
        one = pltpu.make_async_copy(grad_one, total, loads.at[6])
        out = pltpu.make_async_copy(total, frames_grad, loads.at[7])

        def fetch(j):
            slot = lax.rem(j, 2)
            return [
                pltpu.make_async_copy(proj.at[j], proj_v.at[slot], loads.at[slot]),
                pltpu.make_async_copy(peaks.at[pl.ds(j * heads, heads)], peaks_v.at[slot], loads.at[2 + slot]),
                pltpu.make_async_copy(chunks.at[j], weight_v.at[slot], loads.at[4 + slot]),
            ]

        one.start()
        rows_v[...] = jnp.zeros_like(rows_v)
        rows_v[2:6, :] = sums[0:4, :]
        rows_v[7:9, :] = sums[4:6, :]
        small_v[...] = jnp.zeros_like(small_v)
        for row, at, col in bias_places(groups):
            small_v[row : row + 1, 128 : 128 + D // groups] = bias_sums[at : at + 1, col : col + D // groups]

        weight_grads(mixed, act, pre, hidden, ffn, branch, proj_v, left_v, grad_proj, loads, greet, step)
        for copy in fetch(0):
            copy.start()

        @pl.loop(0, CHUNKS)
        def _(j):
            slot = lax.rem(j, 2)
            for copy in fetch(j):
                copy.wait()

            @pl.when(j + 1 < CHUNKS)
            def _():
                for copy in fetch(j + 1):
                    copy.start()

            attend_back(proj_v.at[slot], j, peaks_v.at[slot], key_side, grad_mixed, mixed, grad_proj, inner, grad_query, actions)
            cols = pl.ds(pl.multiple_of(j * CHUNK, CHUNK), CHUNK)
            masked = key_side[:, 7:8].astype(F32)
            grads = grad_proj[...].astype(F32)
            totals = col_sum(grads)
            rows_v[0:1, cols] = totals[:, :CHUNK]
            rows_v[1:2, cols] = totals[:, 2 * CHUNK :]
            put(j, dot(x0[...], grad_proj[...], TN).astype(LOW))
            chunk_done(j)

            @pl.when(j == 0)
            def _():
                one.wait()
                rows_v[6:7, :] = col_sum(total[...] * masked)

            rows_v[16:24, :] = jnp.zeros((8, D), F32)
            for k, part in enumerate(split3(col_sum(grads * masked))):
                rows_v[16 + k : 17 + k, :] = part
            spread = dot(rows_v[16:32, :].astype(LOW), flat(weight_v[slot]), NT)
            rows_v[6:7, :] += col_sum(spread) * features

            @pl.when(j + 1 < CHUNKS)
            def _():
                total[...] += dot(grad_proj[...], flat(weight_v[slot]), NT) * features

        small_v[:, :128] = rows_v[...].T
        put(None, small_v[...])
        chunk_done(None)
        total[...] += dot(grad_proj[...], flat(weight_v[(CHUNKS - 1) % 2]), NT) * features
        out.start()
        return out

    shape = jax.ShapeDtypeStruct
    operands = (codes, proj, peaks, key_side, grad_mixed, mixed, x0, grad_one, chunks, sums, bias_sums, act, pre, hidden, ffn, branch)
    in_specs = [SM, HBM, HBM, VM, VM, VM, VM, HBM, HBM, VM, VM] + [HBM] * 5

    def scratch(weight_shape):
        return [
            pltpu.VMEM((2, count, D), LOW),
            pltpu.VMEM((2, heads, count, 128), LOW),
            pltpu.VMEM((2,) + weight_shape, LOW),
            pltpu.VMEM((count, D), LOW),
            pltpu.VMEM((count, D), LOW),
            pltpu.VMEM((2, count, 128), LOW),
            pltpu.VMEM((count, 128), F32),
            pltpu.VMEM((count, D), F32),
            pltpu.VMEM((128, D), F32),
            pltpu.VMEM((D, SMALL), F32),
            pltpu.SemaphoreType.DMA((8,)),
        ]

    if not depth:

        def plain(*refs):
            inputs, parts, small, weight_parts, rest = refs[:17], refs[17], refs[18], refs[19], refs[20:]

            def step(k, value):
                weight_parts[k] = value.astype(LOW)

            def put(j, value):
                if j is None:
                    small[...] = value
                else:
                    parts[j] = value

            body(*inputs, *rest, lambda: None, step, put, {}, lambda j: None).wait()

        return pl.pallas_call(
            plain,
            out_shape=(shape((count, D), F32), shape((CHUNKS, D, D), LOW), shape((D, SMALL), F32), shape((9, D, D), LOW)),
            in_specs=in_specs,
            out_specs=(HBM, VM, VM, VM),
            scratch_shapes=scratch((D, D)),
            compiler_params=pltpu.CompilerParams(vmem_limit_bytes=62 * MIB),
            name="back_plain",
        )(*operands)

    rows, tall = D // groups, FF // groups
    sizes = [(rows, D)] * 11 + [(rows, D - SMALL), (rows, SMALL), (rows, SMALL)]
    rooms = [reduce_room(depth, *size, cross) for size, cross in zip(sizes, SUM_CROSS)]
    starts = [sum(len(room) for room in rooms[:k]) for k in range(len(rooms) + 1)]

    def fused(*refs):
        inputs, chunk_own, wide_own, down_own, small_own = refs[:17], *refs[17:21]
        inside, (send, recv, ring, chunk_part, small_part), rest = refs[21:32], refs[32:37], refs[37:]
        room_refs, finals = rest[: starts[-1]], rest[starts[-1] :]
        here = Place(depth)
        c = here.c
        copies = Copies(send, recv)
        plans = []

        def plan(sibling, kept):
            k = len(plans)
            plans.append(reduce_part(here, copies, sibling, kept, room_refs[starts[k] : starts[k + 1]], finals[k], sizes[k][1], SUM_CROSS[k]))

        for k in range(9):
            plan(ring.at[k % 3, :, :, 1 - c], lambda zz, xx, k=k: ring[k % 3, zz, xx, c])
        for k in range(2):
            plan(chunk_part.at[k, :, :, 1 - c], lambda zz, xx, k=k: chunk_part[k, zz, xx, c])
        for cut in (pl.ds(0, D - SMALL), pl.ds(D - SMALL, SMALL)):
            plan(chunk_part.at[2, :, :, 1 - c, :, cut], lambda zz, xx, cut=cut: chunk_part[2, zz, xx, c, :, cut])
        plan(small_part.at[:, :, 1 - c], lambda zz, xx: small_part[zz, xx, c])
        def step(k, value):
            hook(k, {at: plans[at - 3][6] for at in range(3, 9)})
            ring[lax.rem(k, 3)] = value.astype(LOW).reshape(depth, 2, 2, rows, D)
            hook(k, {at: functools.partial(run, plans, todo) for at, todo in SUM_EARLY.items()})

        def put(j, value):
            if j is None:
                small_part[...] = value.astype(LOW).reshape(depth, 2, 2, rows, SMALL)
            else:
                chunk_part[j] = value.reshape(depth, 2, 2, rows, D)

        actions = {k: functools.partial(run, plans, todo) for k, todo in SUM_THEN.items()}

        def chunk_done(j):
            if j is None:
                run(plans, SUM_SMALL)
            else:
                hook(j, {k: functools.partial(run, plans, todo) for k, todo in SUM_CHUNK.items()})

        out = body(*inputs, *inside, here.greet, step, put, actions, chunk_done)
        run(plans, SUM_LAST)
        for k in range(4):
            down_own[k * rows : (k + 1) * rows, :] = finals[k][...]
            wide_own[1 + k] = finals[4 + k][...]
        wide_own[0] = finals[8][...]
        for k in range(2):
            chunk_own[k] = finals[9 + k][...]
        chunk_own[2, :, : D - SMALL] = finals[11][...]
        chunk_own[2, :, D - SMALL :] = finals[12][...]
        small_own[...] = finals[13][...]
        out.wait()
        copies.finish()

    copies = reduce_copies(depth) * len(sizes)
    return pl.pallas_call(
        fused,
        out_shape=(
            shape((count, D), F32),
            shape((CHUNKS, rows, D), LOW),
            shape((5, rows, D), LOW),
            shape((tall, D), LOW),
            shape((rows, SMALL), LOW),
        ),
        in_specs=in_specs,
        out_specs=(HBM,) + (VM,) * 4,
        scratch_shapes=scratch((depth, 2, 2, rows, D))
        + [
            pltpu.SemaphoreType.DMA((copies,)),
            pltpu.SemaphoreType.DMA((copies,)),
            pltpu.VMEM((3, depth, 2, 2, rows, D), LOW),
            pltpu.VMEM((CHUNKS, depth, 2, 2, rows, D), LOW),
            pltpu.VMEM((depth, 2, 2, rows, SMALL), LOW),
        ]
        + [ref for room in rooms for ref in room]
        + [pltpu.VMEM(size, LOW) for size in sizes],
        compiler_params=pltpu.CompilerParams(collective_id=1, has_side_effects=True, vmem_limit_bytes=62 * MIB),
        name="back",
    )(*operands)


def finish(total, key_side, chunk_own, wide_own, down_own, small_own):
    count, (_, rows, _), tall = total.shape[0], chunk_own.shape, down_own.shape[0]
    size = count // 4

    def kernel(total, key_side, chunk_own, wide_own, down_own, small_own,
               frames_grad, qkv_grad, out_grad, in_grad, down_grad, bias_grad, gains_grad, shifts_grad, square, in_v):
        frames_grad[...] = total[...] * (1.0 - key_side[:, 7:8].astype(F32))

        @pl.when(pl.program_id(0) == 0)
        def _():
            for j in range(CHUNKS):
                for k in range(3):
                    piece = chunk_own[j, :, k * CHUNK : (k + 1) * CHUNK]
                    qkv_grad[:, k * D + j * CHUNK : k * D + (j + 1) * CHUNK] = piece.astype(F32)
            out_grad[...] = wide_own[0].astype(F32)
            for k in range(4):
                in_v[k] = wide_own[1 + k].astype(F32)
            for k, col, unit in unit_pieces(D // rows):
                in_grad[:, unit : unit + rows] = in_v[k, :, col : col + rows]
            down_grad[...] = down_own[...].astype(F32)
            table = small_own[...].astype(F32)
            square[...] = jnp.zeros_like(square)
            square[0:rows, :] = table[:, :128]
            turned = square[...].T
            shifts_grad[...] = turned[0:7, 0:rows]
            gains_grad[...] = turned[7:9, 0:rows]
            for k in range(4):
                bias_grad[:, k * rows : (k + 1) * rows] = table[k : k + 1, 128 : 128 + rows]

    def whole(*dims):
        return pl.BlockSpec(dims, lambda i: (0,) * len(dims))

    block = pl.BlockSpec((size, D), lambda i: (i, 0))
    outs = [(rows, 3 * D), (rows, D), (rows, FF), (tall, D), (1, tall), (2, rows), (7, rows)]
    return pl.pallas_call(
        kernel,
        grid=(4,),
        in_specs=[block, pl.BlockSpec((size, 128), lambda i: (i, 0))]
        + [whole(*part.shape) for part in (chunk_own, wide_own, down_own, small_own)],
        out_specs=(block,) + tuple(whole(*dims) for dims in outs),
        out_shape=(jax.ShapeDtypeStruct((count, D), F32),) + tuple(jax.ShapeDtypeStruct(dims, F32) for dims in outs),
        scratch_shapes=[pltpu.VMEM((128, 128), F32), pltpu.VMEM((4, rows, D), F32)],
        name="finish",
    )(total, key_side, chunk_own, wide_own, down_own, small_own)


def on_device(dp_size, frames, lengths, mask_starts, width_code, head_code, ffn_code, qkv_weight, out_weight, ffn_in_weight,
              ffn_out_weight, ffn_bias, norm_gains, shifts, cotangent):
    rows, tall = qkv_weight.shape[0], ffn_out_weight.shape[0]
    groups = D // rows
    fused = rows % 16 == 0 and groups % 4 == 0 and dp_size % 2 == 0
    depth = groups // 4 if fused else 0
    codes = jnp.concatenate([width_code, head_code, ffn_code])
    starts = mask_starts.reshape(frames.shape[0] // 128, 128)
    if fused:
        masters = (qkv_weight, out_weight, ffn_in_weight, ffn_out_weight, ffn_bias.reshape(1, tall), norm_gains.T, shifts.T)
        found = front(depth, groups, codes, lengths, starts, frames, masters)
        proj, x0, mixed, peaks, key_side, small, bias, chunks, wide, down = found
    else:
        spread = jnp.zeros((rows, 128), F32).at[:4, :rows].set(ffn_bias.reshape(4, rows))
        head = jnp.concatenate([shifts, norm_gains, jnp.zeros((rows, 119), F32), spread], axis=1).astype(LOW)
        chunks = jnp.stack([jnp.concatenate(chunk_cols(qkv_weight, j), axis=1) for j in range(CHUNKS)]).astype(LOW)
        blocks = ffn_in_weight.reshape(rows, groups, 4, rows).transpose(2, 0, 1, 3).reshape(4, rows, D)
        wide = jnp.concatenate([out_weight[None], blocks]).astype(LOW)
        head = lax.all_gather(head, "group", axis=0, tiled=True)
        chunks = lax.all_gather(chunks, "group", axis=1, tiled=True)
        wide = lax.all_gather(wide, "group", axis=1, tiled=True)
        down = lax.all_gather(ffn_out_weight.astype(LOW).reshape(4, rows, D), "group", axis=1, tiled=True)
        proj, x0, mixed, peaks, key_side, small, bias = front(0, groups, codes, lengths, starts, frames, (head, chunks))
    layer_out, grad_mixed, grad_one, *saved, sums, bias_sums = middle(
        groups, codes, mixed, x0, cotangent, key_side, wide.reshape(5, D, D), down.reshape(4, D, D), small, bias
    )
    shared = (codes, proj, peaks, key_side, grad_mixed, mixed, x0, grad_one, chunks, sums, bias_sums, saved)
    if fused:
        total, *owned = back(depth, groups, *shared)
        if dp_size > 2:
            owned = [0.5 * lax.psum(part, "dp") for part in owned]
    else:
        total, chunk_parts, small_part, weight_parts = back(0, groups, *shared)
        wide_part, down_part = weight_parts[jnp.array([8, 4, 5, 6, 7])], weight_parts[:4]
        owned = [
            lax.psum_scatter(chunk_parts.astype(F32), "group", scatter_dimension=1, tiled=True),
            lax.psum_scatter(wide_part.astype(F32), "group", scatter_dimension=1, tiled=True),
            lax.psum_scatter(down_part.astype(F32), "group", scatter_dimension=1, tiled=True).reshape(tall, D),
            lax.psum_scatter(small_part, "group", scatter_dimension=0, tiled=True),
        ]
        owned = [lax.psum(part.astype(LOW), "dp") for part in owned]
    frames_grad, qkv_grad, out_grad, ffn_in_grad, ffn_out_grad, bias_row, gains_rows, shifts_rows = finish(total, key_side, *owned)
    return (layer_out, frames_grad, qkv_grad, out_grad, ffn_in_grad, ffn_out_grad, bias_row.reshape(tall, 1), gains_rows.T, shifts_rows.T)


def solution(mesh):
    by_all, by_group = P(("group", "dp"), None), P("group", None)
    placed = (by_all, by_all, P(("group", "dp")), P("group"), P("group"), P("group")) + (by_group,) * 7 + (by_all,)
    return jax.shard_map(
        functools.partial(on_device, mesh.shape["dp"]),
        mesh=mesh,
        in_specs=placed,
        out_specs=(by_all, by_all) + (by_group,) * 7,
        check_vma=False,
    )
```
